32 devices in a mesh: batch: 4 (over y, x), seq: 8 (over z, core).
Axes of the slice: x: 2, y: 2, z: 4, core: 2. Of those that a mesh axis runs over, the one named last changes fastest.
Arguments:
- incoming_activations: bfloat16 [8, 2048, 1024], P('batch', 'seq'), may hold values from -6 to 6
- sequence_extents: int32 [8, 8], P('batch'), may hold values from 0 to 2048, as said below
- upstream_sensitivity: bfloat16 [8, 2048, 1024], P('batch', 'seq'), may hold values from -6 to 6
- initial_normalizer_scale: bfloat16 [1024], P(('batch', 'seq')), may hold values from 0.5 to 1.5
- initial_normalizer_offset: bfloat16 [1024], P(('batch', 'seq')), may hold values from -2.5 to 2.5
- temporal_lookup_fraction: bfloat16 [1024], P(('batch', 'seq')), may hold values from 0.099609375 to 0.8984375
- temporal_content_fraction: bfloat16 [1024], P(('batch', 'seq')), may hold values from 0.099609375 to 0.8984375
- temporal_receptance_fraction: bfloat16 [1024], P(('batch', 'seq')), may hold values from 0.099609375 to 0.8984375
- feature_forgetting_rate: bfloat16 [1024], P(('batch', 'seq')), may hold values from 9.536743e-06 to 0.049804688
- present_reward: bfloat16 [1024], P(('batch', 'seq')), may hold values from 0 to 3
- temporal_lookup_projection: bfloat16 [1024, 1024], P(('batch', 'seq')), may hold values from -0.1875 to 0.1875
- temporal_content_projection: bfloat16 [1024, 1024], P(('batch', 'seq')), may hold values from -0.1875 to 0.1875
- temporal_receptance_projection: bfloat16 [1024, 1024], P(('batch', 'seq')), may hold values from -0.1875 to 0.1875
- temporal_result_projection: bfloat16 [1024, 1024], P(('batch', 'seq')), may hold values from -0.75 to 0.75
- later_normalizer_scale: bfloat16 [1024], P(('batch', 'seq')), may hold values from 0.5 to 1.5
- later_normalizer_offset: bfloat16 [1024], P(('batch', 'seq')), may hold values from -2.5 to 2.5
- feature_lookup_fraction: bfloat16 [1024], P(('batch', 'seq')), may hold values from 0.099609375 to 0.8984375
- feature_receptance_fraction: bfloat16 [1024], P(('batch', 'seq')), may hold values from 0.099609375 to 0.8984375
- feature_lookup_projection: bfloat16 [1024, 4096], P(('batch', 'seq')), may hold values from -0.1875 to 0.1875
- feature_content_projection: bfloat16 [4096, 1024], P(('batch', 'seq')), may hold values from -0.09375 to 0.09375
- feature_receptance_projection: bfloat16 [1024, 1024], P(('batch', 'seq')), may hold values from -0.1875 to 0.1875
Outputs:
- output: bfloat16 [8, 2048, 1024], P('batch', 'seq')
- input_grad: float32 [8, 2048, 1024], P('batch', 'seq')
- grad_norm1_gain: float32 [1024], P(('batch', 'seq'))
- grad_norm1_bias: float32 [1024], P(('batch', 'seq'))
- grad_mix_key: float32 [1024], P(('batch', 'seq'))
- grad_mix_value: float32 [1024], P(('batch', 'seq'))
- grad_mix_gate: float32 [1024], P(('batch', 'seq'))
- grad_decay_rate: float32 [1024], P(('batch', 'seq'))
- grad_time_bonus: float32 [1024], P(('batch', 'seq'))
- grad_key_weight: float32 [1024, 1024], P(('batch', 'seq'))
- grad_value_weight: float32 [1024, 1024], P(('batch', 'seq'))
- grad_gate_weight: float32 [1024, 1024], P(('batch', 'seq'))
- grad_output_weight: float32 [1024, 1024], P(('batch', 'seq'))
- grad_norm2_gain: float32 [1024], P(('batch', 'seq'))
- grad_norm2_bias: float32 [1024], P(('batch', 'seq'))
- grad_ffn_mix_key: float32 [1024], P(('batch', 'seq'))
- grad_ffn_mix_gate: float32 [1024], P(('batch', 'seq'))
- grad_ffn_key_weight: float32 [1024, 4096], P(('batch', 'seq'))
- grad_ffn_value_weight: float32 [4096, 1024], P(('batch', 'seq'))
- grad_ffn_gate_weight: float32 [1024, 1024], P(('batch', 'seq'))
The draws below stay inside these ranges and needn't reach their ends.
Inputs may be any that keep to these rules, and one draw needn't show every extreme that they name: `sequence_extents`: each row lists in order the lengths of the documents that fill its 2048 positions end to end, then zeros; the lengths sum to 2048. In each group of 2 rows of one index of batch one row holds a single document of 2048 positions; in the others every document has 256, 1024 or 2048 positions except the last, which may be shorter.
All inputs are finite; a program needn't handle non-finite values.
Results may differ from the reference program's by a relative error of at most 0.0085.
Values may be sent and summed in bfloat16 or wider, within the bound.
No kernel may reach another device: no remote copies, remote signals or barrier semaphores. Data moves between devices by JAX's collectives and lax.ppermute only.
A program may use at most 256 MiB of HBM per device.

```python
import math
from functools import partial
import jax
import jax.numpy as jnp
from jax import lax

EMBED_SIZE = 1024
FF = 4096
ROWS = 2
SPAN = 256
ROWS_ALL = 8
STREAM = 2048
MAXDOCS = 8
N_SEQ = 8


def draw_sequence_extents(key, part):
    key = jax.random.fold_in(key, 11)
    pick_key, single_key = jax.random.split(key)
    buckets = jax.random.randint(pick_key, (ROWS_ALL, MAXDOCS), 0, 3)
    sizes_drawn = jnp.where(buckets == 0, 8 * SPAN, jnp.where(buckets == 1, 4 * SPAN, SPAN)).astype(jnp.int32)
    ends = jnp.cumsum(sizes_drawn, axis=1).astype(jnp.int32)
    starts = ends - sizes_drawn
    packed = jnp.clip(jnp.minimum(ends, STREAM) - starts, 0, STREAM).astype(jnp.int32)
    chosen = jax.random.randint(single_key, (ROWS_ALL // ROWS,), 0, ROWS)
    row_index = jnp.arange(ROWS_ALL)
    single = row_index % ROWS == chosen[row_index // ROWS]
    column = jnp.arange(MAXDOCS)
    whole_row = jnp.where(column == 0, STREAM, 0).astype(jnp.int32)
    return jnp.where(single[:, None], whole_row[None, :], packed).astype(jnp.int32)


def level_of(stream_key, extent, cuts, least, high):
    def one(dim, parts):
        draws = jax.random.uniform(jax.random.fold_in(jax.random.fold_in(stream_key, 6), dim), (parts,), jnp.float32, least / len(cuts), high / len(cuts))
        return jnp.repeat(jnp.exp(draws), extent[dim] // parts).reshape((-1,) + (1,) * (len(extent) - dim - 1))

    loudness = one(*cuts[0])
    for cut in cuts[1:]:
        loudness = loudness * one(*cut)
    return loudness


def scatter_about(own_key, shape, scale, reach, cuts=(), held_as=jnp.bfloat16):
    gain = level_of(own_key, shape, cuts, -0.22, 0.18) if cuts else 1.0
    array = jax.random.normal(own_key, shape, jnp.float32) * scale * gain
    return jnp.minimum(jnp.maximum(array, -reach), reach).astype(held_as)


def setup_inputs(seed: int = 0) -> dict:
    key_list = jax.random.split(jax.random.key(seed), 22)
    incoming_activations = scatter_about(key_list[0], (ROWS_ALL, STREAM, EMBED_SIZE), 1.0, 6.0, ((0, 4), (1, 8)))
    sequence_extents = draw_sequence_extents(jax.random.fold_in(key_list[21], 71), 0)
    upstream_sensitivity = scatter_about(key_list[2], (ROWS_ALL, STREAM, EMBED_SIZE), 1.0, 6.0, ((0, 4), (1, 8)))
    initial_normalizer_scale = jnp.clip(1.0 + 0.1 * jax.random.normal(key_list[3], (EMBED_SIZE,), jnp.float32), 0.5, 1.5).astype(jnp.bfloat16)
    initial_normalizer_offset = scatter_about(key_list[4], (EMBED_SIZE,), 0.3, 2.5, ((0, 32),))
    temporal_lookup_fraction = jnp.clip(0.099609375 + 0.7988281 * jax.random.uniform(key_list[5], (EMBED_SIZE,), jnp.float32) ** level_of(key_list[5], (EMBED_SIZE,), ((0, 32),), -0.2, 0.2), 0.099609375, 0.8984375).astype(jnp.bfloat16)
    temporal_content_fraction = jnp.clip(0.099609375 + 0.7988281 * jax.random.uniform(key_list[6], (EMBED_SIZE,), jnp.float32) ** level_of(key_list[6], (EMBED_SIZE,), ((0, 32),), -0.2, 0.2), 0.099609375, 0.8984375).astype(jnp.bfloat16)
    temporal_receptance_fraction = jnp.clip(0.099609375 + 0.7988281 * jax.random.uniform(key_list[7], (EMBED_SIZE,), jnp.float32) ** level_of(key_list[7], (EMBED_SIZE,), ((0, 32),), -0.2, 0.2), 0.099609375, 0.8984375).astype(jnp.bfloat16)
    feature_forgetting_rate = jnp.clip(jnp.exp(math.log(0.049804688) - 8.56071235 * jax.random.uniform(key_list[8], (EMBED_SIZE,), jnp.float32) ** level_of(key_list[8], (EMBED_SIZE,), ((0, 32),), -0.2, 0.2)), 9.5367431640625e-06, 0.049804688).astype(jnp.bfloat16)
    present_reward = jnp.clip(3.0 * jax.random.uniform(key_list[9], (EMBED_SIZE,), jnp.float32) ** level_of(key_list[9], (EMBED_SIZE,), ((0, 32),), -0.2, 0.2), 0.0, 3.0).astype(jnp.bfloat16)
    temporal_lookup_projection = scatter_about(key_list[10], (EMBED_SIZE, EMBED_SIZE), EMBED_SIZE ** -0.5, 0.1875, ((0, 32),))
    temporal_content_projection = scatter_about(key_list[11], (EMBED_SIZE, EMBED_SIZE), EMBED_SIZE ** -0.5, 0.1875, ((0, 32),))
    temporal_receptance_projection = scatter_about(key_list[12], (EMBED_SIZE, EMBED_SIZE), EMBED_SIZE ** -0.5, 0.1875, ((0, 32),))
    temporal_result_projection = scatter_about(key_list[13], (EMBED_SIZE, EMBED_SIZE), (EMBED_SIZE // 16) ** -0.5, 0.75, ((0, 32),))
    later_normalizer_scale = jnp.clip(1.0 + 0.1 * jax.random.normal(key_list[14], (EMBED_SIZE,), jnp.float32), 0.5, 1.5).astype(jnp.bfloat16)
    later_normalizer_offset = scatter_about(key_list[15], (EMBED_SIZE,), 0.3, 2.5, ((0, 32),))
    feature_lookup_fraction = jnp.clip(0.099609375 + 0.7988281 * jax.random.uniform(key_list[16], (EMBED_SIZE,), jnp.float32) ** level_of(key_list[16], (EMBED_SIZE,), ((0, 32),), -0.2, 0.2), 0.099609375, 0.8984375).astype(jnp.bfloat16)
    feature_receptance_fraction = jnp.clip(0.099609375 + 0.7988281 * jax.random.uniform(key_list[17], (EMBED_SIZE,), jnp.float32) ** level_of(key_list[17], (EMBED_SIZE,), ((0, 32),), -0.2, 0.2), 0.099609375, 0.8984375).astype(jnp.bfloat16)
    feature_lookup_projection = scatter_about(key_list[18], (EMBED_SIZE, FF), EMBED_SIZE ** -0.5, 0.1875, ((0, 32),))
    feature_content_projection = scatter_about(key_list[19], (FF, EMBED_SIZE), FF ** -0.5, 0.09375, ((0, 32),))
    feature_receptance_projection = scatter_about(key_list[20], (EMBED_SIZE, EMBED_SIZE), EMBED_SIZE ** -0.5, 0.1875, ((0, 32),))
    return dict(incoming_activations=incoming_activations, sequence_extents=sequence_extents, upstream_sensitivity=upstream_sensitivity, initial_normalizer_scale=initial_normalizer_scale, initial_normalizer_offset=initial_normalizer_offset, temporal_lookup_fraction=temporal_lookup_fraction, temporal_content_fraction=temporal_content_fraction, temporal_receptance_fraction=temporal_receptance_fraction, feature_forgetting_rate=feature_forgetting_rate, present_reward=present_reward, temporal_lookup_projection=temporal_lookup_projection, temporal_content_projection=temporal_content_projection, temporal_receptance_projection=temporal_receptance_projection, temporal_result_projection=temporal_result_projection, later_normalizer_scale=later_normalizer_scale, later_normalizer_offset=later_normalizer_offset, feature_lookup_fraction=feature_lookup_fraction, feature_receptance_fraction=feature_receptance_fraction, feature_lookup_projection=feature_lookup_projection, feature_content_projection=feature_content_projection, feature_receptance_projection=feature_receptance_projection)


@jax.custom_vjp
def low(v):
    return lax.optimization_barrier(v.astype(jnp.bfloat16)).astype(jnp.float32)

@jax.custom_vjp
def low_back(v):
    return v

def low_keep(v):
    return (low(v), None)

def low_pass(kept, grad):
    return (grad,)

def back_keep(v):
    return (v, None)

def back_low(kept, grad):
    return (low(grad),)
low.defvjp(low_keep, low_pass)
low_back.defvjp(back_keep, back_low)
eps = 1e-05
highest = lax.Precision.HIGHEST

def layer_norm(values, gain_vec, bias_vec):
    centre = values - lax.optimization_barrier(jnp.mean(values, axis=-1, keepdims=True))
    scaled = centre * lax.rsqrt(lax.optimization_barrier(jnp.mean(centre * centre, axis=-1, keepdims=True)) + eps)
    return scaled * gain_vec + bias_vec

def token_shift(rows_in, keep_mask):
    return jnp.concatenate([jnp.zeros_like(rows_in[:1]), rows_in[:-1]], axis=0) * keep_mask

def attention_content_span(running_memory, residual_sublevel, feature_forgetting_rate, present_reward):
    state_numerator, state_denominator = running_memory
    key_row_block, value_row_block, resets = residual_sublevel
    length = key_row_block.shape[0]
    width = key_row_block.shape[1]
    document_segments = jnp.cumsum(resets.astype(jnp.int32)).astype(jnp.int32)
    order_idx = jnp.arange(length)
    step_pos = order_idx.astype(jnp.float32)[:, None]
    powered_lookups = jnp.exp(key_row_block)
    grow_exp = jnp.exp(step_pos * feature_forgetting_rate)
    shrink = jnp.exp((1.0 - step_pos) * feature_forgetting_rate)
    pair_mask = ((order_idx[None, :] < order_idx[:, None]) & (document_segments[None, :] == document_segments[:, None])).astype(jnp.float32)
    weighted = jnp.concatenate([powered_lookups * value_row_block, powered_lookups], axis=1) * jnp.concatenate([grow_exp, grow_exp], axis=1)
    past_sums = jnp.dot(pair_mask, weighted, precision=highest) * jnp.concatenate([shrink, shrink], axis=1)
    carry_fade = (document_segments == 0).astype(jnp.float32)[:, None] * jnp.exp(-step_pos * feature_forgetting_rate)
    present_token_contribution = jnp.exp(present_reward) * powered_lookups
    numer = carry_fade * state_numerator + past_sums[:, :width] + present_token_contribution * value_row_block
    denom = carry_fade * state_denominator + past_sums[:, width:] + present_token_contribution
    tail_fade = (document_segments == document_segments[-1]).astype(jnp.float32)[:, None] * jnp.exp((step_pos - (length - 1)) * feature_forgetting_rate)
    block_fade = (document_segments[-1] == 0).astype(jnp.float32) * jnp.exp(-length * feature_forgetting_rate)
    num_out = block_fade * state_numerator + lax.optimization_barrier(jnp.sum(tail_fade * powered_lookups * value_row_block, axis=0))
    den_out = block_fade * state_denominator + lax.optimization_barrier(jnp.sum(tail_fade * powered_lookups, axis=0))
    return ((num_out, den_out), numer / denom)

def row_forward(learnable_collection, inputs, resets):
    opening_standardize_scale, opening_standardize_offset, temporal_lookup_mixture, temporal_content_mixture, temporal_receptance_mixture, feature_forgetting_rate, present_reward, temporal_lookup_projection, temporal_content_projection, temporal_receptance_projection, temporal_result_projection, closing_standardize_scale, closing_standardize_offset, feature_lookup_mixture, feature_receptance_mixture, feature_lookup_projection, feature_content_projection, feature_receptance_projection = learnable_collection
    keep_mask = 1.0 - resets.astype(jnp.float32)[:, None]
    normed = layer_norm(inputs, opening_standardize_scale, opening_standardize_offset)
    before = token_shift(normed, keep_mask)
    key_in = low(normed * temporal_lookup_mixture + before * (1.0 - temporal_lookup_mixture))
    value_in = low(normed * temporal_content_mixture + before * (1.0 - temporal_content_mixture))
    gate_in = low(normed * temporal_receptance_mixture + before * (1.0 - temporal_receptance_mixture))
    key_row_block = low_back(jnp.dot(key_in, temporal_lookup_projection, precision=highest))
    value_row_block = low_back(jnp.dot(value_in, temporal_content_projection, precision=highest))
    gates = jax.nn.sigmoid(low_back(jnp.dot(gate_in, temporal_receptance_projection, precision=highest)))
    blocks = (key_row_block.reshape(N_SEQ, SPAN, EMBED_SIZE), value_row_block.reshape(N_SEQ, SPAN, EMBED_SIZE), resets.reshape(N_SEQ, SPAN))
    zero_state = jnp.zeros((EMBED_SIZE,), jnp.float32)
    scan_update = jax.checkpoint(partial(attention_content_span, feature_forgetting_rate=feature_forgetting_rate, present_reward=present_reward))
    _, mixed = lax.scan(scan_update, (zero_state, zero_state), blocks)
    branch = low_back(jnp.dot(low(gates * mixed.reshape(STREAM, EMBED_SIZE)), temporal_result_projection, precision=highest))
    middle = inputs + branch
    normed_two = layer_norm(middle, closing_standardize_scale, closing_standardize_offset)
    before_two = token_shift(normed_two, keep_mask)
    ffn_key_in = low(normed_two * feature_lookup_mixture + before_two * (1.0 - feature_lookup_mixture))
    ffn_gate_in = low(normed_two * feature_receptance_mixture + before_two * (1.0 - feature_receptance_mixture))
    hidden_pre = low_back(jnp.dot(ffn_key_in, feature_lookup_projection, precision=highest))
    hidden = low(jnp.square(jax.nn.relu(hidden_pre)))
    ffn_value = low_back(jnp.dot(hidden, feature_content_projection, precision=highest))
    ffn_gates = jax.nn.sigmoid(low_back(jnp.dot(ffn_gate_in, feature_receptance_projection, precision=highest)))
    return middle + ffn_gates * ffn_value

def reference(incoming_activations, sequence_extents, upstream_sensitivity, initial_normalizer_scale, initial_normalizer_offset, temporal_lookup_fraction, temporal_content_fraction, temporal_receptance_fraction, feature_forgetting_rate, present_reward, temporal_lookup_projection, temporal_content_projection, temporal_receptance_projection, temporal_result_projection, later_normalizer_scale, later_normalizer_offset, feature_lookup_fraction, feature_receptance_fraction, feature_lookup_projection, feature_content_projection, feature_receptance_projection):
    learnable_collection = (initial_normalizer_scale.astype(jnp.float32), initial_normalizer_offset.astype(jnp.float32), temporal_lookup_fraction.astype(jnp.float32), temporal_content_fraction.astype(jnp.float32), temporal_receptance_fraction.astype(jnp.float32), feature_forgetting_rate.astype(jnp.float32), present_reward.astype(jnp.float32), temporal_lookup_projection.astype(jnp.float32), temporal_content_projection.astype(jnp.float32), temporal_receptance_projection.astype(jnp.float32), temporal_result_projection.astype(jnp.float32), later_normalizer_scale.astype(jnp.float32), later_normalizer_offset.astype(jnp.float32), feature_lookup_fraction.astype(jnp.float32), feature_receptance_fraction.astype(jnp.float32), feature_lookup_projection.astype(jnp.float32), feature_content_projection.astype(jnp.float32), feature_receptance_projection.astype(jnp.float32))
    positions = jnp.arange(STREAM).astype(jnp.int32)

    def one_row(totals, row):
        inputs, row_lengths, row_cotangent = row
        starts = (jnp.cumsum(row_lengths) - row_lengths).astype(jnp.int32)
        resets = jnp.any((starts[None, :] == positions[:, None]) & (row_lengths[None, :] > 0), axis=1)
        outputs, pull_back = jax.vjp(lambda weights, values: row_forward(weights, values, resets), learnable_collection, inputs.astype(jnp.float32))
        weight_grads, input_grad = pull_back(row_cotangent.astype(jnp.float32))
        totals = jax.tree.map(jnp.add, totals, weight_grads)
        return (totals, (outputs.astype(jnp.bfloat16), input_grad))
    zero_grads = jax.tree.map(jnp.zeros_like, learnable_collection)
    totals, (outputs, input_grads) = lax.scan(one_row, zero_grads, (incoming_activations, sequence_extents, upstream_sensitivity))
    return (outputs, input_grads, totals[0], totals[1], totals[2], totals[3], totals[4], totals[5], totals[6], totals[7], totals[8], totals[9], totals[10], totals[11], totals[12], totals[13], totals[14], totals[15], totals[16], totals[17])
```

```python
from functools import partial

import jax
import jax.numpy as jnp
from jax import lax
from jax.experimental import pallas as pl
from jax.experimental.pallas import tpu as pltpu
from jax.sharding import PartitionSpec as P

eps = 1e-05
highest = lax.Precision.HIGHEST
BOTH = ("batch", "seq")


def moved(rule):
    return [(f, rule(f)) for f in range(32)]


FLIP_X = moved(lambda f: f ^ 8)
FLIP_Y = moved(lambda f: f ^ 16)
FLIP_C = moved(lambda f: f ^ 1)


def turn_z(by):
    return moved(lambda f: (f & 25) | ((((f >> 1) + by) & 3) << 1))


def sent(array, pairs):
    return lax.ppermute(array, BOTH, pairs)


def place_of(flat, dy, dx, dz, dc):
    turned = ((((flat >> 1) & 3) + dz) & 3) * 2
    return ((flat & 25) | turned) ^ (dy * 16 + dx * 8 + dc)


def tied(array, *after):
    zero = jnp.zeros((), jnp.float32)
    for other in after:
        first = other[(0,) * other.ndim].astype(jnp.float32)
        zero = zero + jnp.minimum(jnp.abs(first), 0.0)
    return array + zero.astype(array.dtype)


def assemble_kernel(owners, start, columns, slots_ref, *refs):
    pieces, out_ref, sems = refs[:-2], refs[-2], refs[-1]
    rows = out_ref.shape[1]
    copies = []
    number = 0
    for piece, count in zip(pieces, owners):
        for k in range(count):
            for q in range(columns):
                copies.append(
                    pltpu.make_async_copy(
                        piece.at[k, pl.ds(start + q * rows, rows), :],
                        out_ref.at[slots_ref[number], :, pl.ds(q * 1024, 1024)],
                        sems.at[number, q],
                    )
                )
            number += 1
    for copy in copies:
        copy.start()
    for copy in copies:
        copy.wait()


def assemble(pieces, slots, start, rows, columns):
    counts = [piece.shape[0] for piece in pieces]
    shape = (32, rows, columns * 1024)
    whole = pl.pallas_call(
        partial(assemble_kernel, counts, start, columns),
        out_shape=jax.ShapeDtypeStruct(shape, pieces[0].dtype),
        in_specs=[pl.BlockSpec(memory_space=pltpu.SMEM)]
        + [pl.BlockSpec(memory_space=pl.ANY)] * len(pieces),
        out_specs=pl.BlockSpec(memory_space=pltpu.VMEM),
        scratch_shapes=[pltpu.SemaphoreType.DMA((32, columns))],
        compiler_params=pltpu.CompilerParams(vmem_limit_bytes=24 * 1024 * 1024),
        cost_estimate=pl.CostEstimate(
            flops=0, transcendentals=0, bytes_accessed=2 * 2 * 32 * rows * columns * 1024
        ),
    )(slots, *pieces)
    return whole.reshape(32 * rows, columns * 1024)


def stacked(parts):
    rows = [part[:, q : q + 1024] for part in parts for q in range(0, part.shape[1], 1024)]
    return jnp.concatenate(rows, axis=0) if len(rows) > 1 else rows[0]


def around(part):
    return [sent(part, turn_z(d)) for d in (1, 2, 3)]


def long_slots(flat):
    every = (0, 1, 2, 3)
    steps = [(0, 0, every), (0, 1, every), (1, 0, every), (1, 1, (0, 1)), (1, 1, (2, 3))]
    return jnp.stack(
        [place_of(flat, dy, dx, -dz, dc) for dc in (0, 1) for dy, dx, dzs in steps for dz in dzs]
    ).astype(jnp.int32)


def send_far(from_x, from_y):
    half = from_x.shape[0] // 2
    return sent(from_x[:half], FLIP_Y), sent(from_y[half:], FLIP_X)


def both_cores(pieces):
    return pieces + [sent(piece, FLIP_C) for piece in pieces]


def vectors_of(blocks):
    rows = blocks[:, 0, : 11 * 32].reshape(32, 11, 32).astype(jnp.float32)
    return jnp.swapaxes(rows, 0, 1).reshape(11, 1024)


def choice(flat, width):
    index = jnp.arange(width)
    block, within = index // (width // 32), index % (width // 32)
    dc, rest = block >> 4, block & 15
    dy, dx, dz = rest >> 3, (rest >> 2) & 1, rest & 3
    wanted = place_of(flat, dy, dx, dz, dc) * (width // 32) + within
    return (jnp.arange(width)[:, None] == wanted[None, :]).astype(jnp.bfloat16)


def owner_order(flat):
    block = jnp.arange(32)
    dc, rest = block >> 4, block & 15
    dy, dx, dz = rest >> 3, (rest >> 2) & 1, rest & 3
    return place_of(flat, dy, dx, dz, dc).astype(jnp.int32)


def pick_kernel(order_ref, rows_ref, out_ref, sems):
    copies = [
        pltpu.make_async_copy(
            rows_ref.at[:, pl.ds(pl.multiple_of(order_ref[j] * 128, 128), 128)],
            out_ref.at[:, pl.ds(j * 128, 128)],
            sems.at[j],
        )
        for j in range(32)
    ]
    for copy in copies:
        copy.start()
    for copy in copies:
        copy.wait()


def pick(rows_in, order):
    return pl.pallas_call(
        pick_kernel,
        out_shape=jax.ShapeDtypeStruct(rows_in.shape, rows_in.dtype),
        in_specs=[pl.BlockSpec(memory_space=pltpu.SMEM), pl.BlockSpec(memory_space=pl.ANY)],
        out_specs=pl.BlockSpec(memory_space=pltpu.VMEM),
        scratch_shapes=[pltpu.SemaphoreType.DMA((32,))],
        compiler_params=pltpu.CompilerParams(vmem_limit_bytes=24 * 1024 * 1024),
    )(order, rows_in)


def chip_grad(own_in, other_in, grads, other_grads):
    total = jnp.einsum(
        "td,te->de", own_in, grads, preferred_element_type=jnp.float32
    ) + jnp.einsum("td,te->de", other_in, other_grads, preferred_element_type=jnp.float32)
    return total.astype(jnp.bfloat16).reshape(16, own_in.shape[1] // 16, grads.shape[1])


def ordered_halves(rows_in, flat):
    width = rows_in.shape[-1]
    rows_in = rows_in.reshape(-1, width)
    if width == 4096:
        ordered = pick(rows_in, owner_order(flat))
    else:
        ordered = jnp.dot(
            rows_in, choice(flat, width), preferred_element_type=jnp.bfloat16
        )
    return ordered[:, : width // 2], ordered[:, width // 2 :]


def sent_together(arrays):
    got = sent(jnp.concatenate(arrays, axis=1) if len(arrays) > 1 else arrays[0], FLIP_C)
    ends = [sum(a.shape[1] for a in arrays[: i + 1]) for i in range(len(arrays))]
    return [got[:, end - a.shape[1] : end] for a, end in zip(arrays, ends)]


def wide(array):
    return array.astype(jnp.float32)


def narrow(array):
    return array.astype(jnp.bfloat16)


def quarters(parts):
    return parts.reshape((2, 2, 4) + parts.shape[1:])


def add_corner(quad, add_a, add_b):
    to_y = jnp.concatenate([narrow(wide(quad[1, 0, :2]) + wide(add_a)), quad[1, 0, 2:]])
    to_x = jnp.concatenate([quad[0, 1, :2], narrow(wide(quad[0, 1, 2:]) + wide(add_b))])
    return to_y, to_x


def send_corner(quad):
    return sent(quad[1, 1, :2], FLIP_X), sent(quad[1, 1, 2:], FLIP_Y)


def send_sides(to_y, to_x):
    return sent(to_y, FLIP_Y), sent(to_x, FLIP_X)


def add_sides(quad, from_y, from_x):
    column = wide(quad[0, 0]) + wide(from_y) + wide(from_x)
    return column[0], [narrow(column[d]) for d in (1, 2, 3)]


def send_column(outgoing):
    return [sent(part, turn_z(d)) for d, part in zip((1, 2, 3), outgoing)]


def add_all(first, others):
    for other in others:
        first = first + wide(other)
    return first


def sum_vectors(rows_in, flat):
    total = rows_in
    for pairs in (FLIP_C, FLIP_X, FLIP_Y):
        total = total + sent(total, pairs)
    total = total + sum(sent(total, turn_z(d)) for d in (1, 2, 3))
    count = total.shape[1] // 32
    return lax.dynamic_slice_in_dim(total, flat * count, count, 1)


def shifted(shard, axis, by):
    length = lax.axis_size(axis)
    pairs = [(i, i + by) for i in range(length) if 0 <= i + by < length]
    return lax.ppermute(shard, axis, pairs)


def carried_in(part, starts_in, decay_vec, length, reverse):
    count = lax.axis_size("seq")
    place = lax.axis_index("seq")
    clear = 1.0 - starts_in.astype(jnp.float32)
    block_fade = jnp.exp(-length * decay_vec)

    def clear_of(block):
        return lax.dynamic_index_in_dim(clear, jnp.clip(block, 0, count - 1), 1, True)

    if count == 8:
        chip, core = place >> 1, place & 1
        other = sent(part, FLIP_C)
        is_far = (core == 1) == (not reverse)
        near = jnp.where(is_far, other, part)
        last = jnp.where(is_far, part, other)
        first_block, second_block = chip * 2 + (1 if reverse else 0), chip * 2 + (0 if reverse else 1)
        joined = clear_of(second_block) * block_fade * near + last
        step = -1 if reverse else 1
        entering = jnp.zeros_like(part)
        open_way = jnp.ones((part.shape[1], 1), jnp.float32)
        for d in (1, 2, 3):
            beside = chip - step * d
            live = ((beside >= 0) & (beside < 4)).astype(jnp.float32)
            fade = live * open_way * jnp.exp(-float(2 * (d - 1) * length) * decay_vec)
            entering = entering + fade * sent(joined, turn_z(step * d))
            open_way = open_way * clear_of(2 * beside) * clear_of(2 * beside + 1)
        return jnp.where(is_far, clear_of(first_block) * block_fade * entering + near, entering)
    gathered = lax.all_gather(part, "seq")

    def one(lap, state):
        source = count - 1 - lap if reverse else lap
        return clear_of(source) * block_fade * state + lax.dynamic_index_in_dim(gathered, source, 0, False)

    ahead = count - 1 - place if reverse else place
    return lax.fori_loop(0, ahead, one, jnp.zeros_like(part))


def norm_forward(values, gain_vec, bias_vec):
    centre = values - jnp.mean(values, axis=-1, keepdims=True)
    inv_std = lax.rsqrt(jnp.mean(centre * centre, axis=-1, keepdims=True) + eps)
    normed = centre * inv_std
    return (normed * gain_vec + bias_vec, normed, inv_std)


def norm_backward(grads, normed, inv_std, gain_vec):
    scaled = grads * gain_vec
    inner = (
        scaled
        - jnp.mean(scaled, axis=-1, keepdims=True)
        - normed * jnp.mean(scaled * normed, axis=-1, keepdims=True)
    )
    return (inv_std * inner, jnp.sum(grads * normed, axis=(0, 1)), jnp.sum(grads, axis=(0, 1)))


def project(rows_in, weight):
    return jnp.einsum("rtd,de->rte", rows_in, weight, preferred_element_type=jnp.float32)


def project_back(grads, weight):
    return jnp.einsum("rte,de->rtd", grads, weight, preferred_element_type=jnp.float32)


def weight_grad(rows_in, grads):
    total = jnp.einsum("rtd,rte->de", rows_in, grads, preferred_element_type=jnp.float32)
    return lax.psum_scatter(total, BOTH, scatter_dimension=0, tiled=True)


def weighted_value_local(
    key_row_block,
    value_row_block,
    feature_forgetting_rate,
    present_reward,
    state_numerator,
    state_denominator,
    document_segments,
):
    length = key_row_block.shape[1]
    width = key_row_block.shape[2]
    order_idx = jnp.arange(length)
    step_pos = order_idx.astype(jnp.float32)[:, None]
    powered_lookups = jnp.exp(key_row_block)
    grow_exp = jnp.exp(step_pos * feature_forgetting_rate)
    shrink = jnp.exp((1.0 - step_pos) * feature_forgetting_rate)
    pair_mask = (
        (order_idx[None, :] < order_idx[:, None])[None]
        & (document_segments[:, None, :] == document_segments[:, :, None])
    ).astype(jnp.float32)
    weighted = jnp.concatenate(
        [powered_lookups * value_row_block, powered_lookups], axis=2
    ) * jnp.concatenate([grow_exp, grow_exp], axis=1)
    past_sums = jnp.einsum(
        "rti,rie->rte", pair_mask, weighted, precision=highest
    ) * jnp.concatenate([shrink, shrink], axis=1)
    carry_fade = (document_segments == 0).astype(jnp.float32)[:, :, None] * jnp.exp(
        -step_pos * feature_forgetting_rate
    )
    present_token_contribution = jnp.exp(present_reward) * powered_lookups
    numer = (
        carry_fade * state_numerator[:, None, :]
        + past_sums[:, :, :width]
        + present_token_contribution * value_row_block
    )
    denom = (
        carry_fade * state_denominator[:, None, :]
        + past_sums[:, :, width:]
        + present_token_contribution
    )
    return numer / denom


def tail_terms(key_row_block, value_row_block, feature_forgetting_rate, document_segments):
    length = key_row_block.shape[1]
    step_pos = jnp.arange(length).astype(jnp.float32)[:, None]
    powered_lookups = jnp.exp(key_row_block)
    tail_fade = (document_segments == document_segments[:, -1:]).astype(jnp.float32)[
        :, :, None
    ] * jnp.exp((step_pos - (length - 1)) * feature_forgetting_rate)
    return (
        jnp.sum(tail_fade * powered_lookups * value_row_block, axis=1),
        jnp.sum(tail_fade * powered_lookups, axis=1),
        tail_fade,
        powered_lookups,
    )


def shards(
    tuned,
    incoming_activations,
    sequence_extents,
    upstream_sensitivity,
    initial_normalizer_scale,
    initial_normalizer_offset,
    temporal_lookup_fraction,
    temporal_content_fraction,
    temporal_receptance_fraction,
    feature_forgetting_rate,
    present_reward,
    temporal_lookup_projection,
    temporal_content_projection,
    temporal_receptance_projection,
    temporal_result_projection,
    later_normalizer_scale,
    later_normalizer_offset,
    feature_lookup_fraction,
    feature_receptance_fraction,
    feature_lookup_projection,
    feature_content_projection,
    feature_receptance_projection,
):
    flat = lax.axis_index("batch") * lax.axis_size("seq") + lax.axis_index("seq")
    vectors = jnp.stack(
        [
            initial_normalizer_scale,
            initial_normalizer_offset,
            temporal_lookup_fraction,
            temporal_content_fraction,
            temporal_receptance_fraction,
            feature_forgetting_rate,
            present_reward,
            later_normalizer_scale,
            later_normalizer_offset,
            feature_lookup_fraction,
            feature_receptance_fraction,
        ]
    )
    if tuned:
        order = long_slots(flat)
        late = lax.all_gather(
            stacked(
                [
                    feature_lookup_projection,
                    feature_content_projection,
                    feature_receptance_projection,
                    temporal_result_projection,
                ]
            ),
            BOTH,
        )
        packed = jnp.pad(vectors.reshape(1, -1), ((0, 15), (0, 1024 - vectors.size)))
        part = stacked(
            [
                temporal_lookup_projection,
                temporal_content_projection,
                temporal_receptance_projection,
                packed,
            ]
        )
        column = jnp.stack([part] + around(part))
        from_x, from_y = sent(column, FLIP_X), sent(column, FLIP_Y)
        early = both_cores([column, from_x, from_y, *send_far(from_x, from_y)])
        vectors = vectors_of(assemble(early, order, 96, 16, 1).reshape(32, 16, 1024))
        lookup_weight = assemble(early, order, 0, 32, 1)
        content_weight = assemble(early, order, 32, 32, 1)
        receptance_weight = assemble(early, order, 64, 32, 1)
        in_turn = jnp.arange(32, dtype=jnp.int32)
        ffn_key_weight = assemble([late], in_turn, 0, 32, 4)
        ffn_value_weight = assemble([late], in_turn, 128, 128, 1)
        ffn_gate_weight = assemble([late], in_turn, 256, 32, 1)
        result_weight = assemble([late], in_turn, 288, 32, 1)
    else:
        (
            lookup_weight,
            content_weight,
            receptance_weight,
            result_weight,
            ffn_key_weight,
            ffn_gate_weight,
            ffn_value_weight,
        ) = [
            lax.all_gather(part, BOTH, axis=0, tiled=True)
            for part in (
                temporal_lookup_projection,
                temporal_content_projection,
                temporal_receptance_projection,
                temporal_result_projection,
                feature_lookup_projection,
                feature_receptance_projection,
                feature_content_projection,
            )
        ]
        vectors = lax.all_gather(vectors, BOTH, axis=1, tiled=True).astype(jnp.float32)
    (
        opening_standardize_scale,
        opening_standardize_offset,
        temporal_lookup_mixture,
        temporal_content_mixture,
        temporal_receptance_mixture,
        decay_vec,
        reward_array,
        closing_standardize_scale,
        closing_standardize_offset,
        feature_lookup_mixture,
        feature_receptance_mixture,
    ) = tuple(vectors[i] for i in range(11))
    rows, length, width = incoming_activations.shape
    starts = jnp.cumsum(sequence_extents, axis=1) - sequence_extents
    places = lax.axis_index("seq") * length + jnp.arange(length, dtype=jnp.int32)
    resets = jnp.any(
        (starts[:, None, :] == places[None, :, None]) & (sequence_extents[:, None, :] > 0), axis=2
    )
    document_segments = jnp.cumsum(resets.astype(jnp.int32), axis=1)
    keep_mask = 1.0 - resets.astype(jnp.float32)[:, :, None]
    clear_flag = (document_segments[:, -1:] == 0).astype(jnp.float32)
    starts_in = jnp.any(
        (starts[:, None, :] // length == jnp.arange(lax.axis_size("seq"))[None, :, None])
        & (sequence_extents[:, None, :] > 0),
        axis=2,
    )

    inputs = incoming_activations.astype(jnp.float32)
    left_rows = shifted(incoming_activations[:, length - 1 :, :], "seq", 1)
    normed_one, unit_one, inv_one = norm_forward(
        inputs, opening_standardize_scale, opening_standardize_offset
    )
    left_normed, _, _ = norm_forward(
        left_rows.astype(jnp.float32), opening_standardize_scale, opening_standardize_offset
    )
    before_one = jnp.concatenate([left_normed, normed_one[:, :-1, :]], axis=1) * keep_mask
    key_in = (
        normed_one * temporal_lookup_mixture + before_one * (1.0 - temporal_lookup_mixture)
    ).astype(jnp.bfloat16)
    value_in = (
        normed_one * temporal_content_mixture + before_one * (1.0 - temporal_content_mixture)
    ).astype(jnp.bfloat16)
    gate_in = (
        normed_one * temporal_receptance_mixture + before_one * (1.0 - temporal_receptance_mixture)
    ).astype(jnp.bfloat16)
    key_row_block = project(key_in, lookup_weight)
    value_row_block = project(value_in, content_weight)
    gates = jax.nn.sigmoid(project(gate_in, receptance_weight))
    tail_num, tail_den, tail_fade, powered_lookups = tail_terms(
        key_row_block, value_row_block, decay_vec, document_segments
    )
    state_numerator, state_denominator = carried_in(
        jnp.stack([tail_num, tail_den]), starts_in, decay_vec, length, False
    )
    mixed, weighted_value_backward = jax.vjp(
        partial(weighted_value_local, document_segments=document_segments),
        key_row_block,
        value_row_block,
        decay_vec,
        reward_array,
        state_numerator,
        state_denominator,
    )
    gated = (gates * mixed).astype(jnp.bfloat16)
    if tuned:
        own_key, far_key = ordered_halves(key_in, flat)
        own_value, far_value = ordered_halves(value_in, flat)
        own_gate, far_gate = ordered_halves(gate_in, flat)
        own_gated, far_gated = ordered_halves(gated, flat)
        other_key, other_value, other_gate, other_gated = sent_together(
            [far_key, far_value, far_gate, far_gated]
        )
    middle = inputs + project(gated, result_weight)
    normed_two, unit_two, inv_two = norm_forward(
        middle, closing_standardize_scale, closing_standardize_offset
    )
    before_rows = shifted(normed_two[:, length - 1 :, :], "seq", 1)
    before_two = jnp.concatenate([before_rows, normed_two[:, :-1, :]], axis=1) * keep_mask
    ffn_key_in = (
        normed_two * feature_lookup_mixture + before_two * (1.0 - feature_lookup_mixture)
    ).astype(jnp.bfloat16)
    ffn_gate_in = (
        normed_two * feature_receptance_mixture + before_two * (1.0 - feature_receptance_mixture)
    ).astype(jnp.bfloat16)
    hidden_pre = project(ffn_key_in, ffn_key_weight)
    hidden = jnp.square(jax.nn.relu(hidden_pre)).astype(jnp.bfloat16)
    if tuned:
        own_ffn_key, far_ffn_key = ordered_halves(ffn_key_in, flat)
        own_ffn_gate, far_ffn_gate = ordered_halves(ffn_gate_in, flat)
        own_hidden, far_hidden = ordered_halves(hidden, flat)
        other_ffn_key, other_ffn_gate = sent_together([far_ffn_key, far_ffn_gate])
        (other_hidden,) = sent_together([far_hidden])
    ffn_value = project(hidden, ffn_value_weight)
    ffn_gates = jax.nn.sigmoid(project(ffn_gate_in, ffn_gate_weight))
    output = (middle + ffn_gates * ffn_value).astype(jnp.bfloat16)
    matrices = (
        lookup_weight,
        content_weight,
        receptance_weight,
        result_weight,
        ffn_key_weight,
        ffn_value_weight,
        ffn_gate_weight,
    )
    grad_out = upstream_sensitivity.astype(jnp.float32)
    value_grad = (grad_out * ffn_gates).astype(jnp.bfloat16)
    ffn_gate_grad = (grad_out * ffn_value * ffn_gates * (1.0 - ffn_gates)).astype(jnp.bfloat16)
    hidden_grad = project_back(value_grad, matrices[5])
    pre_grad = (hidden_grad * 2.0 * jax.nn.relu(hidden_pre)).astype(jnp.bfloat16)
    if tuned:
        flat_value_grad = value_grad.reshape(-1, width)
        flat_gate_grad = ffn_gate_grad.reshape(-1, width)
        flat_pre_grad = pre_grad.reshape(-1, pre_grad.shape[2])
        other_value_grad, other_gate_grad = sent_together([flat_value_grad, flat_gate_grad])
        (other_pre_grad,) = sent_together([flat_pre_grad])
        ffn_value_part = chip_grad(own_hidden, other_hidden, flat_value_grad, other_value_grad)
        ffn_key_part = chip_grad(own_ffn_key, other_ffn_key, flat_pre_grad, other_pre_grad)
        ffn_gate_part = chip_grad(own_ffn_gate, other_ffn_gate, flat_gate_grad, other_gate_grad)
        value_quad = quarters(ffn_value_part)
        value_corner = send_corner(value_quad)
        key_quad = quarters(
            jnp.concatenate(
                [ffn_key_part[:, :, q : q + 1024] for q in range(0, 4096, 1024)] + [ffn_gate_part],
                axis=1,
            )
        )
        value_from = send_sides(*add_corner(value_quad, *value_corner))
        value_first, value_outgoing = add_sides(value_quad, *value_from)
    else:
        grad_ffn_value = weight_grad(hidden, value_grad)
        grad_ffn_key = weight_grad(ffn_key_in, pre_grad)
        grad_ffn_gate = weight_grad(ffn_gate_in, ffn_gate_grad)
    key_two_grad = project_back(tied(pre_grad, ffn_value_part, key_quad) if tuned else pre_grad, matrices[4])
    gate_two_grad = project_back(ffn_gate_grad, matrices[6])
    spread_two = normed_two - before_two
    grad_ffn_mix_key = jnp.sum(key_two_grad * spread_two, axis=(0, 1))
    grad_ffn_mix_gate = jnp.sum(gate_two_grad * spread_two, axis=(0, 1))
    normed_two_grad = (
        key_two_grad * feature_lookup_mixture + gate_two_grad * feature_receptance_mixture
    )
    before_two_grad = (
        key_two_grad * (1.0 - feature_lookup_mixture)
        + gate_two_grad * (1.0 - feature_receptance_mixture)
    ) * keep_mask
    from_right = shifted(before_two_grad[:, :1, :], "seq", -1)
    normed_two_grad = normed_two_grad + jnp.concatenate(
        [before_two_grad[:, 1:, :], from_right], axis=1
    )
    middle_norm_grad, grad_gain_two, grad_bias_two = norm_backward(
        normed_two_grad, unit_two, inv_two, closing_standardize_scale
    )
    middle_grad = grad_out + middle_norm_grad
    branch_grad = middle_grad.astype(jnp.bfloat16)
    if tuned:
        flat_branch_grad = branch_grad.reshape(-1, width)
        (other_branch_grad,) = sent_together([flat_branch_grad])
        output_part = chip_grad(own_gated, other_gated, flat_branch_grad, other_branch_grad)
        value_got = send_column(value_outgoing)
        key_sides = add_corner(key_quad, *send_corner(key_quad))
    else:
        grad_output = weight_grad(gated, branch_grad)
    gated_grad = project_back(
        tied(branch_grad, *value_outgoing) if tuned else branch_grad, matrices[3]
    )
    gate_pre_grad = (gated_grad * mixed * gates * (1.0 - gates)).astype(jnp.bfloat16)
    blended_gradient = gated_grad * gates
    if tuned:
        blended_gradient = tied(blended_gradient, *key_sides)
    (
        key_gradient,
        value_gradient,
        decay_gradient,
        reward_derivative,
        numerator_gradient,
        denominator_gradient,
    ) = weighted_value_backward(blended_gradient)
    if tuned:
        key_from = send_sides(*key_sides)
        key_first, key_outgoing = add_sides(key_quad, *key_from)
    num_next, den_next = carried_in(
        jnp.stack([numerator_gradient, denominator_gradient]), starts_in, decay_vec, length, True
    )
    num_tail = tail_fade * num_next[:, None, :]
    den_tail = tail_fade * den_next[:, None, :]
    tail_grad = powered_lookups * (value_row_block * num_tail + den_tail)
    key_gradient = key_gradient + tail_grad
    value_gradient = value_gradient + powered_lookups * num_tail
    offsets = (jnp.arange(length).astype(jnp.float32) - (length - 1))[:, None]
    block_fade = clear_flag * jnp.exp(-length * decay_vec)
    decay_gradient = decay_gradient + jnp.sum(offsets * tail_grad, axis=(0, 1))
    decay_gradient = decay_gradient - length * jnp.sum(
        block_fade * (state_numerator * num_next + state_denominator * den_next), axis=0
    )
    key_grad16 = key_gradient.astype(jnp.bfloat16)
    val_grad16 = value_gradient.astype(jnp.bfloat16)
    if tuned:
        flat_grads = [g.reshape(-1, width) for g in (key_grad16, val_grad16, gate_pre_grad)]
        other_grads = sent_together(flat_grads)
        key_part = chip_grad(own_key, other_key, flat_grads[0], other_grads[0])
        value_part = chip_grad(own_value, other_value, flat_grads[1], other_grads[1])
        gate_part = chip_grad(own_gate, other_gate, flat_grads[2], other_grads[2])
        time_quad = quarters(
            jnp.concatenate([key_part, value_part, gate_part, output_part], axis=1)
        )
        key_got = send_column(key_outgoing)
        time_sides = add_corner(time_quad, *send_corner(time_quad))
        time_from = send_sides(*time_sides)
        time_first, time_outgoing = add_sides(time_quad, *time_from)
        time_total = add_all(time_first, send_column(time_outgoing))
        grad_key, grad_value, grad_gate, grad_output = (
            time_total[i : i + 32] for i in (0, 32, 64, 96)
        )
        grad_ffn_value = add_all(value_first, value_got)
        key_total = add_all(key_first, key_got)
        grad_ffn_key = jnp.concatenate([key_total[i : i + 32] for i in (0, 32, 64, 96)], axis=1)
        grad_ffn_gate = key_total[128:]
    else:
        grad_key = weight_grad(key_in, key_grad16)
        grad_value = weight_grad(value_in, val_grad16)
        grad_gate = weight_grad(gate_in, gate_pre_grad)
    key_in_grad = project_back(
        tied(key_grad16, time_quad, *key_outgoing) if tuned else key_grad16, matrices[0]
    )
    value_in_grad = project_back(val_grad16, matrices[1])
    gate_in_grad = project_back(gate_pre_grad, matrices[2])
    spread_one = normed_one - before_one
    grad_mix_key = jnp.sum(key_in_grad * spread_one, axis=(0, 1))
    grad_mix_value = jnp.sum(value_in_grad * spread_one, axis=(0, 1))
    grad_mix_gate = jnp.sum(gate_in_grad * spread_one, axis=(0, 1))
    normed_one_grad = (
        key_in_grad * temporal_lookup_mixture
        + value_in_grad * temporal_content_mixture
        + gate_in_grad * temporal_receptance_mixture
    )
    before_one_grad = (
        key_in_grad * (1.0 - temporal_lookup_mixture)
        + value_in_grad * (1.0 - temporal_content_mixture)
        + gate_in_grad * (1.0 - temporal_receptance_mixture)
    ) * keep_mask
    from_next = shifted(before_one_grad[:, :1, :], "seq", -1)
    normed_one_grad = normed_one_grad + jnp.concatenate(
        [before_one_grad[:, 1:, :], from_next], axis=1
    )
    input_norm_grad, grad_gain_one, grad_bias_one = norm_backward(
        normed_one_grad, unit_one, inv_one, opening_standardize_scale
    )
    input_grad = middle_grad + input_norm_grad
    vector_grads = jnp.stack(
        [
            grad_gain_one,
            grad_bias_one,
            grad_mix_key,
            grad_mix_value,
            grad_mix_gate,
            decay_gradient,
            reward_derivative,
            grad_gain_two,
            grad_bias_two,
            grad_ffn_mix_key,
            grad_ffn_mix_gate,
        ]
    )
    if tuned:
        vector_grads = sum_vectors(vector_grads, flat)
    else:
        vector_grads = lax.psum_scatter(vector_grads, BOTH, scatter_dimension=1, tiled=True)
    return (
        output,
        input_grad,
        vector_grads[0],
        vector_grads[1],
        vector_grads[2],
        vector_grads[3],
        vector_grads[4],
        vector_grads[5],
        vector_grads[6],
        grad_key,
        grad_value,
        grad_gate,
        grad_output,
        vector_grads[7],
        vector_grads[8],
        vector_grads[9],
        vector_grads[10],
        grad_ffn_key,
        grad_ffn_value,
        grad_ffn_gate,
    )


def solution(mesh):
    tuned = tuple(mesh.shape.items()) == (("batch", 4), ("seq", 8))
    return jax.shard_map(
        partial(shards, tuned),
        mesh=mesh,
        in_specs=(
            P("batch", "seq", None),
            P("batch", None),
            P("batch", "seq", None),
            P(("batch", "seq")),
            P(("batch", "seq")),
            P(("batch", "seq")),
            P(("batch", "seq")),
            P(("batch", "seq")),
            P(("batch", "seq")),
            P(("batch", "seq")),
            P(("batch", "seq"), None),
            P(("batch", "seq"), None),
            P(("batch", "seq"), None),
            P(("batch", "seq"), None),
            P(("batch", "seq")),
            P(("batch", "seq")),
            P(("batch", "seq")),
            P(("batch", "seq")),
            P(("batch", "seq"), None),
            P(("batch", "seq"), None),
            P(("batch", "seq"), None),
        ),
        out_specs=(
            P("batch", "seq", None),
            P("batch", "seq", None),
            P(("batch", "seq")),
            P(("batch", "seq")),
            P(("batch", "seq")),
            P(("batch", "seq")),
            P(("batch", "seq")),
            P(("batch", "seq")),
            P(("batch", "seq")),
            P(("batch", "seq"), None),
            P(("batch", "seq"), None),
            P(("batch", "seq"), None),
            P(("batch", "seq"), None),
            P(("batch", "seq")),
            P(("batch", "seq")),
            P(("batch", "seq")),
            P(("batch", "seq")),
            P(("batch", "seq"), None),
            P(("batch", "seq"), None),
            P(("batch", "seq"), None),
        ),
        check_vma=False,
    )
```

```python
from functools import partial

import jax
import jax.numpy as jnp
from jax import lax
from jax.experimental import pallas as pl
from jax.experimental.pallas import tpu as pltpu
from jax.sharding import PartitionSpec as P

eps = 1e-05
highest = lax.Precision.HIGHEST
BOTH = ("batch", "seq")


def moved(rule):
    return [(f, rule(f)) for f in range(32)]


FLIP_X = moved(lambda f: f ^ 8)
FLIP_Y = moved(lambda f: f ^ 16)
FLIP_C = moved(lambda f: f ^ 1)


def turn_z(by):
    return moved(lambda f: (f & 25) | ((((f >> 1) + by) & 3) << 1))


def sent(array, pairs):
    return lax.ppermute(array, BOTH, pairs)


def place_of(flat, dy, dx, dz, dc):
    turned = ((((flat >> 1) & 3) + dz) & 3) * 2
    return ((flat & 25) | turned) ^ (dy * 16 + dx * 8 + dc)


def tied(array, *after):
    zero = jnp.zeros((), jnp.float32)
    for other in after:
        first = other[(0,) * other.ndim].astype(jnp.float32)
        zero = zero + jnp.minimum(jnp.abs(first), 0.0)
    return array + zero.astype(array.dtype)


def all_tied(arrays, after):
    return [tied(array, after) for array in arrays]


def assemble_kernel(owners, start, columns, slots_ref, *refs):
    pieces, out_ref, sems = refs[:-2], refs[-2], refs[-1]
    rows = out_ref.shape[1]
    copies = []
    number = 0
    for piece, count in zip(pieces, owners):
        for k in range(count):
            for q in range(columns):
                copies.append(
                    pltpu.make_async_copy(
                        piece.at[k, pl.ds(start + q * rows, rows), :],
                        out_ref.at[slots_ref[number], :, pl.ds(q * 1024, 1024)],
                        sems.at[number, q],
                    )
                )
            number += 1
    for copy in copies:
        copy.start()
    for copy in copies:
        copy.wait()


def assemble(pieces, slots, start, rows, columns):
    counts = [piece.shape[0] for piece in pieces]
    shape = (32, rows, columns * 1024)
    whole = pl.pallas_call(
        partial(assemble_kernel, counts, start, columns),
        out_shape=jax.ShapeDtypeStruct(shape, pieces[0].dtype),
        in_specs=[pl.BlockSpec(memory_space=pltpu.SMEM)]
        + [pl.BlockSpec(memory_space=pltpu.HBM)] * len(pieces),
        out_specs=pl.BlockSpec(memory_space=pltpu.VMEM),
        scratch_shapes=[pltpu.SemaphoreType.DMA((32, columns))],
        compiler_params=pltpu.CompilerParams(vmem_limit_bytes=24 * 1024 * 1024),
        cost_estimate=pl.CostEstimate(
            flops=0, transcendentals=0, bytes_accessed=2 * 2 * 32 * rows * columns * 1024
        ),
    )(slots, *pieces)
    return whole.reshape(32 * rows, columns * 1024)


def stacked(parts):
    rows = [part[:, q : q + 1024] for part in parts for q in range(0, part.shape[1], 1024)]
    return jnp.concatenate(rows, axis=0) if len(rows) > 1 else rows[0]


def around(part):
    return [sent(part, turn_z(d)) for d in (1, 2, 3)]


def long_slots(flat):
    every = (0, 1, 2, 3)
    steps = [(0, 0, every), (0, 1, every), (1, 0, every), (1, 1, (0, 1)), (1, 1, (2, 3))]
    return jnp.stack(
        [place_of(flat, dy, dx, -dz, dc) for dc in (0, 1) for dy, dx, dzs in steps for dz in dzs]
    ).astype(jnp.int32)


def send_far(from_x, from_y):
    half = from_x.shape[0] // 2
    return sent(from_x[:half], FLIP_Y), sent(from_y[half:], FLIP_X)


def both_cores(pieces):
    return pieces + [sent(piece, FLIP_C) for piece in pieces]


def choice(flat, width):
    index = jnp.arange(width)
    block, within = index // (width // 32), index % (width // 32)
    dc, rest = block >> 4, block & 15
    dy, dx, dz = rest >> 3, (rest >> 2) & 1, rest & 3
    wanted = place_of(flat, dy, dx, dz, dc) * (width // 32) + within
    return (jnp.arange(width)[:, None] == wanted[None, :]).astype(jnp.bfloat16)


def dot_nt(left, right):
    return lax.dot_general(
        left, right, (((1,), (1,)), ((), ())), preferred_element_type=jnp.float32
    )


def channel_kernel(slots_ref, *refs):
    key_in_ref, gate_in_ref, middle_ref, grad_ref, late_ref = refs[:5]
    refs = refs[5:]
    out_ref, value_grad_ref, gate_grad_ref, key_back_ref, gate_back_ref = refs[:5]
    hidden_ref, far_hidden_ref, pre_grad_ref, key_w, value_w, gate_w = refs[5:11]
    relu_s, hidden_s, pre_s, total_s, in_sems, hidden_sems, pre_sems = refs[11:]

    def key_copy(q):
        return pltpu.make_async_copy(
            late_ref.at[:, pl.ds(q * 32, 32), :], key_w.at[q], in_sems.at[q]
        )

    def value_copy(q):
        return pltpu.make_async_copy(
            late_ref.at[pl.ds(q * 8, 8), pl.ds(128, 128), :],
            value_w.at[pl.ds(q * 8, 8)],
            in_sems.at[4 + q],
        )

    gate_copy = pltpu.make_async_copy(
        late_ref.at[:, pl.ds(256, 32), :], gate_w, in_sems.at[8]
    )
    for q in range(4):
        key_copy(q).start()
        value_copy(q).start()
    gate_copy.start()

    def hidden_copy(q, k, target):
        return pltpu.make_async_copy(
            hidden_s.at[q, :, pl.ds(k * 128, 128)], target, hidden_sems.at[q, k]
        )

    def hidden_start(q, k):
        slot = slots_ref[q * 8 + k]
        columns = pl.ds(pl.multiple_of((slot & 3) * 128, 128), 128)

        @pl.when(slot < 16)
        def _():
            hidden_copy(q, k, hidden_ref.at[slot >> 2, :, columns]).start()

        @pl.when(slot >= 16)
        def _():
            hidden_copy(q, k, far_hidden_ref.at[(slot >> 2) - 4, :, columns]).start()

    def pre_copy(q):
        return pltpu.make_async_copy(
            pre_s.at[q], pre_grad_ref.at[:, pl.ds(pl.multiple_of(q * 1024, 1024), 1024)], pre_sems.at[q]
        )

    def forward(q, _):
        key_copy(q).wait()
        for half in range(2):
            rows = pl.ds(half * 256, 256)
            relu_s[q, rows, :] = jnp.maximum(
                jnp.dot(
                    key_in_ref[rows, :],
                    key_w[q].reshape(1024, 1024),
                    preferred_element_type=jnp.float32,
                ),
                0.0,
            )
            hidden_s[q, rows, :] = (relu_s[q, rows, :] * relu_s[q, rows, :]).astype(jnp.bfloat16)
        for k in range(8):
            hidden_start(q, k)
        value_copy(q).wait()
        for half in range(2):
            rows = pl.ds(half * 256, 256)
            more = jnp.dot(
                hidden_s[q, rows, :],
                value_w[pl.ds(q * 8, 8)].reshape(1024, 1024),
                preferred_element_type=jnp.float32,
            )

            @pl.when(q == 0)
            def _():
                total_s[rows, :] = more

            @pl.when(q > 0)
            def _():
                total_s[rows, :] += more

        return 0

    lax.fori_loop(0, 4, forward, 0)
    gate_copy.wait()
    for half in range(2):
        rows = pl.ds(half * 256, 256)
        gates = jax.nn.sigmoid(
            jnp.dot(
                gate_in_ref[rows, :],
                gate_w[...].reshape(1024, 1024),
                preferred_element_type=jnp.float32,
            )
        )
        value = total_s[rows, :]
        grads = grad_ref[rows, :].astype(jnp.float32)
        out_ref[rows, :] = (middle_ref[rows, :] + gates * value).astype(jnp.bfloat16)
        value_grad_ref[rows, :] = (grads * gates).astype(jnp.bfloat16)
        gate_grad_ref[rows, :] = (grads * value * gates * (1.0 - gates)).astype(jnp.bfloat16)

    def backward(q, _):
        for half in range(2):
            rows = pl.ds(half * 256, 256)
            pre_s[q, rows, :] = (
                dot_nt(value_grad_ref[rows, :], value_w[pl.ds(q * 8, 8)].reshape(1024, 1024))
                * 2.0
                * relu_s[q, rows, :]
            ).astype(jnp.bfloat16)
        pre_copy(q).start()
        for half in range(2):
            rows = pl.ds(half * 256, 256)
            more = dot_nt(pre_s[q, rows, :], key_w[q].reshape(1024, 1024))

            @pl.when(q == 0)
            def _():
                key_back_ref[rows, :] = more

            @pl.when(q > 0)
            def _():
                key_back_ref[rows, :] += more

        return 0

    lax.fori_loop(0, 4, backward, 0)
    for half in range(2):
        rows = pl.ds(half * 256, 256)
        gate_back_ref[rows, :] = dot_nt(gate_grad_ref[rows, :], gate_w[...].reshape(1024, 1024))
    for q in range(4):
        for k in range(8):
            hidden_copy(q, k, hidden_ref.at[0, :, pl.ds(0, 128)]).wait()
        pre_copy(q).wait()


def channel_mix(slots, key_in, gate_in, middle, grads, late):
    tokens = key_in.shape[0]
    wide_rows = jax.ShapeDtypeStruct((tokens, 1024), jnp.float32)
    half_rows = jax.ShapeDtypeStruct((tokens, 1024), jnp.bfloat16)
    whole = pl.BlockSpec(memory_space=pltpu.VMEM)
    far = pl.BlockSpec(memory_space=pltpu.HBM)
    return pl.pallas_call(
        channel_kernel,
        out_shape=(
            half_rows,
            half_rows,
            half_rows,
            wide_rows,
            wide_rows,
            jax.ShapeDtypeStruct((4, tokens, 512), jnp.bfloat16),
            jax.ShapeDtypeStruct((4, tokens, 512), jnp.bfloat16),
            jax.ShapeDtypeStruct((tokens, 4096), jnp.bfloat16),
        ),
        in_specs=[pl.BlockSpec(memory_space=pltpu.SMEM), whole, whole, whole, whole, far],
        out_specs=(whole,) * 5 + (far,) * 3,
        scratch_shapes=[
            pltpu.VMEM((4, 32, 32, 1024), jnp.bfloat16),
            pltpu.VMEM((32, 128, 1024), jnp.bfloat16),
            pltpu.VMEM((32, 32, 1024), jnp.bfloat16),
            pltpu.VMEM((4, tokens, 1024), jnp.float32),
            pltpu.VMEM((4, tokens, 1024), jnp.bfloat16),
            pltpu.VMEM((4, tokens, 1024), jnp.bfloat16),
            pltpu.VMEM((tokens, 1024), jnp.float32),
            pltpu.SemaphoreType.DMA((9,)),
            pltpu.SemaphoreType.DMA((4, 8)),
            pltpu.SemaphoreType.DMA((4,)),
        ],
        compiler_params=pltpu.CompilerParams(vmem_limit_bytes=54 * 1024 * 1024),
        cost_estimate=pl.CostEstimate(
            flops=2 * tokens * 1024 * 1024 * 18, transcendentals=0, bytes_accessed=40 * 1024 * 1024
        ),
    )(slots, key_in, gate_in, middle, grads, late)


def owner_slots(flat):
    other = jnp.arange(32)
    apart = other ^ flat
    dz = ((other >> 1) - (flat >> 1)) & 3
    return ((apart & 1) * 16 + ((apart >> 4) & 1) * 8 + ((apart >> 3) & 1) * 4 + dz).astype(jnp.int32)


def dot_tn(left, right):
    return lax.dot_general(
        left, right, (((0,), (0,)), ((), ())), preferred_element_type=jnp.float32
    )


def chip_rows(own_in, own_grads, other_in, other_grads):
    return (dot_tn(own_in, own_grads) + dot_tn(other_in, other_grads)).astype(jnp.bfloat16)


def value_part_kernel(own_ref, other_ref, grad_ref, other_grad_ref, near, side_x, side_y, far_a, far_b):
    quarter = pl.program_id(0)
    part = chip_rows(own_ref[0], grad_ref[...], other_ref[0], other_grad_ref[...])
    part = part.reshape((4, part.shape[0] // 4, 1024))

    @pl.when(quarter == 0)
    def _():
        near[...] = part

    @pl.when(quarter == 1)
    def _():
        side_x[...] = part

    @pl.when(quarter == 2)
    def _():
        side_y[...] = part

    @pl.when(quarter == 3)
    def _():
        far_a[...] = part[:2]
        far_b[...] = part[2:]


def store_quarters(part, outs):
    near, side_x, side_y, far_a, far_b = outs
    quarters = part.reshape(4, 4, 32, 1024)
    near[...] = quarters[0]
    side_x[...] = quarters[1]
    side_y[...] = quarters[2]
    far_a[...] = quarters[3, :2]
    far_b[...] = quarters[3, 2:]


def key_part_kernel(key_ref, other_key_ref, gate_ref, other_gate_ref, *refs):
    pre_ref, other_pre_ref, gate_grad_ref, other_gate_grad_ref = refs[:4]
    step = pl.program_id(0)

    @pl.when(step < 4)
    def _():
        store_quarters(
            chip_rows(key_ref[...], pre_ref[...], other_key_ref[...], other_pre_ref[...]), refs[4:]
        )

    @pl.when(step == 4)
    def _():
        store_quarters(
            chip_rows(
                gate_ref[...], gate_grad_ref[...], other_gate_ref[...], other_gate_grad_ref[...]
            ),
            refs[4:],
        )


def time_part_kernel(own_ref, other_ref, grad_ref, other_grad_ref, *refs):
    branch_ref, other_branch_ref = refs[:2]
    step = pl.program_id(0)

    @pl.when(step < 3)
    def _():
        store_quarters(
            chip_rows(own_ref[...], grad_ref[...], other_ref[...], other_grad_ref[...]), refs[2:]
        )

    @pl.when(step == 3)
    def _():
        store_quarters(
            chip_rows(own_ref[...], branch_ref[...], other_ref[...], other_branch_ref[...]), refs[2:]
        )


def quarters_call(kernel, steps, rows, in_specs, by_quarter, arguments):
    if by_quarter:
        outs = [pl.BlockSpec((n, rows, 1024), lambda i: (0, 0, 0)) for n in (4, 4, 4, 2, 2)]
    else:
        outs = [pl.BlockSpec((n, 32, 1024), lambda i: (0, i, 0)) for n in (4, 4, 4, 2, 2)]
    return pl.pallas_call(
        kernel,
        grid=(steps,),
        out_shape=tuple(
            jax.ShapeDtypeStruct((n, rows, 1024), jnp.bfloat16) for n in (4, 4, 4, 2, 2)
        ),
        in_specs=in_specs,
        out_specs=tuple(outs),
        compiler_params=pltpu.CompilerParams(vmem_limit_bytes=48 * 1024 * 1024),
        cost_estimate=pl.CostEstimate(
            flops=2 * 1024 * 16 * rows * 1024,
            transcendentals=0,
            bytes_accessed=(16 * rows + 8 * 1024) * 2048,
        ),
    )(*arguments)


def value_part(own_hidden, other_hidden, grads, other_grads):
    tokens = grads.shape[0]
    whole = pl.BlockSpec((tokens, 1024), lambda i: (0, 0))
    block = pl.BlockSpec((1, tokens, 512), lambda i: (i, 0, 0))
    return quarters_call(
        value_part_kernel,
        4,
        128,
        [block, block, whole, whole],
        True,
        (own_hidden, other_hidden, grads, other_grads),
    )


def key_part(key, other_key, gate, other_gate, pre, other_pre, gate_grad, other_gate_grad):
    tokens = pre.shape[0]
    half = pl.BlockSpec((tokens, 512), lambda i: (0, 0))
    whole = pl.BlockSpec((tokens, 1024), lambda i: (0, 0))
    block = pl.BlockSpec((tokens, 1024), lambda i: (0, jnp.minimum(i, 3)))
    return quarters_call(
        key_part_kernel,
        5,
        160,
        [half, half, half, half, block, block, whole, whole],
        False,
        (key, other_key, gate, other_gate, pre, other_pre, gate_grad, other_gate_grad),
    )


def time_part(own, other, grads, other_grads, branch, other_branch):
    tokens = grads.shape[0]
    half = pl.BlockSpec((tokens, 512), lambda i: (0, i))
    whole = pl.BlockSpec((tokens, 1024), lambda i: (0, 0))
    block = pl.BlockSpec((tokens, 1024), lambda i: (0, jnp.minimum(i, 2)))
    return quarters_call(
        time_part_kernel,
        4,
        128,
        [half, half, block, block, whole, whole],
        False,
        (own, other, grads, other_grads, branch, other_branch),
    )


def ordered_halves(rows_in, flat):
    width = rows_in.shape[-1]
    rows_in = rows_in.reshape(-1, width)
    ordered = jnp.dot(rows_in, choice(flat, width), preferred_element_type=jnp.bfloat16)
    return ordered[:, : width // 2], ordered[:, width // 2 :]


def sent_together(arrays):
    got = sent(jnp.concatenate(arrays, axis=1) if len(arrays) > 1 else arrays[0], FLIP_C)
    ends = [sum(a.shape[1] for a in arrays[: i + 1]) for i in range(len(arrays))]
    return [got[:, end - a.shape[1] : end] for a, end in zip(arrays, ends)]


def wide(array):
    return array.astype(jnp.float32)


def narrow(array):
    return array.astype(jnp.bfloat16)


def send_corner(parts):
    return sent(parts[3], FLIP_X), sent(parts[4], FLIP_Y)


def add_corner(parts, add_a, add_b):
    to_y = jnp.concatenate([narrow(wide(parts[2][:2]) + wide(add_a)), parts[2][2:]])
    to_x = jnp.concatenate([parts[1][:2], narrow(wide(parts[1][2:]) + wide(add_b))])
    return to_y, to_x


def send_sides(to_y, to_x):
    return sent(to_y, FLIP_Y), sent(to_x, FLIP_X)


def add_sides(parts, from_y, from_x):
    column = wide(parts[0]) + wide(from_y) + wide(from_x)
    return column[0], [narrow(column[d]) for d in (1, 2, 3)]


def send_column(outgoing):
    return [sent(part, turn_z(d)) for d, part in zip((1, 2, 3), outgoing)]


def add_all(first, others):
    for other in others:
        first = first + wide(other)
    return first


def sum_vectors(rows_in, flat):
    total = rows_in + sum(sent(rows_in, turn_z(d)) for d in (1, 2, 3))
    for pairs in (FLIP_X, FLIP_Y, FLIP_C):
        total = total + sent(total, pairs)
    count = total.shape[1] // 32
    return lax.dynamic_slice_in_dim(total, flat * count, count, 1)


def shifted(shard, axis, by):
    length = lax.axis_size(axis)
    pairs = [(i, i + by) for i in range(length) if 0 <= i + by < length]
    return lax.ppermute(shard, axis, pairs)


def carried_in(part, starts_in, decay_vec, length, reverse):
    count = lax.axis_size("seq")
    place = lax.axis_index("seq")
    clear = 1.0 - starts_in.astype(jnp.float32)
    block_fade = jnp.exp(-length * decay_vec)

    def clear_of(block):
        return lax.dynamic_index_in_dim(clear, jnp.clip(block, 0, count - 1), 1, True)

    if count == 8:
        chip, core = place >> 1, place & 1
        other = sent(part, FLIP_C)
        is_far = (core == 1) == (not reverse)
        near = jnp.where(is_far, other, part)
        last = jnp.where(is_far, part, other)
        first_block, second_block = chip * 2 + (1 if reverse else 0), chip * 2 + (0 if reverse else 1)
        joined = clear_of(second_block) * block_fade * near + last
        step = -1 if reverse else 1
        entering = jnp.zeros_like(part)
        open_way = jnp.ones((part.shape[1], 1), jnp.float32)
        for d in (1, 2, 3):
            beside = chip - step * d
            live = ((beside >= 0) & (beside < 4)).astype(jnp.float32)
            fade = live * open_way * jnp.exp(-float(2 * (d - 1) * length) * decay_vec)
            entering = entering + fade * sent(joined, turn_z(step * d))
            open_way = open_way * clear_of(2 * beside) * clear_of(2 * beside + 1)
        return jnp.where(is_far, clear_of(first_block) * block_fade * entering + near, entering)
    gathered = lax.all_gather(part, "seq")

    def one(lap, state):
        source = count - 1 - lap if reverse else lap
        return clear_of(source) * block_fade * state + lax.dynamic_index_in_dim(gathered, source, 0, False)

    ahead = count - 1 - place if reverse else place
    return lax.fori_loop(0, ahead, one, jnp.zeros_like(part))


def norm_forward(values, gain_vec, bias_vec):
    centre = values - jnp.mean(values, axis=-1, keepdims=True)
    inv_std = lax.rsqrt(jnp.mean(centre * centre, axis=-1, keepdims=True) + eps)
    normed = centre * inv_std
    return (normed * gain_vec + bias_vec, normed, inv_std)


def norm_backward(grads, normed, inv_std, gain_vec):
    scaled = grads * gain_vec
    inner = (
        scaled
        - jnp.mean(scaled, axis=-1, keepdims=True)
        - normed * jnp.mean(scaled * normed, axis=-1, keepdims=True)
    )
    return (inv_std * inner, jnp.sum(grads * normed, axis=(0, 1)), jnp.sum(grads, axis=(0, 1)))


def project(rows_in, weight):
    return jnp.einsum("rtd,de->rte", rows_in, weight, preferred_element_type=jnp.float32)


def project_back(grads, weight):
    return jnp.einsum("rte,de->rtd", grads, weight, preferred_element_type=jnp.float32)


def weight_grad(rows_in, grads):
    total = jnp.einsum("rtd,rte->de", rows_in, grads, preferred_element_type=jnp.float32)
    return lax.psum_scatter(total, BOTH, scatter_dimension=0, tiled=True)


def weighted_value_local(
    key_row_block,
    value_row_block,
    feature_forgetting_rate,
    present_reward,
    state_numerator,
    state_denominator,
    document_segments,
):
    length = key_row_block.shape[1]
    width = key_row_block.shape[2]
    order_idx = jnp.arange(length)
    step_pos = order_idx.astype(jnp.float32)[:, None]
    powered_lookups = jnp.exp(key_row_block)
    grow_exp = jnp.exp(step_pos * feature_forgetting_rate)
    shrink = jnp.exp((1.0 - step_pos) * feature_forgetting_rate)
    pair_mask = (
        (order_idx[None, :] < order_idx[:, None])[None]
        & (document_segments[:, None, :] == document_segments[:, :, None])
    ).astype(jnp.float32)
    weighted = jnp.concatenate(
        [powered_lookups * value_row_block, powered_lookups], axis=2
    ) * jnp.concatenate([grow_exp, grow_exp], axis=1)
    past_sums = jnp.einsum(
        "rti,rie->rte", pair_mask, weighted, precision=highest
    ) * jnp.concatenate([shrink, shrink], axis=1)
    carry_fade = (document_segments == 0).astype(jnp.float32)[:, :, None] * jnp.exp(
        -step_pos * feature_forgetting_rate
    )
    present_token_contribution = jnp.exp(present_reward) * powered_lookups
    numer = (
        carry_fade * state_numerator[:, None, :]
        + past_sums[:, :, :width]
        + present_token_contribution * value_row_block
    )
    denom = (
        carry_fade * state_denominator[:, None, :]
        + past_sums[:, :, width:]
        + present_token_contribution
    )
    return numer / denom


def tail_terms(key_row_block, value_row_block, feature_forgetting_rate, document_segments):
    length = key_row_block.shape[1]
    step_pos = jnp.arange(length).astype(jnp.float32)[:, None]
    powered_lookups = jnp.exp(key_row_block)
    tail_fade = (document_segments == document_segments[:, -1:]).astype(jnp.float32)[
        :, :, None
    ] * jnp.exp((step_pos - (length - 1)) * feature_forgetting_rate)
    return (
        jnp.sum(tail_fade * powered_lookups * value_row_block, axis=1),
        jnp.sum(tail_fade * powered_lookups, axis=1),
        tail_fade,
        powered_lookups,
    )


def shards(
    tuned,
    incoming_activations,
    sequence_extents,
    upstream_sensitivity,
    initial_normalizer_scale,
    initial_normalizer_offset,
    temporal_lookup_fraction,
    temporal_content_fraction,
    temporal_receptance_fraction,
    feature_forgetting_rate,
    present_reward,
    temporal_lookup_projection,
    temporal_content_projection,
    temporal_receptance_projection,
    temporal_result_projection,
    later_normalizer_scale,
    later_normalizer_offset,
    feature_lookup_fraction,
    feature_receptance_fraction,
    feature_lookup_projection,
    feature_content_projection,
    feature_receptance_projection,
):
    flat = lax.axis_index("batch") * lax.axis_size("seq") + lax.axis_index("seq")
    vectors = jnp.stack(
        [
            initial_normalizer_scale,
            initial_normalizer_offset,
            temporal_lookup_fraction,
            temporal_content_fraction,
            temporal_receptance_fraction,
            feature_forgetting_rate,
            present_reward,
            later_normalizer_scale,
            later_normalizer_offset,
            feature_lookup_fraction,
            feature_receptance_fraction,
        ]
    )
    if tuned:
        order = long_slots(flat)
        late = lax.all_gather(
            stacked(
                [
                    feature_lookup_projection,
                    feature_content_projection,
                    feature_receptance_projection,
                ]
            ),
            BOTH,
        )
        spread = jnp.tile(jnp.pad(vectors, ((0, 5), (0, 0))), (1, 32))
        packed = jnp.where(jnp.arange(1024) // 32 == flat, spread, jnp.zeros_like(spread))
        part = stacked(
            [
                temporal_lookup_projection,
                temporal_content_projection,
                temporal_receptance_projection,
                temporal_result_projection,
                packed,
            ]
        )
        column = jnp.stack([part] + around(part))
        from_x, from_y = sent(column, FLIP_X), sent(column, FLIP_Y)
        early = both_cores([column, from_x, from_y, *send_far(from_x, from_y)])
        vectors = jnp.sum(
            assemble(early, order, 128, 16, 1).reshape(32, 16, 1024).astype(jnp.float32), axis=0
        )
        lookup_weight = assemble(early, order, 0, 32, 1)
        content_weight = assemble(early, order, 32, 32, 1)
        receptance_weight = assemble(early, order, 64, 32, 1)
        result_weight = assemble(early, order, 96, 32, 1)
    else:
        (
            lookup_weight,
            content_weight,
            receptance_weight,
            result_weight,
            ffn_key_weight,
            ffn_gate_weight,
            ffn_value_weight,
        ) = [
            lax.all_gather(part, BOTH, axis=0, tiled=True)
            for part in (
                temporal_lookup_projection,
                temporal_content_projection,
                temporal_receptance_projection,
                temporal_result_projection,
                feature_lookup_projection,
                feature_receptance_projection,
                feature_content_projection,
            )
        ]
        vectors = lax.all_gather(vectors, BOTH, axis=1, tiled=True).astype(jnp.float32)
    (
        opening_standardize_scale,
        opening_standardize_offset,
        temporal_lookup_mixture,
        temporal_content_mixture,
        temporal_receptance_mixture,
        decay_vec,
        reward_array,
        closing_standardize_scale,
        closing_standardize_offset,
        feature_lookup_mixture,
        feature_receptance_mixture,
    ) = tuple(vectors[i] for i in range(11))
    rows, length, width = incoming_activations.shape
    starts = jnp.cumsum(sequence_extents, axis=1) - sequence_extents
    places = lax.axis_index("seq") * length + jnp.arange(length, dtype=jnp.int32)
    resets = jnp.any(
        (starts[:, None, :] == places[None, :, None]) & (sequence_extents[:, None, :] > 0), axis=2
    )
    document_segments = jnp.cumsum(resets.astype(jnp.int32), axis=1)
    keep_mask = 1.0 - resets.astype(jnp.float32)[:, :, None]
    clear_flag = (document_segments[:, -1:] == 0).astype(jnp.float32)
    starts_in = jnp.any(
        (starts[:, None, :] // length == jnp.arange(lax.axis_size("seq"))[None, :, None])
        & (sequence_extents[:, None, :] > 0),
        axis=2,
    )

    inputs = incoming_activations.astype(jnp.float32)
    left_rows = shifted(incoming_activations[:, length - 1 :, :], "seq", 1)
    normed_one, unit_one, inv_one = norm_forward(
        inputs, opening_standardize_scale, opening_standardize_offset
    )
    left_normed, _, _ = norm_forward(
        left_rows.astype(jnp.float32), opening_standardize_scale, opening_standardize_offset
    )
    before_one = jnp.concatenate([left_normed, normed_one[:, :-1, :]], axis=1) * keep_mask
    key_in = (
        normed_one * temporal_lookup_mixture + before_one * (1.0 - temporal_lookup_mixture)
    ).astype(jnp.bfloat16)
    value_in = (
        normed_one * temporal_content_mixture + before_one * (1.0 - temporal_content_mixture)
    ).astype(jnp.bfloat16)
    gate_in = (
        normed_one * temporal_receptance_mixture + before_one * (1.0 - temporal_receptance_mixture)
    ).astype(jnp.bfloat16)
    key_row_block = project(key_in, lookup_weight)
    value_row_block = project(value_in, content_weight)
    gates = jax.nn.sigmoid(project(gate_in, receptance_weight))
    tail_num, tail_den, tail_fade, powered_lookups = tail_terms(
        key_row_block, value_row_block, decay_vec, document_segments
    )
    state_numerator, state_denominator = carried_in(
        jnp.stack([tail_num, tail_den]), starts_in, decay_vec, length, False
    )
    mixed, weighted_value_backward = jax.vjp(
        partial(weighted_value_local, document_segments=document_segments),
        key_row_block,
        value_row_block,
        decay_vec,
        reward_array,
        state_numerator,
        state_denominator,
    )
    gated = (gates * mixed).astype(jnp.bfloat16)
    if tuned:
        own_key, far_key = ordered_halves(key_in, flat)
        own_value, far_value = ordered_halves(value_in, flat)
        own_gate, far_gate = ordered_halves(gate_in, flat)
        own_gated, far_gated = ordered_halves(gated, flat)
        other_time = sent(
            jnp.concatenate([far_key, far_value, far_gate, far_gated], axis=1), FLIP_C
        )
        own_time = jnp.concatenate([own_key, own_value, own_gate, own_gated], axis=1)
    middle = inputs + project(gated, result_weight)
    normed_two, unit_two, inv_two = norm_forward(
        middle, closing_standardize_scale, closing_standardize_offset
    )
    before_rows = shifted(normed_two[:, length - 1 :, :], "seq", 1)
    before_two = jnp.concatenate([before_rows, normed_two[:, :-1, :]], axis=1) * keep_mask
    ffn_key_in = (
        normed_two * feature_lookup_mixture + before_two * (1.0 - feature_lookup_mixture)
    ).astype(jnp.bfloat16)
    ffn_gate_in = (
        normed_two * feature_receptance_mixture + before_two * (1.0 - feature_receptance_mixture)
    ).astype(jnp.bfloat16)
    grad_out = upstream_sensitivity.astype(jnp.float32)
    if tuned:
        own_ffn_key, far_ffn_key = ordered_halves(ffn_key_in, flat)
        own_ffn_gate, far_ffn_gate = ordered_halves(ffn_gate_in, flat)
        other_ffn_key, other_ffn_gate = sent_together([far_ffn_key, far_ffn_gate])
        output, value_grad, ffn_gate_grad, key_two_grad, gate_two_grad, *kept = channel_mix(
            owner_slots(flat),
            ffn_key_in.reshape(-1, width),
            ffn_gate_in.reshape(-1, width),
            middle.reshape(-1, width),
            upstream_sensitivity.reshape(-1, width),
            late,
        )
        output, key_two_grad, gate_two_grad = (
            a.reshape(rows, length, width) for a in (output, key_two_grad, gate_two_grad)
        )
        own_hidden, far_hidden, pre_grad = kept
        other_value_grad = sent(value_grad, FLIP_C)
        other_hidden = sent(far_hidden, FLIP_C)
        other_gate_grad = sent(ffn_gate_grad, FLIP_C)
        other_pre_grad = sent(pre_grad, FLIP_C)
        value_parts = value_part(own_hidden, other_hidden, value_grad, other_value_grad)
        value_corner = send_corner(value_parts)
        key_parts = key_part(
            own_ffn_key,
            other_ffn_key,
            own_ffn_gate,
            other_ffn_gate,
            pre_grad,
            other_pre_grad,
            ffn_gate_grad,
            other_gate_grad,
        )
        value_sides = add_corner(value_parts, *all_tied(value_corner, key_parts[4]))
        value_from = send_sides(*value_sides)
    else:
        hidden_pre = project(ffn_key_in, ffn_key_weight)
        hidden = jnp.square(jax.nn.relu(hidden_pre)).astype(jnp.bfloat16)
        ffn_value = project(hidden, ffn_value_weight)
        ffn_gates = jax.nn.sigmoid(project(ffn_gate_in, ffn_gate_weight))
        output = (middle + ffn_gates * ffn_value).astype(jnp.bfloat16)
        value_grad = (grad_out * ffn_gates).astype(jnp.bfloat16)
        ffn_gate_grad = (grad_out * ffn_value * ffn_gates * (1.0 - ffn_gates)).astype(jnp.bfloat16)
        hidden_grad = project_back(value_grad, ffn_value_weight)
        pre_grad = (hidden_grad * 2.0 * jax.nn.relu(hidden_pre)).astype(jnp.bfloat16)
        grad_ffn_value = weight_grad(hidden, value_grad)
        grad_ffn_key = weight_grad(ffn_key_in, pre_grad)
        grad_ffn_gate = weight_grad(ffn_gate_in, ffn_gate_grad)
        key_two_grad = project_back(pre_grad, ffn_key_weight)
        gate_two_grad = project_back(ffn_gate_grad, ffn_gate_weight)
    spread_two = normed_two - before_two
    grad_ffn_mix_key = jnp.sum(key_two_grad * spread_two, axis=(0, 1))
    grad_ffn_mix_gate = jnp.sum(gate_two_grad * spread_two, axis=(0, 1))
    normed_two_grad = (
        key_two_grad * feature_lookup_mixture + gate_two_grad * feature_receptance_mixture
    )
    before_two_grad = (
        key_two_grad * (1.0 - feature_lookup_mixture)
        + gate_two_grad * (1.0 - feature_receptance_mixture)
    ) * keep_mask
    from_right = shifted(before_two_grad[:, :1, :], "seq", -1)
    normed_two_grad = normed_two_grad + jnp.concatenate(
        [before_two_grad[:, 1:, :], from_right], axis=1
    )
    middle_norm_grad, grad_gain_two, grad_bias_two = norm_backward(
        normed_two_grad, unit_two, inv_two, closing_standardize_scale
    )
    middle_grad = grad_out + middle_norm_grad
    branch_grad = middle_grad.astype(jnp.bfloat16)
    if tuned:
        flat_branch_grad = branch_grad.reshape(-1, width)
        other_branch_grad = sent(flat_branch_grad, FLIP_C)
        key_corner = send_corner(key_parts)
    else:
        grad_output = weight_grad(gated, branch_grad)
    gated_grad = project_back(
        tied(branch_grad, value_sides[0]) if tuned else branch_grad, result_weight
    )
    gate_pre_grad = (gated_grad * mixed * gates * (1.0 - gates)).astype(jnp.bfloat16)
    blended_gradient = gated_grad * gates
    (
        key_gradient,
        value_gradient,
        decay_gradient,
        reward_derivative,
        numerator_gradient,
        denominator_gradient,
    ) = weighted_value_backward(blended_gradient)
    state_gradient = jnp.stack([numerator_gradient, denominator_gradient])
    if tuned:
        value_first, value_outgoing = add_sides(value_parts, *all_tied(value_from, state_gradient))
        key_sides = add_corner(key_parts, *all_tied(key_corner, state_gradient))
        key_from = send_sides(*key_sides)
        state_gradient = tied(state_gradient, key_sides[0], value_outgoing[0])
    num_next, den_next = carried_in(state_gradient, starts_in, decay_vec, length, True)
    num_tail = tail_fade * num_next[:, None, :]
    den_tail = tail_fade * den_next[:, None, :]
    tail_grad = powered_lookups * (value_row_block * num_tail + den_tail)
    key_gradient = key_gradient + tail_grad
    value_gradient = value_gradient + powered_lookups * num_tail
    offsets = (jnp.arange(length).astype(jnp.float32) - (length - 1))[:, None]
    block_fade = clear_flag * jnp.exp(-length * decay_vec)
    decay_gradient = decay_gradient + jnp.sum(offsets * tail_grad, axis=(0, 1))
    decay_gradient = decay_gradient - length * jnp.sum(
        block_fade * (state_numerator * num_next + state_denominator * den_next), axis=0
    )
    key_grad16 = key_gradient.astype(jnp.bfloat16)
    val_grad16 = value_gradient.astype(jnp.bfloat16)
    if tuned:
        flat_grads = jnp.concatenate(
            [g.reshape(-1, width) for g in (key_grad16, val_grad16, gate_pre_grad)], axis=1
        )
        other_grads = sent(flat_grads, FLIP_C)
        time_parts = time_part(
            own_time, other_time, flat_grads, other_grads, flat_branch_grad, other_branch_grad
        )
        value_got = all_tied(send_column(all_tied(value_outgoing, num_next)), time_parts[4])
        key_first, key_outgoing = add_sides(key_parts, *all_tied(key_from, time_parts[4]))
        time_corner = send_corner(time_parts)
    else:
        grad_key = weight_grad(key_in, key_grad16)
        grad_value = weight_grad(value_in, val_grad16)
        grad_gate = weight_grad(gate_in, gate_pre_grad)
    if tuned:
        key_grad16 = tied(key_grad16, key_outgoing[0])
    key_in_grad = project_back(key_grad16, lookup_weight)
    value_in_grad = project_back(val_grad16, content_weight)
    gate_in_grad = project_back(gate_pre_grad, receptance_weight)
    spread_one = normed_one - before_one
    grad_mix_key = jnp.sum(key_in_grad * spread_one, axis=(0, 1))
    grad_mix_value = jnp.sum(value_in_grad * spread_one, axis=(0, 1))
    grad_mix_gate = jnp.sum(gate_in_grad * spread_one, axis=(0, 1))
    normed_one_grad = (
        key_in_grad * temporal_lookup_mixture
        + value_in_grad * temporal_content_mixture
        + gate_in_grad * temporal_receptance_mixture
    )
    before_one_grad = (
        key_in_grad * (1.0 - temporal_lookup_mixture)
        + value_in_grad * (1.0 - temporal_content_mixture)
        + gate_in_grad * (1.0 - temporal_receptance_mixture)
    ) * keep_mask
    if tuned:
        time_sides = add_corner(time_parts, *all_tied(time_corner, before_one_grad))
        time_from = send_sides(*time_sides)
    from_next = shifted(before_one_grad[:, :1, :], "seq", -1)
    if tuned:
        key_got = send_column(all_tied(key_outgoing, from_next))
    normed_one_grad = normed_one_grad + jnp.concatenate(
        [before_one_grad[:, 1:, :], from_next], axis=1
    )
    input_norm_grad, grad_gain_one, grad_bias_one = norm_backward(
        normed_one_grad, unit_one, inv_one, opening_standardize_scale
    )
    if tuned:
        time_first, time_outgoing = add_sides(time_parts, *time_from)
        time_total = add_all(time_first, send_column(time_outgoing))
        grad_key, grad_value, grad_gate, grad_output = (
            time_total[i : i + 32] for i in (0, 32, 64, 96)
        )
        grad_ffn_value = add_all(value_first, value_got)
        key_total = add_all(key_first, key_got)
        grad_ffn_key = jnp.concatenate([key_total[i : i + 32] for i in (0, 32, 64, 96)], axis=1)
        grad_ffn_gate = key_total[128:]
    input_grad = middle_grad + input_norm_grad
    vector_grads = jnp.stack(
        [
            grad_gain_one,
            grad_bias_one,
            grad_mix_key,
            grad_mix_value,
            grad_mix_gate,
            decay_gradient,
            reward_derivative,
            grad_gain_two,
            grad_bias_two,
            grad_ffn_mix_key,
            grad_ffn_mix_gate,
        ]
    )
    if tuned:
        vector_grads = sum_vectors(vector_grads, flat)
    else:
        vector_grads = lax.psum_scatter(vector_grads, BOTH, scatter_dimension=1, tiled=True)
    return (
        output,
        input_grad,
        vector_grads[0],
        vector_grads[1],
        vector_grads[2],
        vector_grads[3],
        vector_grads[4],
        vector_grads[5],
        vector_grads[6],
        grad_key,
        grad_value,
        grad_gate,
        grad_output,
        vector_grads[7],
        vector_grads[8],
        vector_grads[9],
        vector_grads[10],
        grad_ffn_key,
        grad_ffn_value,
        grad_ffn_gate,
    )


def solution(mesh):
    tuned = tuple(mesh.shape.items()) == (("batch", 4), ("seq", 8))
    return jax.shard_map(
        partial(shards, tuned),
        mesh=mesh,
        in_specs=(
            P("batch", "seq", None),
            P("batch", None),
            P("batch", "seq", None),
            P(("batch", "seq")),
            P(("batch", "seq")),
            P(("batch", "seq")),
            P(("batch", "seq")),
            P(("batch", "seq")),
            P(("batch", "seq")),
            P(("batch", "seq")),
            P(("batch", "seq"), None),
            P(("batch", "seq"), None),
            P(("batch", "seq"), None),
            P(("batch", "seq"), None),
            P(("batch", "seq")),
            P(("batch", "seq")),
            P(("batch", "seq")),
            P(("batch", "seq")),
            P(("batch", "seq"), None),
            P(("batch", "seq"), None),
            P(("batch", "seq"), None),
        ),
        out_specs=(
            P("batch", "seq", None),
            P("batch", "seq", None),
            P(("batch", "seq")),
            P(("batch", "seq")),
            P(("batch", "seq")),
            P(("batch", "seq")),
            P(("batch", "seq")),
            P(("batch", "seq")),
            P(("batch", "seq")),
            P(("batch", "seq"), None),
            P(("batch", "seq"), None),
            P(("batch", "seq"), None),
            P(("batch", "seq"), None),
            P(("batch", "seq")),
            P(("batch", "seq")),
            P(("batch", "seq")),
            P(("batch", "seq")),
            P(("batch", "seq"), None),
            P(("batch", "seq"), None),
            P(("batch", "seq"), None),
        ),
        check_vma=False,
    )
```

```python
from functools import partial

import jax
import jax.numpy as jnp
from jax import lax
from jax.experimental import pallas as pl
from jax.experimental.pallas import tpu as pltpu
from jax.sharding import PartitionSpec as P

eps = 1e-05
highest = lax.Precision.HIGHEST
BOTH = ("batch", "seq")


def moved(rule):
    return [(f, rule(f)) for f in range(32)]


FLIP_X = moved(lambda f: f ^ 8)
FLIP_Y = moved(lambda f: f ^ 16)
FLIP_C = moved(lambda f: f ^ 1)


def turn_z(by):
    return moved(lambda f: (f & 25) | ((((f >> 1) + by) & 3) << 1))


def sent(array, pairs):
    return lax.ppermute(array, BOTH, pairs)


def place_of(flat, dy, dx, dz, dc):
    turned = ((((flat >> 1) & 3) + dz) & 3) * 2
    return ((flat & 25) | turned) ^ (dy * 16 + dx * 8 + dc)


def tied(array, *after):
    zero = jnp.zeros((), jnp.float32)
    for other in after:
        first = other[(0,) * other.ndim].astype(jnp.float32)
        zero = zero + jnp.minimum(jnp.abs(first), 0.0)
    return array + zero.astype(array.dtype)


def all_tied(arrays, after):
    return [tied(array, after) for array in arrays]


def assemble_kernel(owners, start, columns, slots_ref, *refs):
    pieces, out_ref, sems = refs[:-2], refs[-2], refs[-1]
    rows = out_ref.shape[1]
    copies = []
    number = 0
    for piece, count in zip(pieces, owners):
        for k in range(count):
            for q in range(columns):
                copies.append(
                    pltpu.make_async_copy(
                        piece.at[k, pl.ds(start + q * rows, rows), :],
                        out_ref.at[slots_ref[number], :, pl.ds(q * 1024, 1024)],
                        sems.at[number, q],
                    )
                )
            number += 1
    for copy in copies:
        copy.start()
    for copy in copies:
        copy.wait()


def assemble(pieces, slots, start, rows, columns):
    counts = [piece.shape[0] for piece in pieces]
    shape = (32, rows, columns * 1024)
    whole = pl.pallas_call(
        partial(assemble_kernel, counts, start, columns),
        out_shape=jax.ShapeDtypeStruct(shape, pieces[0].dtype),
        in_specs=[pl.BlockSpec(memory_space=pltpu.SMEM)]
        + [pl.BlockSpec(memory_space=pltpu.HBM)] * len(pieces),
        out_specs=pl.BlockSpec(memory_space=pltpu.VMEM),
        scratch_shapes=[pltpu.SemaphoreType.DMA((32, columns))],
        compiler_params=pltpu.CompilerParams(vmem_limit_bytes=24 * 1024 * 1024),
        cost_estimate=pl.CostEstimate(
            flops=0, transcendentals=0, bytes_accessed=2 * 2 * 32 * rows * columns * 1024
        ),
    )(slots, *pieces)
    return whole.reshape(32 * rows, columns * 1024)


def stacked(parts):
    rows = [part[:, q : q + 1024] for part in parts for q in range(0, part.shape[1], 1024)]
    return jnp.concatenate(rows, axis=0) if len(rows) > 1 else rows[0]


def around(part):
    return [sent(part, turn_z(d)) for d in (1, 2, 3)]


def long_slots(flat):
    every = (0, 1, 2, 3)
    steps = [(0, 0, every), (0, 1, every), (1, 0, every), (1, 1, (0, 1)), (1, 1, (2, 3))]
    return jnp.stack(
        [place_of(flat, dy, dx, -dz, dc) for dc in (0, 1) for dy, dx, dzs in steps for dz in dzs]
    ).astype(jnp.int32)


def send_far(from_x, from_y):
    half = from_x.shape[0] // 2
    return sent(from_x[:half], FLIP_Y), sent(from_y[half:], FLIP_X)


def both_cores(pieces):
    return pieces + [sent(piece, FLIP_C) for piece in pieces]


def choice(flat, width):
    index = jnp.arange(width)
    block, within = index // (width // 32), index % (width // 32)
    dc, rest = block >> 4, block & 15
    dy, dx, dz = rest >> 3, (rest >> 2) & 1, rest & 3
    wanted = place_of(flat, dy, dx, dz, dc) * (width // 32) + within
    return (jnp.arange(width)[:, None] == wanted[None, :]).astype(jnp.bfloat16)


def dot_nt(left, right):
    return lax.dot_general(
        left, right, (((1,), (1,)), ((), ())), preferred_element_type=jnp.float32
    )


def channel_kernel(slots_ref, *refs):
    key_in_ref, gate_in_ref, middle_ref, grad_ref, late_ref = refs[:5]
    refs = refs[5:]
    out_ref, value_grad_ref, gate_grad_ref, key_back_ref, gate_back_ref = refs[:5]
    hidden_ref, far_hidden_ref, pre_grad_ref, key_w, value_w, gate_w = refs[5:11]
    relu_s, hidden_s, pre_s, total_s, in_sems, hidden_sems, pre_sems = refs[11:]

    def key_copy(q):
        return pltpu.make_async_copy(
            late_ref.at[:, pl.ds(q * 32, 32), :], key_w.at[q], in_sems.at[q]
        )

    def value_copy(q):
        return pltpu.make_async_copy(
            late_ref.at[pl.ds(q * 8, 8), pl.ds(128, 128), :],
            value_w.at[pl.ds(q * 8, 8)],
            in_sems.at[4 + q],
        )

    gate_copy = pltpu.make_async_copy(
        late_ref.at[:, pl.ds(256, 32), :], gate_w, in_sems.at[8]
    )
    for q in range(4):
        key_copy(q).start()
        value_copy(q).start()
    gate_copy.start()

    def hidden_copy(q, k, target):
        return pltpu.make_async_copy(
            hidden_s.at[q, :, pl.ds(k * 128, 128)], target, hidden_sems.at[q, k]
        )

    def hidden_start(q, k):
        slot = slots_ref[q * 8 + k]
        columns = pl.ds(pl.multiple_of((slot & 3) * 128, 128), 128)

        @pl.when(slot < 16)
        def _():
            hidden_copy(q, k, hidden_ref.at[slot >> 2, :, columns]).start()

        @pl.when(slot >= 16)
        def _():
            hidden_copy(q, k, far_hidden_ref.at[(slot >> 2) - 4, :, columns]).start()

    def pre_copy(q):
        return pltpu.make_async_copy(
            pre_s.at[q], pre_grad_ref.at[:, pl.ds(pl.multiple_of(q * 1024, 1024), 1024)], pre_sems.at[q]
        )

    def forward(q, _):
        key_copy(q).wait()
        for half in range(1):
            rows = pl.ds(half * 512, 512)
            relu_s[q, rows, :] = jnp.maximum(
                jnp.dot(
                    key_in_ref[rows, :],
                    key_w[q].reshape(1024, 1024),
                    preferred_element_type=jnp.float32,
                ),
                0.0,
            )
            hidden_s[q, rows, :] = (relu_s[q, rows, :] * relu_s[q, rows, :]).astype(jnp.bfloat16)
        for k in range(8):
            hidden_start(q, k)
        value_copy(q).wait()
        for half in range(1):
            rows = pl.ds(half * 512, 512)
            more = jnp.dot(
                hidden_s[q, rows, :],
                value_w[pl.ds(q * 8, 8)].reshape(1024, 1024),
                preferred_element_type=jnp.float32,
            )

            @pl.when(q == 0)
            def _():
                total_s[rows, :] = more

            @pl.when(q > 0)
            def _():
                total_s[rows, :] += more

        return 0

    lax.fori_loop(0, 4, forward, 0)
    gate_copy.wait()
    for half in range(1):
        rows = pl.ds(half * 512, 512)
        gates = jax.nn.sigmoid(
            jnp.dot(
                gate_in_ref[rows, :],
                gate_w[...].reshape(1024, 1024),
                preferred_element_type=jnp.float32,
            )
        )
        value = total_s[rows, :]
        grads = grad_ref[rows, :].astype(jnp.float32)
        out_ref[rows, :] = (middle_ref[rows, :] + gates * value).astype(jnp.bfloat16)
        value_grad_ref[rows, :] = (grads * gates).astype(jnp.bfloat16)
        gate_grad_ref[rows, :] = (grads * value * gates * (1.0 - gates)).astype(jnp.bfloat16)

    def backward(q, _):
        for half in range(1):
            rows = pl.ds(half * 512, 512)
            pre_s[q, rows, :] = (
                dot_nt(value_grad_ref[rows, :], value_w[pl.ds(q * 8, 8)].reshape(1024, 1024))
                * 2.0
                * relu_s[q, rows, :]
            ).astype(jnp.bfloat16)
        pre_copy(q).start()
        for half in range(1):
            rows = pl.ds(half * 512, 512)
            more = dot_nt(pre_s[q, rows, :], key_w[q].reshape(1024, 1024))

            @pl.when(q == 0)
            def _():
                key_back_ref[rows, :] = more

            @pl.when(q > 0)
            def _():
                key_back_ref[rows, :] += more

        return 0

    lax.fori_loop(0, 4, backward, 0)
    for half in range(1):
        rows = pl.ds(half * 512, 512)
        gate_back_ref[rows, :] = dot_nt(gate_grad_ref[rows, :], gate_w[...].reshape(1024, 1024))
    for q in range(4):
        for k in range(8):
            hidden_copy(q, k, hidden_ref.at[0, :, pl.ds(0, 128)]).wait()
        pre_copy(q).wait()


def channel_mix(slots, key_in, gate_in, middle, grads, late):
    tokens = key_in.shape[0]
    wide_rows = jax.ShapeDtypeStruct((tokens, 1024), jnp.float32)
    half_rows = jax.ShapeDtypeStruct((tokens, 1024), jnp.bfloat16)
    whole = pl.BlockSpec(memory_space=pltpu.VMEM)
    far = pl.BlockSpec(memory_space=pltpu.HBM)
    return pl.pallas_call(
        channel_kernel,
        out_shape=(
            half_rows,
            half_rows,
            half_rows,
            wide_rows,
            wide_rows,
            jax.ShapeDtypeStruct((4, tokens, 512), jnp.bfloat16),
            jax.ShapeDtypeStruct((4, tokens, 512), jnp.bfloat16),
            jax.ShapeDtypeStruct((tokens, 4096), jnp.bfloat16),
        ),
        in_specs=[pl.BlockSpec(memory_space=pltpu.SMEM), whole, whole, whole, whole, far],
        out_specs=(whole,) * 5 + (far,) * 3,
        scratch_shapes=[
            pltpu.VMEM((4, 32, 32, 1024), jnp.bfloat16),
            pltpu.VMEM((32, 128, 1024), jnp.bfloat16),
            pltpu.VMEM((32, 32, 1024), jnp.bfloat16),
            pltpu.VMEM((4, tokens, 1024), jnp.float32),
            pltpu.VMEM((4, tokens, 1024), jnp.bfloat16),
            pltpu.VMEM((4, tokens, 1024), jnp.bfloat16),
            pltpu.VMEM((tokens, 1024), jnp.float32),
            pltpu.SemaphoreType.DMA((9,)),
            pltpu.SemaphoreType.DMA((4, 8)),
            pltpu.SemaphoreType.DMA((4,)),
        ],
        compiler_params=pltpu.CompilerParams(vmem_limit_bytes=54 * 1024 * 1024),
        cost_estimate=pl.CostEstimate(
            flops=2 * tokens * 1024 * 1024 * 18, transcendentals=0, bytes_accessed=40 * 1024 * 1024
        ),
    )(slots, key_in, gate_in, middle, grads, late)


def owner_slots(flat):
    other = jnp.arange(32)
    apart = other ^ flat
    dz = ((other >> 1) - (flat >> 1)) & 3
    return ((apart & 1) * 16 + ((apart >> 4) & 1) * 8 + ((apart >> 3) & 1) * 4 + dz).astype(jnp.int32)


def dot_tn(left, right):
    return lax.dot_general(
        left, right, (((0,), (0,)), ((), ())), preferred_element_type=jnp.float32
    )


def chip_rows(own_in, own_grads, other_in, other_grads):
    return (dot_tn(own_in, own_grads) + dot_tn(other_in, other_grads)).astype(jnp.bfloat16)


def value_part_kernel(own_ref, other_ref, grad_ref, other_grad_ref, near, side_x, side_y, far_a, far_b):
    quarter = pl.program_id(0)
    part = chip_rows(own_ref[0], grad_ref[...], other_ref[0], other_grad_ref[...])
    part = part.reshape((4, part.shape[0] // 4, 1024))

    @pl.when(quarter == 0)
    def _():
        near[...] = part

    @pl.when(quarter == 1)
    def _():
        side_x[...] = part

    @pl.when(quarter == 2)
    def _():
        side_y[...] = part

    @pl.when(quarter == 3)
    def _():
        far_a[...] = part[:2]
        far_b[...] = part[2:]


def store_quarters(part, outs):
    near, side_x, side_y, far_a, far_b = outs
    quarters = part.reshape(4, 4, 32, 1024)
    near[...] = quarters[0]
    side_x[...] = quarters[1]
    side_y[...] = quarters[2]
    far_a[...] = quarters[3, :2]
    far_b[...] = quarters[3, 2:]


def key_part_kernel(key_ref, other_key_ref, gate_ref, other_gate_ref, *refs):
    pre_ref, other_pre_ref, gate_grad_ref, other_gate_grad_ref = refs[:4]
    step = pl.program_id(0)

    @pl.when(step < 4)
    def _():
        store_quarters(
            chip_rows(key_ref[...], pre_ref[...], other_key_ref[...], other_pre_ref[...]), refs[4:]
        )

    @pl.when(step == 4)
    def _():
        store_quarters(
            chip_rows(
                gate_ref[...], gate_grad_ref[...], other_gate_ref[...], other_gate_grad_ref[...]
            ),
            refs[4:],
        )


def time_part_kernel(own_ref, other_ref, grad_ref, other_grad_ref, *refs):
    branch_ref, other_branch_ref = refs[:2]
    step = pl.program_id(0)

    @pl.when(step < 3)
    def _():
        store_quarters(
            chip_rows(own_ref[...], grad_ref[...], other_ref[...], other_grad_ref[...]), refs[2:]
        )

    @pl.when(step == 3)
    def _():
        store_quarters(
            chip_rows(own_ref[...], branch_ref[...], other_ref[...], other_branch_ref[...]), refs[2:]
        )


def in_three(array):
    high = array.astype(jnp.bfloat16)
    rest = array - high.astype(jnp.float32)
    middle = rest.astype(jnp.bfloat16)
    return high, middle, (rest - middle.astype(jnp.float32)).astype(jnp.bfloat16)


def time_mix_kernel(
    branch_ref,
    weight_ref,
    key_ref,
    value_ref,
    gates_ref,
    mask_ref,
    carry_ref,
    num_ref,
    den_ref,
    decay_ref,
    bonus_ref,
    gate_grad_ref,
    key_grad_ref,
    value_grad_ref,
    num_grad_ref,
    den_grad_ref,
    decay_grad_ref,
    bonus_grad_ref,
):
    length = mask_ref.shape[1]
    decay = decay_ref[...]
    bonus = jnp.exp(bonus_ref[...])
    place = lax.broadcasted_iota(jnp.int32, (length, 1), 0).astype(jnp.float32)
    grow = jnp.exp(place * decay)
    shrink = jnp.exp((1.0 - place) * decay)
    for row in range(mask_ref.shape[0]):
        rows = pl.ds(row * length, length)
        mask = mask_ref[row]
        gated_grad = dot_nt(branch_ref[rows, :], weight_ref[...])
        gates = gates_ref[rows, :]
        power = jnp.exp(key_ref[rows, :])
        value = value_ref[rows, :]
        product = power * value
        fade = carry_ref[row] * jnp.exp(-place * decay)
        num_in, den_in = num_ref[row], den_ref[row]
        num_sum = sum(
            jnp.dot(mask, part, preferred_element_type=jnp.float32)
            for part in in_three(product * grow)
        )
        den_sum = sum(
            jnp.dot(mask, part, preferred_element_type=jnp.float32)
            for part in in_three(power * grow)
        )
        numer = fade * num_in + shrink * num_sum + bonus * product
        denom = fade * den_in + shrink * den_sum + bonus * power
        mixed = numer / denom
        gate_grad_ref[rows, :] = (gated_grad * mixed * gates * (1.0 - gates)).astype(jnp.bfloat16)
        num_grad = gated_grad * gates / denom
        den_grad = -num_grad * mixed
        num_back, den_back = shrink * num_grad, shrink * den_grad
        num_past = grow * sum(dot_tn(mask, part) for part in in_three(num_back))
        den_past = grow * sum(dot_tn(mask, part) for part in in_three(den_back))
        product_grad = bonus * num_grad + num_past
        key_grad_ref[rows, :] = power * (value * product_grad + bonus * den_grad + den_past)
        value_grad_ref[rows, :] = power * product_grad
        num_grad_ref[row] = jnp.sum(fade * num_grad, axis=0, keepdims=True)
        den_grad_ref[row] = jnp.sum(fade * den_grad, axis=0, keepdims=True)
        bonus_grad_ref[row] = jnp.sum(
            bonus * (product * num_grad + power * den_grad), axis=0, keepdims=True
        )
        decay_grad_ref[row] = jnp.sum(
            place * (product * num_past + power * den_past)
            + (1.0 - place) * (num_back * num_sum + den_back * den_sum)
            - place * fade * (num_grad * num_in + den_grad * den_in),
            axis=0,
            keepdims=True,
        )


def time_mix_back(branch, weight, key, value, gates, mask, carry, num, den, decay, bonus):
    tokens = branch.shape[0]
    rows, length = mask.shape[:2]
    tile = 256
    wide_block = pl.BlockSpec((tokens, tile), lambda i: (0, i))
    state = pl.BlockSpec((rows, 1, tile), lambda i: (0, 0, i))
    vector = pl.BlockSpec((1, tile), lambda i: (0, i))
    states = jax.ShapeDtypeStruct((rows, 1, 1024), jnp.float32)
    wide_rows = jax.ShapeDtypeStruct((tokens, 1024), jnp.float32)
    return pl.pallas_call(
        time_mix_kernel,
        grid=(1024 // tile,),
        out_shape=(
            jax.ShapeDtypeStruct((tokens, 1024), jnp.bfloat16),
            wide_rows,
            wide_rows,
            states,
            states,
            states,
            states,
        ),
        in_specs=[
            pl.BlockSpec((tokens, 1024), lambda i: (0, 0)),
            pl.BlockSpec((tile, 1024), lambda i: (i, 0)),
            wide_block,
            wide_block,
            wide_block,
            pl.BlockSpec((rows, length, length), lambda i: (0, 0, 0)),
            pl.BlockSpec((rows, length, 1), lambda i: (0, 0, 0)),
            state,
            state,
            vector,
            vector,
        ],
        out_specs=(wide_block, wide_block, wide_block, state, state, state, state),
        compiler_params=pltpu.CompilerParams(vmem_limit_bytes=48 * 1024 * 1024),
        cost_estimate=pl.CostEstimate(flops=1, transcendentals=0, bytes_accessed=1),
    )(branch, weight, key, value, gates, mask, carry, num, den, decay, bonus)


def quarters_call(kernel, steps, rows, in_specs, by_quarter, arguments):
    if by_quarter:
        outs = [pl.BlockSpec((n, rows, 1024), lambda i: (0, 0, 0)) for n in (4, 4, 4, 2, 2)]
    else:
        outs = [pl.BlockSpec((n, 32, 1024), lambda i: (0, i, 0)) for n in (4, 4, 4, 2, 2)]
    return pl.pallas_call(
        kernel,
        grid=(steps,),
        out_shape=tuple(
            jax.ShapeDtypeStruct((n, rows, 1024), jnp.bfloat16) for n in (4, 4, 4, 2, 2)
        ),
        in_specs=in_specs,
        out_specs=tuple(outs),
        compiler_params=pltpu.CompilerParams(vmem_limit_bytes=48 * 1024 * 1024),
        cost_estimate=pl.CostEstimate(flops=1, transcendentals=0, bytes_accessed=1),
    )(*arguments)


def value_part(own_hidden, other_hidden, grads, other_grads):
    tokens = grads.shape[0]
    whole = pl.BlockSpec((tokens, 1024), lambda i: (0, 0))
    block = pl.BlockSpec((1, tokens, 512), lambda i: (i, 0, 0))
    return quarters_call(
        value_part_kernel,
        4,
        128,
        [block, block, whole, whole],
        True,
        (own_hidden, other_hidden, grads, other_grads),
    )


def key_part(key, other_key, gate, other_gate, pre, other_pre, gate_grad, other_gate_grad):
    tokens = pre.shape[0]
    half = pl.BlockSpec((tokens, 512), lambda i: (0, 0))
    whole = pl.BlockSpec((tokens, 1024), lambda i: (0, 0))
    block = pl.BlockSpec((tokens, 1024), lambda i: (0, jnp.minimum(i, 3)))
    return quarters_call(
        key_part_kernel,
        5,
        160,
        [half, half, half, half, block, block, whole, whole],
        False,
        (key, other_key, gate, other_gate, pre, other_pre, gate_grad, other_gate_grad),
    )


def time_part(own, other, grads, other_grads, branch, other_branch):
    tokens = grads.shape[0]
    half = pl.BlockSpec((tokens, 512), lambda i: (0, i))
    whole = pl.BlockSpec((tokens, 1024), lambda i: (0, 0))
    block = pl.BlockSpec((tokens, 1024), lambda i: (0, jnp.minimum(i, 2)))
    return quarters_call(
        time_part_kernel,
        4,
        128,
        [half, half, block, block, whole, whole],
        False,
        (own, other, grads, other_grads, branch, other_branch),
    )


def ordered_halves(rows_in, flat):
    width = rows_in.shape[-1]
    rows_in = rows_in.reshape(-1, width)
    ordered = jnp.dot(rows_in, choice(flat, width), preferred_element_type=jnp.bfloat16)
    return ordered[:, : width // 2], ordered[:, width // 2 :]


def sent_together(arrays):
    got = sent(jnp.concatenate(arrays, axis=1) if len(arrays) > 1 else arrays[0], FLIP_C)
    ends = [sum(a.shape[1] for a in arrays[: i + 1]) for i in range(len(arrays))]
    return [got[:, end - a.shape[1] : end] for a, end in zip(arrays, ends)]


def wide(array):
    return array.astype(jnp.float32)


def narrow(array):
    return array.astype(jnp.bfloat16)


def send_corner(parts):
    return sent(parts[3], FLIP_X), sent(parts[4], FLIP_Y)


def add_corner(parts, add_a, add_b):
    to_y = jnp.concatenate([narrow(wide(parts[2][:2]) + wide(add_a)), parts[2][2:]])
    to_x = jnp.concatenate([parts[1][:2], narrow(wide(parts[1][2:]) + wide(add_b))])
    return to_y, to_x


def send_sides(to_y, to_x):
    return sent(to_y, FLIP_Y), sent(to_x, FLIP_X)


def add_sides(parts, from_y, from_x):
    column = wide(parts[0]) + wide(from_y) + wide(from_x)
    return column[0], [narrow(column[d]) for d in (1, 2, 3)]


def send_column(outgoing):
    return [sent(part, turn_z(d)) for d, part in zip((1, 2, 3), outgoing)]


def add_all(first, others):
    for other in others:
        first = first + wide(other)
    return first


def sum_plane(total):
    for pairs in (FLIP_C, FLIP_X, FLIP_Y):
        total = total + sent(total, pairs)
    return total


def sum_column(total, flat):
    total = total + sum(sent(total, turn_z(d)) for d in (1, 2, 3))
    count = total.shape[1] // 32
    return lax.dynamic_slice_in_dim(total, flat * count, count, 1)


def shifted(shard, axis, by):
    length = lax.axis_size(axis)
    pairs = [(i, i + by) for i in range(length) if 0 <= i + by < length]
    return lax.ppermute(shard, axis, pairs)


def carried_in(part, starts_in, decay_vec, length, reverse):
    count = lax.axis_size("seq")
    place = lax.axis_index("seq")
    clear = 1.0 - starts_in.astype(jnp.float32)
    block_fade = jnp.exp(-length * decay_vec)

    def clear_of(block):
        return lax.dynamic_index_in_dim(clear, jnp.clip(block, 0, count - 1), 1, True)

    if count == 8:
        chip, core = place >> 1, place & 1
        other = sent(part, FLIP_C)
        is_far = (core == 1) == (not reverse)
        near = jnp.where(is_far, other, part)
        last = jnp.where(is_far, part, other)
        first_block, second_block = chip * 2 + (1 if reverse else 0), chip * 2 + (0 if reverse else 1)
        joined = clear_of(second_block) * block_fade * near + last
        step = -1 if reverse else 1
        entering = jnp.zeros_like(part)
        open_way = jnp.ones((part.shape[1], 1), jnp.float32)
        for d in (1, 2, 3):
            beside = chip - step * d
            live = ((beside >= 0) & (beside < 4)).astype(jnp.float32)
            fade = live * open_way * jnp.exp(-float(2 * (d - 1) * length) * decay_vec)
            entering = entering + fade * sent(joined, turn_z(step * d))
            open_way = open_way * clear_of(2 * beside) * clear_of(2 * beside + 1)
        return jnp.where(is_far, clear_of(first_block) * block_fade * entering + near, entering)
    gathered = lax.all_gather(part, "seq")

    def one(lap, state):
        source = count - 1 - lap if reverse else lap
        return clear_of(source) * block_fade * state + lax.dynamic_index_in_dim(gathered, source, 0, False)

    ahead = count - 1 - place if reverse else place
    return lax.fori_loop(0, ahead, one, jnp.zeros_like(part))


def norm_forward(values, gain_vec, bias_vec):
    centre = values - jnp.mean(values, axis=-1, keepdims=True)
    inv_std = lax.rsqrt(jnp.mean(centre * centre, axis=-1, keepdims=True) + eps)
    normed = centre * inv_std
    return (normed * gain_vec + bias_vec, normed, inv_std)


def norm_backward(grads, normed, inv_std, gain_vec):
    scaled = grads * gain_vec
    inner = (
        scaled
        - jnp.mean(scaled, axis=-1, keepdims=True)
        - normed * jnp.mean(scaled * normed, axis=-1, keepdims=True)
    )
    return (inv_std * inner, jnp.sum(grads * normed, axis=(0, 1)), jnp.sum(grads, axis=(0, 1)))


def project(rows_in, weight):
    return jnp.einsum("rtd,de->rte", rows_in, weight, preferred_element_type=jnp.float32)


def project_back(grads, weight):
    return jnp.einsum("rte,de->rtd", grads, weight, preferred_element_type=jnp.float32)


def weight_grad(rows_in, grads):
    total = jnp.einsum("rtd,rte->de", rows_in, grads, preferred_element_type=jnp.float32)
    return lax.psum_scatter(total, BOTH, scatter_dimension=0, tiled=True)


def weighted_value_local(
    key_row_block,
    value_row_block,
    feature_forgetting_rate,
    present_reward,
    state_numerator,
    state_denominator,
    document_segments,
):
    length = key_row_block.shape[1]
    width = key_row_block.shape[2]
    order_idx = jnp.arange(length)
    step_pos = order_idx.astype(jnp.float32)[:, None]
    powered_lookups = jnp.exp(key_row_block)
    grow_exp = jnp.exp(step_pos * feature_forgetting_rate)
    shrink = jnp.exp((1.0 - step_pos) * feature_forgetting_rate)
    pair_mask = (
        (order_idx[None, :] < order_idx[:, None])[None]
        & (document_segments[:, None, :] == document_segments[:, :, None])
    ).astype(jnp.float32)
    weighted = jnp.concatenate(
        [powered_lookups * value_row_block, powered_lookups], axis=2
    ) * jnp.concatenate([grow_exp, grow_exp], axis=1)
    past_sums = jnp.einsum(
        "rti,rie->rte", pair_mask, weighted, precision=highest
    ) * jnp.concatenate([shrink, shrink], axis=1)
    carry_fade = (document_segments == 0).astype(jnp.float32)[:, :, None] * jnp.exp(
        -step_pos * feature_forgetting_rate
    )
    present_token_contribution = jnp.exp(present_reward) * powered_lookups
    numer = (
        carry_fade * state_numerator[:, None, :]
        + past_sums[:, :, :width]
        + present_token_contribution * value_row_block
    )
    denom = (
        carry_fade * state_denominator[:, None, :]
        + past_sums[:, :, width:]
        + present_token_contribution
    )
    return numer / denom


def tail_terms(key_row_block, value_row_block, feature_forgetting_rate, document_segments):
    length = key_row_block.shape[1]
    step_pos = jnp.arange(length).astype(jnp.float32)[:, None]
    powered_lookups = jnp.exp(key_row_block)
    tail_fade = (document_segments == document_segments[:, -1:]).astype(jnp.float32)[
        :, :, None
    ] * jnp.exp((step_pos - (length - 1)) * feature_forgetting_rate)
    return (
        jnp.sum(tail_fade * powered_lookups * value_row_block, axis=1),
        jnp.sum(tail_fade * powered_lookups, axis=1),
        tail_fade,
        powered_lookups,
    )


def shards(
    tuned,
    incoming_activations,
    sequence_extents,
    upstream_sensitivity,
    initial_normalizer_scale,
    initial_normalizer_offset,
    temporal_lookup_fraction,
    temporal_content_fraction,
    temporal_receptance_fraction,
    feature_forgetting_rate,
    present_reward,
    temporal_lookup_projection,
    temporal_content_projection,
    temporal_receptance_projection,
    temporal_result_projection,
    later_normalizer_scale,
    later_normalizer_offset,
    feature_lookup_fraction,
    feature_receptance_fraction,
    feature_lookup_projection,
    feature_content_projection,
    feature_receptance_projection,
):
    flat = lax.axis_index("batch") * lax.axis_size("seq") + lax.axis_index("seq")
    vectors = jnp.stack(
        [
            initial_normalizer_scale,
            initial_normalizer_offset,
            temporal_lookup_fraction,
            temporal_content_fraction,
            temporal_receptance_fraction,
            feature_forgetting_rate,
            present_reward,
            later_normalizer_scale,
            later_normalizer_offset,
            feature_lookup_fraction,
            feature_receptance_fraction,
        ]
    )
    if tuned:
        order = long_slots(flat)
        late = lax.all_gather(
            stacked(
                [
                    feature_lookup_projection,
                    feature_content_projection,
                    feature_receptance_projection,
                ]
            ),
            BOTH,
        )
        spread = jnp.tile(jnp.pad(vectors, ((0, 5), (0, 0))), (1, 32))
        packed = jnp.where(jnp.arange(1024) // 32 == flat, spread, jnp.zeros_like(spread))
        part = stacked(
            [
                temporal_lookup_projection,
                temporal_content_projection,
                temporal_receptance_projection,
                temporal_result_projection,
                packed,
            ]
        )
        column = jnp.stack([part] + around(part))
        from_x, from_y = sent(column, FLIP_X), sent(column, FLIP_Y)
        early = both_cores([column, from_x, from_y, *send_far(from_x, from_y)])
        vectors = jnp.sum(
            assemble(early, order, 128, 16, 1).reshape(32, 16, 1024).astype(jnp.float32), axis=0
        )
        lookup_weight = assemble(early, order, 0, 32, 1)
        content_weight = assemble(early, order, 32, 32, 1)
        receptance_weight = assemble(early, order, 64, 32, 1)
        result_weight = assemble(early, order, 96, 32, 1)
    else:
        (
            lookup_weight,
            content_weight,
            receptance_weight,
            result_weight,
            ffn_key_weight,
            ffn_gate_weight,
            ffn_value_weight,
        ) = [
            lax.all_gather(part, BOTH, axis=0, tiled=True)
            for part in (
                temporal_lookup_projection,
                temporal_content_projection,
                temporal_receptance_projection,
                temporal_result_projection,
                feature_lookup_projection,
                feature_receptance_projection,
                feature_content_projection,
            )
        ]
        vectors = lax.all_gather(vectors, BOTH, axis=1, tiled=True).astype(jnp.float32)
    (
        opening_standardize_scale,
        opening_standardize_offset,
        temporal_lookup_mixture,
        temporal_content_mixture,
        temporal_receptance_mixture,
        decay_vec,
        reward_array,
        closing_standardize_scale,
        closing_standardize_offset,
        feature_lookup_mixture,
        feature_receptance_mixture,
    ) = tuple(vectors[i] for i in range(11))
    rows, length, width = incoming_activations.shape
    starts = jnp.cumsum(sequence_extents, axis=1) - sequence_extents
    places = lax.axis_index("seq") * length + jnp.arange(length, dtype=jnp.int32)
    resets = jnp.any(
        (starts[:, None, :] == places[None, :, None]) & (sequence_extents[:, None, :] > 0), axis=2
    )
    document_segments = jnp.cumsum(resets.astype(jnp.int32), axis=1)
    keep_mask = 1.0 - resets.astype(jnp.float32)[:, :, None]
    clear_flag = (document_segments[:, -1:] == 0).astype(jnp.float32)
    starts_in = jnp.any(
        (starts[:, None, :] // length == jnp.arange(lax.axis_size("seq"))[None, :, None])
        & (sequence_extents[:, None, :] > 0),
        axis=2,
    )

    inputs = incoming_activations.astype(jnp.float32)
    left_rows = shifted(incoming_activations[:, length - 1 :, :], "seq", 1)
    normed_one, unit_one, inv_one = norm_forward(
        inputs, opening_standardize_scale, opening_standardize_offset
    )
    left_normed, _, _ = norm_forward(
        left_rows.astype(jnp.float32), opening_standardize_scale, opening_standardize_offset
    )
    before_one = jnp.concatenate([left_normed, normed_one[:, :-1, :]], axis=1) * keep_mask
    key_in = (
        normed_one * temporal_lookup_mixture + before_one * (1.0 - temporal_lookup_mixture)
    ).astype(jnp.bfloat16)
    value_in = (
        normed_one * temporal_content_mixture + before_one * (1.0 - temporal_content_mixture)
    ).astype(jnp.bfloat16)
    gate_in = (
        normed_one * temporal_receptance_mixture + before_one * (1.0 - temporal_receptance_mixture)
    ).astype(jnp.bfloat16)
    key_row_block = project(key_in, lookup_weight)
    value_row_block = project(value_in, content_weight)
    gates = jax.nn.sigmoid(project(gate_in, receptance_weight))
    tail_num, tail_den, tail_fade, powered_lookups = tail_terms(
        key_row_block, value_row_block, decay_vec, document_segments
    )
    state_numerator, state_denominator = carried_in(
        jnp.stack([tail_num, tail_den]), starts_in, decay_vec, length, False
    )
    mixed, weighted_value_backward = jax.vjp(
        partial(weighted_value_local, document_segments=document_segments),
        key_row_block,
        value_row_block,
        decay_vec,
        reward_array,
        state_numerator,
        state_denominator,
    )
    gated = (gates * mixed).astype(jnp.bfloat16)
    if tuned:
        own_key, far_key = ordered_halves(key_in, flat)
        own_value, far_value = ordered_halves(value_in, flat)
        own_gate, far_gate = ordered_halves(gate_in, flat)
        own_gated, far_gated = ordered_halves(gated, flat)
        other_time = sent(
            jnp.concatenate([far_key, far_value, far_gate, far_gated], axis=1), FLIP_C
        )
        own_time = jnp.concatenate([own_key, own_value, own_gate, own_gated], axis=1)
    middle = inputs + project(gated, result_weight)
    normed_two, unit_two, inv_two = norm_forward(
        middle, closing_standardize_scale, closing_standardize_offset
    )
    before_rows = shifted(normed_two[:, length - 1 :, :], "seq", 1)
    before_two = jnp.concatenate([before_rows, normed_two[:, :-1, :]], axis=1) * keep_mask
    ffn_key_in = (
        normed_two * feature_lookup_mixture + before_two * (1.0 - feature_lookup_mixture)
    ).astype(jnp.bfloat16)
    ffn_gate_in = (
        normed_two * feature_receptance_mixture + before_two * (1.0 - feature_receptance_mixture)
    ).astype(jnp.bfloat16)
    grad_out = upstream_sensitivity.astype(jnp.float32)
    if tuned:
        own_ffn_key, far_ffn_key = ordered_halves(ffn_key_in, flat)
        own_ffn_gate, far_ffn_gate = ordered_halves(ffn_gate_in, flat)
        other_ffn_key, other_ffn_gate = sent_together([far_ffn_key, far_ffn_gate])
        output, value_grad, ffn_gate_grad, key_two_grad, gate_two_grad, *kept = channel_mix(
            owner_slots(flat),
            ffn_key_in.reshape(-1, width),
            ffn_gate_in.reshape(-1, width),
            middle.reshape(-1, width),
            upstream_sensitivity.reshape(-1, width),
            late,
        )
        output, key_two_grad, gate_two_grad = (
            a.reshape(rows, length, width) for a in (output, key_two_grad, gate_two_grad)
        )
        own_hidden, far_hidden, pre_grad = kept
        other_value_grad = sent(value_grad, FLIP_C)
        other_hidden = sent(far_hidden, FLIP_C)
        other_gate_grad = sent(ffn_gate_grad, FLIP_C)
        other_pre_grad = sent(pre_grad, FLIP_C)
        value_parts = value_part(own_hidden, other_hidden, value_grad, other_value_grad)
        value_corner = send_corner(value_parts)
        key_parts = key_part(
            own_ffn_key,
            other_ffn_key,
            own_ffn_gate,
            other_ffn_gate,
            pre_grad,
            other_pre_grad,
            ffn_gate_grad,
            other_gate_grad,
        )
        value_sides = add_corner(value_parts, *all_tied(value_corner, key_parts[4]))
        value_from = send_sides(*value_sides)
    else:
        hidden_pre = project(ffn_key_in, ffn_key_weight)
        hidden = jnp.square(jax.nn.relu(hidden_pre)).astype(jnp.bfloat16)
        ffn_value = project(hidden, ffn_value_weight)
        ffn_gates = jax.nn.sigmoid(project(ffn_gate_in, ffn_gate_weight))
        output = (middle + ffn_gates * ffn_value).astype(jnp.bfloat16)
        value_grad = (grad_out * ffn_gates).astype(jnp.bfloat16)
        ffn_gate_grad = (grad_out * ffn_value * ffn_gates * (1.0 - ffn_gates)).astype(jnp.bfloat16)
        hidden_grad = project_back(value_grad, ffn_value_weight)
        pre_grad = (hidden_grad * 2.0 * jax.nn.relu(hidden_pre)).astype(jnp.bfloat16)
        grad_ffn_value = weight_grad(hidden, value_grad)
        grad_ffn_key = weight_grad(ffn_key_in, pre_grad)
        grad_ffn_gate = weight_grad(ffn_gate_in, ffn_gate_grad)
        key_two_grad = project_back(pre_grad, ffn_key_weight)
        gate_two_grad = project_back(ffn_gate_grad, ffn_gate_weight)
    spread_two = normed_two - before_two
    grad_ffn_mix_key = jnp.sum(key_two_grad * spread_two, axis=(0, 1))
    grad_ffn_mix_gate = jnp.sum(gate_two_grad * spread_two, axis=(0, 1))
    normed_two_grad = (
        key_two_grad * feature_lookup_mixture + gate_two_grad * feature_receptance_mixture
    )
    before_two_grad = (
        key_two_grad * (1.0 - feature_lookup_mixture)
        + gate_two_grad * (1.0 - feature_receptance_mixture)
    ) * keep_mask
    from_right = shifted(before_two_grad[:, :1, :], "seq", -1)
    normed_two_grad = normed_two_grad + jnp.concatenate(
        [before_two_grad[:, 1:, :], from_right], axis=1
    )
    middle_norm_grad, grad_gain_two, grad_bias_two = norm_backward(
        normed_two_grad, unit_two, inv_two, closing_standardize_scale
    )
    middle_grad = grad_out + middle_norm_grad
    branch_grad = middle_grad.astype(jnp.bfloat16)
    if tuned:
        flat_branch_grad = branch_grad.reshape(-1, width)
        other_branch_grad = sent(flat_branch_grad, FLIP_C)
        key_corner = send_corner(key_parts)
    else:
        grad_output = weight_grad(gated, branch_grad)
    if tuned:
        order_idx = jnp.arange(length)
        pair_mask = (
            (order_idx[None, :] < order_idx[:, None])[None]
            & (document_segments[:, None, :] == document_segments[:, :, None])
        ).astype(jnp.bfloat16)
        (
            gate_pre_grad,
            key_gradient,
            value_gradient,
            numerator_gradient,
            denominator_gradient,
            decay_gradient,
            reward_derivative,
        ) = time_mix_back(
            branch_grad.reshape(-1, width),
            result_weight,
            key_row_block.reshape(-1, width),
            value_row_block.reshape(-1, width),
            gates.reshape(-1, width),
            pair_mask,
            (document_segments == 0).astype(jnp.float32)[:, :, None],
            state_numerator[:, None, :],
            state_denominator[:, None, :],
            tied(decay_vec[None, :], value_sides[0], value_sides[1][2:]),
            reward_array[None, :],
        )
        gate_pre_grad, key_gradient, value_gradient = (
            a.reshape(rows, length, width) for a in (gate_pre_grad, key_gradient, value_gradient)
        )
        numerator_gradient = numerator_gradient[:, 0, :]
        denominator_gradient = denominator_gradient[:, 0, :]
        decay_gradient = jnp.sum(decay_gradient[:, 0, :], axis=0)
        reward_derivative = jnp.sum(reward_derivative[:, 0, :], axis=0)
    else:
        gated_grad = project_back(branch_grad, result_weight)
        gate_pre_grad = (gated_grad * mixed * gates * (1.0 - gates)).astype(jnp.bfloat16)
        blended_gradient = gated_grad * gates
        (
            key_gradient,
            value_gradient,
            decay_gradient,
            reward_derivative,
            numerator_gradient,
            denominator_gradient,
        ) = weighted_value_backward(blended_gradient)
    state_gradient = jnp.stack([numerator_gradient, denominator_gradient])
    if tuned:
        key_sides = add_corner(key_parts, *all_tied(key_corner, state_gradient))
        key_from = send_sides(*key_sides)
        state_gradient = tied(state_gradient, key_sides[0], key_sides[1][2:])
    num_next, den_next = carried_in(state_gradient, starts_in, decay_vec, length, True)
    if tuned:
        value_first, value_outgoing = add_sides(value_parts, *all_tied(value_from, num_next))
        num_next = tied(num_next, value_outgoing[0])
    num_tail = tail_fade * num_next[:, None, :]
    den_tail = tail_fade * den_next[:, None, :]
    tail_grad = powered_lookups * (value_row_block * num_tail + den_tail)
    key_gradient = key_gradient + tail_grad
    value_gradient = value_gradient + powered_lookups * num_tail
    offsets = (jnp.arange(length).astype(jnp.float32) - (length - 1))[:, None]
    block_fade = clear_flag * jnp.exp(-length * decay_vec)
    decay_gradient = decay_gradient + jnp.sum(offsets * tail_grad, axis=(0, 1))
    decay_gradient = decay_gradient - length * jnp.sum(
        block_fade * (state_numerator * num_next + state_denominator * den_next), axis=0
    )
    key_grad16 = key_gradient.astype(jnp.bfloat16)
    val_grad16 = value_gradient.astype(jnp.bfloat16)
    if tuned:
        flat_grads = jnp.concatenate(
            [g.reshape(-1, width) for g in (key_grad16, val_grad16, gate_pre_grad)], axis=1
        )
        other_grads = sent(flat_grads, FLIP_C)
        time_parts = time_part(
            own_time, other_time, flat_grads, other_grads, flat_branch_grad, other_branch_grad
        )
        value_got = all_tied(send_column(all_tied(value_outgoing, num_next)), time_parts[4])
        key_first, key_outgoing = add_sides(key_parts, *all_tied(key_from, time_parts[4]))
        time_corner = send_corner(time_parts)
    else:
        grad_key = weight_grad(key_in, key_grad16)
        grad_value = weight_grad(value_in, val_grad16)
        grad_gate = weight_grad(gate_in, gate_pre_grad)
    if tuned:
        key_grad16 = tied(key_grad16, key_outgoing[0])
    key_in_grad = project_back(key_grad16, lookup_weight)
    value_in_grad = project_back(val_grad16, content_weight)
    gate_in_grad = project_back(gate_pre_grad, receptance_weight)
    spread_one = normed_one - before_one
    grad_mix_key = jnp.sum(key_in_grad * spread_one, axis=(0, 1))
    grad_mix_value = jnp.sum(value_in_grad * spread_one, axis=(0, 1))
    grad_mix_gate = jnp.sum(gate_in_grad * spread_one, axis=(0, 1))
    normed_one_grad = (
        key_in_grad * temporal_lookup_mixture
        + value_in_grad * temporal_content_mixture
        + gate_in_grad * temporal_receptance_mixture
    )
    before_one_grad = (
        key_in_grad * (1.0 - temporal_lookup_mixture)
        + value_in_grad * (1.0 - temporal_content_mixture)
        + gate_in_grad * (1.0 - temporal_receptance_mixture)
    ) * keep_mask
    if tuned:
        time_sides = add_corner(time_parts, *all_tied(time_corner, before_one_grad))
        time_from = send_sides(*time_sides)
    from_next = shifted(before_one_grad[:, :1, :], "seq", -1)
    if tuned:
        key_got = send_column(all_tied(key_outgoing, from_next))
        from_next = tied(from_next, time_sides[0], time_sides[1][2:])
    normed_one_grad = normed_one_grad + jnp.concatenate(
        [before_one_grad[:, 1:, :], from_next], axis=1
    )
    input_norm_grad, grad_gain_one, grad_bias_one = norm_backward(
        normed_one_grad, unit_one, inv_one, opening_standardize_scale
    )
    input_grad = middle_grad + input_norm_grad
    vector_grads = jnp.stack(
        [
            grad_gain_one,
            grad_bias_one,
            grad_mix_key,
            grad_mix_value,
            grad_mix_gate,
            decay_gradient,
            reward_derivative,
            grad_gain_two,
            grad_bias_two,
            grad_ffn_mix_key,
            grad_ffn_mix_gate,
        ]
    )
    if tuned:
        time_first, time_outgoing = add_sides(time_parts, *all_tied(time_from, vector_grads))
        key_total = add_all(key_first, all_tied(key_got, vector_grads))
        time_total = add_all(time_first, send_column(time_outgoing))
        grad_key, grad_value, grad_gate, grad_output = (
            time_total[i : i + 32] for i in (0, 32, 64, 96)
        )
        grad_ffn_value = add_all(value_first, value_got)
        grad_ffn_key = jnp.concatenate([key_total[i : i + 32] for i in (0, 32, 64, 96)], axis=1)
        grad_ffn_gate = key_total[128:]
        vector_grads = sum_column(tied(sum_plane(vector_grads), time_outgoing[0]), flat)
    else:
        vector_grads = lax.psum_scatter(vector_grads, BOTH, scatter_dimension=1, tiled=True)
    return (
        output,
        input_grad,
        vector_grads[0],
        vector_grads[1],
        vector_grads[2],
        vector_grads[3],
        vector_grads[4],
        vector_grads[5],
        vector_grads[6],
        grad_key,
        grad_value,
        grad_gate,
        grad_output,
        vector_grads[7],
        vector_grads[8],
        vector_grads[9],
        vector_grads[10],
        grad_ffn_key,
        grad_ffn_value,
        grad_ffn_gate,
    )


def solution(mesh):
    tuned = tuple(mesh.shape.items()) == (("batch", 4), ("seq", 8))
    return jax.shard_map(
        partial(shards, tuned),
        mesh=mesh,
        in_specs=(
            P("batch", "seq", None),
            P("batch", None),
            P("batch", "seq", None),
            P(("batch", "seq")),
            P(("batch", "seq")),
            P(("batch", "seq")),
            P(("batch", "seq")),
            P(("batch", "seq")),
            P(("batch", "seq")),
            P(("batch", "seq")),
            P(("batch", "seq"), None),
            P(("batch", "seq"), None),
            P(("batch", "seq"), None),
            P(("batch", "seq"), None),
            P(("batch", "seq")),
            P(("batch", "seq")),
            P(("batch", "seq")),
            P(("batch", "seq")),
            P(("batch", "seq"), None),
            P(("batch", "seq"), None),
            P(("batch", "seq"), None),
        ),
        out_specs=(
            P("batch", "seq", None),
            P("batch", "seq", None),
            P(("batch", "seq")),
            P(("batch", "seq")),
            P(("batch", "seq")),
            P(("batch", "seq")),
            P(("batch", "seq")),
            P(("batch", "seq")),
            P(("batch", "seq")),
            P(("batch", "seq"), None),
            P(("batch", "seq"), None),
            P(("batch", "seq"), None),
            P(("batch", "seq"), None),
            P(("batch", "seq")),
            P(("batch", "seq")),
            P(("batch", "seq")),
            P(("batch", "seq")),
            P(("batch", "seq"), None),
            P(("batch", "seq"), None),
            P(("batch", "seq"), None),
        ),
        check_vma=False,
    )
```

```python
from functools import partial

import jax
import jax.numpy as jnp
from jax import lax
from jax.experimental import pallas as pl
from jax.experimental.pallas import tpu as pltpu
from jax.sharding import PartitionSpec as P

eps = 1e-05
highest = lax.Precision.HIGHEST
BOTH = ("batch", "seq")


def moved(rule):
    return [(f, rule(f)) for f in range(32)]


FLIP_X = moved(lambda f: f ^ 8)
FLIP_Y = moved(lambda f: f ^ 16)
FLIP_C = moved(lambda f: f ^ 1)


def turn_z(by):
    return moved(lambda f: (f & 25) | ((((f >> 1) + by) & 3) << 1))


def sent(array, pairs):
    return lax.ppermute(array, BOTH, pairs)


def place_of(flat, dy, dx, dz, dc):
    turned = ((((flat >> 1) & 3) + dz) & 3) * 2
    return ((flat & 25) | turned) ^ (dy * 16 + dx * 8 + dc)


def tied(array, *after):
    zero = jnp.zeros((), jnp.float32)
    for other in after:
        first = other[(0,) * other.ndim].astype(jnp.float32)
        zero = zero + jnp.minimum(jnp.abs(first), 0.0)
    return array + zero.astype(array.dtype)


def all_tied(arrays, after):
    return [tied(array, after) for array in arrays]


def assemble_kernel(owners, start, columns, slots_ref, *refs):
    pieces, out_ref, sems = refs[:-2], refs[-2], refs[-1]
    rows = out_ref.shape[1]
    copies = []
    number = 0
    for piece, count in zip(pieces, owners):
        for k in range(count):
            for q in range(columns):
                copies.append(
                    pltpu.make_async_copy(
                        piece.at[k, pl.ds(start + q * rows, rows), :],
                        out_ref.at[slots_ref[number], :, pl.ds(q * 1024, 1024)],
                        sems.at[number, q],
                    )
                )
            number += 1
    for copy in copies:
        copy.start()
    for copy in copies:
        copy.wait()


def assemble(pieces, slots, start, rows, columns):
    counts = [piece.shape[0] for piece in pieces]
    shape = (32, rows, columns * 1024)
    whole = pl.pallas_call(
        partial(assemble_kernel, counts, start, columns),
        out_shape=jax.ShapeDtypeStruct(shape, pieces[0].dtype),
        in_specs=[pl.BlockSpec(memory_space=pltpu.SMEM)]
        + [pl.BlockSpec(memory_space=pltpu.HBM)] * len(pieces),
        out_specs=pl.BlockSpec(memory_space=pltpu.VMEM),
        scratch_shapes=[pltpu.SemaphoreType.DMA((32, columns))],
        compiler_params=pltpu.CompilerParams(vmem_limit_bytes=24 * 1024 * 1024),
        cost_estimate=pl.CostEstimate(
            flops=0, transcendentals=0, bytes_accessed=2 * 2 * 32 * rows * columns * 1024
        ),
    )(slots, *pieces)
    return whole.reshape(32 * rows, columns * 1024)


def stacked(parts):
    rows = [part[:, q : q + 1024] for part in parts for q in range(0, part.shape[1], 1024)]
    return jnp.concatenate(rows, axis=0) if len(rows) > 1 else rows[0]


def around(part):
    return [sent(part, turn_z(d)) for d in (1, 2, 3)]


def pack_kernel(key_ref, value_ref, gate_ref, out_ref):
    for q in range(4):
        out_ref[q * 32 : q * 32 + 32, :] = key_ref[:, q * 1024 : q * 1024 + 1024]
    out_ref[128:256, :] = value_ref[...]
    out_ref[256:288, :] = gate_ref[...]


def pack_late(key, value, gate):
    whole = pl.BlockSpec(memory_space=pltpu.VMEM)
    return pl.pallas_call(
        pack_kernel,
        out_shape=jax.ShapeDtypeStruct((288, 1024), key.dtype),
        in_specs=[whole] * 3,
        out_specs=whole,
    )(key, value, gate)


def long_slots(flat):
    every = (0, 1, 2, 3)
    steps = [(0, 0, every), (0, 1, every), (1, 0, every), (1, 1, (0, 1)), (1, 1, (2, 3))]
    return jnp.stack(
        [place_of(flat, dy, dx, -dz, dc) for dc in (0, 1) for dy, dx, dzs in steps for dz in dzs]
    ).astype(jnp.int32)


def send_far(from_x, from_y):
    half = from_x.shape[0] // 2
    return sent(from_x[:half], FLIP_Y), sent(from_y[half:], FLIP_X)


def both_cores(pieces):
    return pieces + [sent(piece, FLIP_C) for piece in pieces]


def choice(flat, width):
    index = jnp.arange(width)
    block, within = index // (width // 32), index % (width // 32)
    dc, rest = block >> 4, block & 15
    dy, dx, dz = rest >> 3, (rest >> 2) & 1, rest & 3
    wanted = place_of(flat, dy, dx, dz, dc) * (width // 32) + within
    return (jnp.arange(width)[:, None] == wanted[None, :]).astype(jnp.bfloat16)


def dot_nt(left, right):
    return lax.dot_general(
        left, right, (((1,), (1,)), ((), ())), preferred_element_type=jnp.float32
    )


def channel_kernel(slots_ref, *refs):
    key_in_ref, gate_in_ref, middle_ref, grad_ref, late_ref = refs[:5]
    refs = refs[5:]
    out_ref, value_grad_ref, gate_grad_ref, key_back_ref, gate_back_ref = refs[:5]
    hidden_ref, far_hidden_ref, pre_grad_ref, key_w, value_w, gate_w = refs[5:11]
    relu_s, hidden_s, pre_s, total_s, in_sems, hidden_sems, pre_sems = refs[11:]

    def key_copy(q):
        return pltpu.make_async_copy(
            late_ref.at[:, pl.ds(q * 32, 32), :], key_w.at[q], in_sems.at[q]
        )

    def value_copy(q):
        return pltpu.make_async_copy(
            late_ref.at[pl.ds(q * 8, 8), pl.ds(128, 128), :],
            value_w.at[pl.ds(q * 8, 8)],
            in_sems.at[4 + q],
        )

    gate_copy = pltpu.make_async_copy(
        late_ref.at[:, pl.ds(256, 32), :], gate_w, in_sems.at[8]
    )
    for q in range(4):
        key_copy(q).start()
        value_copy(q).start()
    gate_copy.start()

    def hidden_copy(q, k, target):
        return pltpu.make_async_copy(
            hidden_s.at[q, :, pl.ds(k * 128, 128)], target, hidden_sems.at[q, k]
        )

    def hidden_start(q, k):
        slot = slots_ref[q * 8 + k]
        columns = pl.ds(pl.multiple_of((slot & 3) * 128, 128), 128)

        @pl.when(slot < 16)
        def _():
            hidden_copy(q, k, hidden_ref.at[slot >> 2, :, columns]).start()

        @pl.when(slot >= 16)
        def _():
            hidden_copy(q, k, far_hidden_ref.at[(slot >> 2) - 4, :, columns]).start()

    def pre_copy(q):
        return pltpu.make_async_copy(
            pre_s.at[q], pre_grad_ref.at[:, pl.ds(pl.multiple_of(q * 1024, 1024), 1024)], pre_sems.at[q]
        )

    def forward(q, _):
        key_copy(q).wait()
        for half in range(1):
            rows = pl.ds(half * 512, 512)
            relu_s[q, rows, :] = jnp.maximum(
                jnp.dot(
                    key_in_ref[rows, :],
                    key_w[q].reshape(1024, 1024),
                    preferred_element_type=jnp.float32,
                ),
                0.0,
            )
            hidden_s[q, rows, :] = (relu_s[q, rows, :] * relu_s[q, rows, :]).astype(jnp.bfloat16)
        for k in range(8):
            hidden_start(q, k)
        value_copy(q).wait()
        for half in range(1):
            rows = pl.ds(half * 512, 512)
            more = jnp.dot(
                hidden_s[q, rows, :],
                value_w[pl.ds(q * 8, 8)].reshape(1024, 1024),
                preferred_element_type=jnp.float32,
            )

            @pl.when(q == 0)
            def _():
                total_s[rows, :] = more

            @pl.when(q > 0)
            def _():
                total_s[rows, :] += more

        return 0

    lax.fori_loop(0, 4, forward, 0)
    gate_copy.wait()
    for half in range(1):
        rows = pl.ds(half * 512, 512)
        gates = jax.nn.sigmoid(
            jnp.dot(
                gate_in_ref[rows, :],
                gate_w[...].reshape(1024, 1024),
                preferred_element_type=jnp.float32,
            )
        )
        value = total_s[rows, :]
        grads = grad_ref[rows, :].astype(jnp.float32)
        out_ref[rows, :] = (middle_ref[rows, :] + gates * value).astype(jnp.bfloat16)
        value_grad_ref[rows, :] = (grads * gates).astype(jnp.bfloat16)
        gate_grad_ref[rows, :] = (grads * value * gates * (1.0 - gates)).astype(jnp.bfloat16)

    def backward(q, _):
        for half in range(1):
            rows = pl.ds(half * 512, 512)
            pre_s[q, rows, :] = (
                dot_nt(value_grad_ref[rows, :], value_w[pl.ds(q * 8, 8)].reshape(1024, 1024))
                * 2.0
                * relu_s[q, rows, :]
            ).astype(jnp.bfloat16)
        pre_copy(q).start()
        for half in range(1):
            rows = pl.ds(half * 512, 512)
            more = dot_nt(pre_s[q, rows, :], key_w[q].reshape(1024, 1024))

            @pl.when(q == 0)
            def _():
                key_back_ref[rows, :] = more

            @pl.when(q > 0)
            def _():
                key_back_ref[rows, :] += more

        return 0

    lax.fori_loop(0, 4, backward, 0)
    for half in range(1):
        rows = pl.ds(half * 512, 512)
        gate_back_ref[rows, :] = dot_nt(gate_grad_ref[rows, :], gate_w[...].reshape(1024, 1024))
    for q in range(4):
        for k in range(8):
            hidden_copy(q, k, hidden_ref.at[0, :, pl.ds(0, 128)]).wait()
        pre_copy(q).wait()


def channel_mix(slots, key_in, gate_in, middle, grads, late):
    tokens = key_in.shape[0]
    wide_rows = jax.ShapeDtypeStruct((tokens, 1024), jnp.float32)
    half_rows = jax.ShapeDtypeStruct((tokens, 1024), jnp.bfloat16)
    whole = pl.BlockSpec(memory_space=pltpu.VMEM)
    far = pl.BlockSpec(memory_space=pltpu.HBM)
    return pl.pallas_call(
        channel_kernel,
        out_shape=(
            half_rows,
            half_rows,
            half_rows,
            wide_rows,
            wide_rows,
            jax.ShapeDtypeStruct((4, tokens, 512), jnp.bfloat16),
            jax.ShapeDtypeStruct((4, tokens, 512), jnp.bfloat16),
            jax.ShapeDtypeStruct((tokens, 4096), jnp.bfloat16),
        ),
        in_specs=[pl.BlockSpec(memory_space=pltpu.SMEM), whole, whole, whole, whole, far],
        out_specs=(whole,) * 5 + (far,) * 3,
        scratch_shapes=[
            pltpu.VMEM((4, 32, 32, 1024), jnp.bfloat16),
            pltpu.VMEM((32, 128, 1024), jnp.bfloat16),
            pltpu.VMEM((32, 32, 1024), jnp.bfloat16),
            pltpu.VMEM((4, tokens, 1024), jnp.float32),
            pltpu.VMEM((4, tokens, 1024), jnp.bfloat16),
            pltpu.VMEM((4, tokens, 1024), jnp.bfloat16),
            pltpu.VMEM((tokens, 1024), jnp.float32),
            pltpu.SemaphoreType.DMA((9,)),
            pltpu.SemaphoreType.DMA((4, 8)),
            pltpu.SemaphoreType.DMA((4,)),
        ],
        compiler_params=pltpu.CompilerParams(vmem_limit_bytes=54 * 1024 * 1024),
        cost_estimate=pl.CostEstimate(
            flops=2 * tokens * 1024 * 1024 * 18, transcendentals=0, bytes_accessed=40 * 1024 * 1024
        ),
    )(slots, key_in, gate_in, middle, grads, late)


def owner_slots(flat):
    other = jnp.arange(32)
    apart = other ^ flat
    dz = ((other >> 1) - (flat >> 1)) & 3
    return ((apart & 1) * 16 + ((apart >> 4) & 1) * 8 + ((apart >> 3) & 1) * 4 + dz).astype(jnp.int32)


def dot_tn(left, right):
    return lax.dot_general(
        left, right, (((0,), (0,)), ((), ())), preferred_element_type=jnp.float32
    )


def chip_rows(own_in, own_grads, other_in, other_grads):
    return (dot_tn(own_in, own_grads) + dot_tn(other_in, other_grads)).astype(jnp.bfloat16)


def value_part_kernel(own_ref, other_ref, grad_ref, other_grad_ref, near, side_x, side_y, far_a, far_b):
    quarter = pl.program_id(0)
    part = chip_rows(own_ref[0], grad_ref[...], other_ref[0], other_grad_ref[...])
    part = part.reshape((4, part.shape[0] // 4, 1024))

    @pl.when(quarter == 0)
    def _():
        near[...] = part

    @pl.when(quarter == 1)
    def _():
        side_x[...] = part

    @pl.when(quarter == 2)
    def _():
        side_y[...] = part

    @pl.when(quarter == 3)
    def _():
        far_a[...] = part[:2]
        far_b[...] = part[2:]


def store_quarters(part, outs):
    near, side_x, side_y, far_a, far_b = outs
    quarters = part.reshape(4, 4, 32, 1024)
    near[...] = quarters[0]
    side_x[...] = quarters[1]
    side_y[...] = quarters[2]
    far_a[...] = quarters[3, :2]
    far_b[...] = quarters[3, 2:]


def key_part_kernel(key_ref, other_key_ref, gate_ref, other_gate_ref, *refs):
    pre_ref, other_pre_ref, gate_grad_ref, other_gate_grad_ref = refs[:4]
    step = pl.program_id(0)

    @pl.when(step < 4)
    def _():
        store_quarters(
            chip_rows(key_ref[...], pre_ref[...], other_key_ref[...], other_pre_ref[...]), refs[4:]
        )

    @pl.when(step == 4)
    def _():
        store_quarters(
            chip_rows(
                gate_ref[...], gate_grad_ref[...], other_gate_ref[...], other_gate_grad_ref[...]
            ),
            refs[4:],
        )


def time_part_kernel(own_ref, other_ref, grad_ref, other_grad_ref, *refs):
    branch_ref, other_branch_ref = refs[:2]
    step = pl.program_id(0)

    @pl.when(step < 3)
    def _():
        store_quarters(
            chip_rows(own_ref[...], grad_ref[...], other_ref[...], other_grad_ref[...]), refs[2:]
        )

    @pl.when(step == 3)
    def _():
        store_quarters(
            chip_rows(own_ref[...], branch_ref[...], other_ref[...], other_branch_ref[...]), refs[2:]
        )


def in_three(array):
    high = array.astype(jnp.bfloat16)
    rest = array - high.astype(jnp.float32)
    middle = rest.astype(jnp.bfloat16)
    return high, middle, (rest - middle.astype(jnp.float32)).astype(jnp.bfloat16)


def time_mix_kernel(
    branch_ref,
    weight_ref,
    key_ref,
    value_ref,
    gates_ref,
    mask_ref,
    carry_ref,
    num_ref,
    den_ref,
    decay_ref,
    bonus_ref,
    gate_grad_ref,
    key_grad_ref,
    value_grad_ref,
    num_grad_ref,
    den_grad_ref,
    decay_grad_ref,
    bonus_grad_ref,
):
    length = mask_ref.shape[1]
    decay = decay_ref[...]
    bonus = jnp.exp(bonus_ref[...])
    place = lax.broadcasted_iota(jnp.int32, (length, 1), 0).astype(jnp.float32)
    grow = jnp.exp(place * decay)
    shrink = jnp.exp((1.0 - place) * decay)
    for row in range(mask_ref.shape[0]):
        rows = pl.ds(row * length, length)
        mask = mask_ref[row]
        gated_grad = dot_nt(branch_ref[rows, :], weight_ref[...])
        gates = gates_ref[rows, :]
        power = jnp.exp(key_ref[rows, :])
        value = value_ref[rows, :]
        product = power * value
        fade = carry_ref[row] * jnp.exp(-place * decay)
        num_in, den_in = num_ref[row], den_ref[row]
        num_sum = sum(
            jnp.dot(mask, part, preferred_element_type=jnp.float32)
            for part in in_three(product * grow)
        )
        den_sum = sum(
            jnp.dot(mask, part, preferred_element_type=jnp.float32)
            for part in in_three(power * grow)
        )
        numer = fade * num_in + shrink * num_sum + bonus * product
        denom = fade * den_in + shrink * den_sum + bonus * power
        mixed = numer / denom
        gate_grad_ref[rows, :] = (gated_grad * mixed * gates * (1.0 - gates)).astype(jnp.bfloat16)
        num_grad = gated_grad * gates / denom
        den_grad = -num_grad * mixed
        num_back, den_back = shrink * num_grad, shrink * den_grad
        num_past = grow * sum(dot_tn(mask, part) for part in in_three(num_back))
        den_past = grow * sum(dot_tn(mask, part) for part in in_three(den_back))
        product_grad = bonus * num_grad + num_past
        key_grad_ref[rows, :] = power * (value * product_grad + bonus * den_grad + den_past)
        value_grad_ref[rows, :] = power * product_grad
        num_grad_ref[row] = jnp.sum(fade * num_grad, axis=0, keepdims=True)
        den_grad_ref[row] = jnp.sum(fade * den_grad, axis=0, keepdims=True)
        bonus_grad_ref[row] = jnp.sum(
            bonus * (product * num_grad + power * den_grad), axis=0, keepdims=True
        )
        decay_grad_ref[row] = jnp.sum(
            place * (product * num_past + power * den_past)
            + (1.0 - place) * (num_back * num_sum + den_back * den_sum)
            - place * fade * (num_grad * num_in + den_grad * den_in),
            axis=0,
            keepdims=True,
        )


def time_mix_back(branch, weight, key, value, gates, mask, carry, num, den, decay, bonus):
    tokens = branch.shape[0]
    rows, length = mask.shape[:2]
    tile = 256
    wide_block = pl.BlockSpec((tokens, tile), lambda i: (0, i))
    state = pl.BlockSpec((rows, 1, tile), lambda i: (0, 0, i))
    vector = pl.BlockSpec((1, tile), lambda i: (0, i))
    states = jax.ShapeDtypeStruct((rows, 1, 1024), jnp.float32)
    wide_rows = jax.ShapeDtypeStruct((tokens, 1024), jnp.float32)
    return pl.pallas_call(
        time_mix_kernel,
        grid=(1024 // tile,),
        out_shape=(
            jax.ShapeDtypeStruct((tokens, 1024), jnp.bfloat16),
            wide_rows,
            wide_rows,
            states,
            states,
            states,
            states,
        ),
        in_specs=[
            pl.BlockSpec((tokens, 1024), lambda i: (0, 0)),
            pl.BlockSpec((tile, 1024), lambda i: (i, 0)),
            wide_block,
            wide_block,
            wide_block,
            pl.BlockSpec((rows, length, length), lambda i: (0, 0, 0)),
            pl.BlockSpec((rows, length, 1), lambda i: (0, 0, 0)),
            state,
            state,
            vector,
            vector,
        ],
        out_specs=(wide_block, wide_block, wide_block, state, state, state, state),
        compiler_params=pltpu.CompilerParams(vmem_limit_bytes=48 * 1024 * 1024),
        cost_estimate=pl.CostEstimate(flops=1, transcendentals=0, bytes_accessed=1),
    )(branch, weight, key, value, gates, mask, carry, num, den, decay, bonus)


def quarters_call(kernel, steps, rows, in_specs, by_quarter, arguments):
    if by_quarter:
        outs = [pl.BlockSpec((n, rows, 1024), lambda i: (0, 0, 0)) for n in (4, 4, 4, 2, 2)]
    else:
        outs = [pl.BlockSpec((n, 32, 1024), lambda i: (0, i, 0)) for n in (4, 4, 4, 2, 2)]
    return pl.pallas_call(
        kernel,
        grid=(steps,),
        out_shape=tuple(
            jax.ShapeDtypeStruct((n, rows, 1024), jnp.bfloat16) for n in (4, 4, 4, 2, 2)
        ),
        in_specs=in_specs,
        out_specs=tuple(outs),
        compiler_params=pltpu.CompilerParams(vmem_limit_bytes=48 * 1024 * 1024),
        cost_estimate=pl.CostEstimate(flops=1, transcendentals=0, bytes_accessed=1),
    )(*arguments)


def value_part(own_hidden, other_hidden, grads, other_grads):
    tokens = grads.shape[0]
    whole = pl.BlockSpec((tokens, 1024), lambda i: (0, 0))
    block = pl.BlockSpec((1, tokens, 512), lambda i: (i, 0, 0))
    return quarters_call(
        value_part_kernel,
        4,
        128,
        [block, block, whole, whole],
        True,
        (own_hidden, other_hidden, grads, other_grads),
    )


def key_part(key, other_key, gate, other_gate, pre, other_pre, gate_grad, other_gate_grad):
    tokens = pre.shape[0]
    half = pl.BlockSpec((tokens, 512), lambda i: (0, 0))
    whole = pl.BlockSpec((tokens, 1024), lambda i: (0, 0))
    block = pl.BlockSpec((tokens, 1024), lambda i: (0, jnp.minimum(i, 3)))
    return quarters_call(
        key_part_kernel,
        5,
        160,
        [half, half, half, half, block, block, whole, whole],
        False,
        (key, other_key, gate, other_gate, pre, other_pre, gate_grad, other_gate_grad),
    )


def time_part(own, other, grads, other_grads, branch, other_branch):
    tokens = grads.shape[0]
    half = pl.BlockSpec((tokens, 512), lambda i: (0, i))
    whole = pl.BlockSpec((tokens, 1024), lambda i: (0, 0))
    block = pl.BlockSpec((tokens, 1024), lambda i: (0, jnp.minimum(i, 2)))
    return quarters_call(
        time_part_kernel,
        4,
        128,
        [half, half, block, block, whole, whole],
        False,
        (own, other, grads, other_grads, branch, other_branch),
    )


def ordered_halves(rows_in, flat):
    width = rows_in.shape[-1]
    rows_in = rows_in.reshape(-1, width)
    ordered = jnp.dot(rows_in, choice(flat, width), preferred_element_type=jnp.bfloat16)
    return ordered[:, : width // 2], ordered[:, width // 2 :]


def sent_together(arrays):
    got = sent(jnp.concatenate(arrays, axis=1) if len(arrays) > 1 else arrays[0], FLIP_C)
    ends = [sum(a.shape[1] for a in arrays[: i + 1]) for i in range(len(arrays))]
    return [got[:, end - a.shape[1] : end] for a, end in zip(arrays, ends)]


def wide(array):
    return array.astype(jnp.float32)


def narrow(array):
    return array.astype(jnp.bfloat16)


def send_corner(parts):
    return sent(parts[3], FLIP_X), sent(parts[4], FLIP_Y)


def add_corner(parts, add_a, add_b):
    to_y = lax.dynamic_update_slice(parts[2], narrow(wide(parts[2][:2]) + wide(add_a)), (0, 0, 0))
    to_x = lax.dynamic_update_slice(parts[1], narrow(wide(parts[1][2:]) + wide(add_b)), (2, 0, 0))
    return to_y, to_x


def send_sides(to_y, to_x):
    return sent(to_y, FLIP_Y), sent(to_x, FLIP_X)


def add_sides(parts, from_y, from_x):
    column = wide(parts[0]) + wide(from_y) + wide(from_x)
    return column[0], [narrow(column[d]) for d in (1, 2, 3)]


def send_column(outgoing):
    return [sent(part, turn_z(d)) for d, part in zip((1, 2, 3), outgoing)]


def add_all(first, others):
    for other in others:
        first = first + wide(other)
    return first


def sum_plane(total):
    for pairs in (FLIP_C, FLIP_X, FLIP_Y):
        total = total + sent(total, pairs)
    return total


def sum_column(total, flat):
    total = total + sum(sent(total, turn_z(d)) for d in (1, 2, 3))
    count = total.shape[1] // 32
    return lax.dynamic_slice_in_dim(total, flat * count, count, 1)


def shifted(shard, axis, by):
    length = lax.axis_size(axis)
    pairs = [(i, i + by) for i in range(length) if 0 <= i + by < length]
    return lax.ppermute(shard, axis, pairs)


def carried_in(part, starts_in, decay_vec, length, reverse):
    count = lax.axis_size("seq")
    place = lax.axis_index("seq")
    clear = 1.0 - starts_in.astype(jnp.float32)
    block_fade = jnp.exp(-length * decay_vec)

    def clear_of(block):
        return lax.dynamic_index_in_dim(clear, jnp.clip(block, 0, count - 1), 1, True)

    if count == 8:
        chip, core = place >> 1, place & 1
        other = sent(part, FLIP_C)
        is_far = (core == 1) == (not reverse)
        near = jnp.where(is_far, other, part)
        last = jnp.where(is_far, part, other)
        first_block, second_block = chip * 2 + (1 if reverse else 0), chip * 2 + (0 if reverse else 1)
        joined = clear_of(second_block) * block_fade * near + last
        step = -1 if reverse else 1
        entering = jnp.zeros_like(part)
        open_way = jnp.ones((part.shape[1], 1), jnp.float32)
        for d in (1, 2, 3):
            beside = chip - step * d
            live = ((beside >= 0) & (beside < 4)).astype(jnp.float32)
            fade = live * open_way * jnp.exp(-float(2 * (d - 1) * length) * decay_vec)
            entering = entering + fade * sent(joined, turn_z(step * d))
            open_way = open_way * clear_of(2 * beside) * clear_of(2 * beside + 1)
        return jnp.where(is_far, clear_of(first_block) * block_fade * entering + near, entering)
    gathered = lax.all_gather(part, "seq")

    def one(lap, state):
        source = count - 1 - lap if reverse else lap
        return clear_of(source) * block_fade * state + lax.dynamic_index_in_dim(gathered, source, 0, False)

    ahead = count - 1 - place if reverse else place
    return lax.fori_loop(0, ahead, one, jnp.zeros_like(part))


def norm_forward(values, gain_vec, bias_vec):
    centre = values - jnp.mean(values, axis=-1, keepdims=True)
    inv_std = lax.rsqrt(jnp.mean(centre * centre, axis=-1, keepdims=True) + eps)
    normed = centre * inv_std
    return (normed * gain_vec + bias_vec, normed, inv_std)


def norm_backward(grads, normed, inv_std, gain_vec):
    scaled = grads * gain_vec
    inner = (
        scaled
        - jnp.mean(scaled, axis=-1, keepdims=True)
        - normed * jnp.mean(scaled * normed, axis=-1, keepdims=True)
    )
    return (inv_std * inner, jnp.sum(grads * normed, axis=(0, 1)), jnp.sum(grads, axis=(0, 1)))


def project(rows_in, weight):
    return jnp.einsum("rtd,de->rte", rows_in, weight, preferred_element_type=jnp.float32)


def project_back(grads, weight):
    return jnp.einsum("rte,de->rtd", grads, weight, preferred_element_type=jnp.float32)


def weight_grad(rows_in, grads):
    total = jnp.einsum("rtd,rte->de", rows_in, grads, preferred_element_type=jnp.float32)
    return lax.psum_scatter(total, BOTH, scatter_dimension=0, tiled=True)


def weighted_value_local(
    key_row_block,
    value_row_block,
    feature_forgetting_rate,
    present_reward,
    state_numerator,
    state_denominator,
    document_segments,
):
    length = key_row_block.shape[1]
    width = key_row_block.shape[2]
    order_idx = jnp.arange(length)
    step_pos = order_idx.astype(jnp.float32)[:, None]
    powered_lookups = jnp.exp(key_row_block)
    grow_exp = jnp.exp(step_pos * feature_forgetting_rate)
    shrink = jnp.exp((1.0 - step_pos) * feature_forgetting_rate)
    pair_mask = (
        (order_idx[None, :] < order_idx[:, None])[None]
        & (document_segments[:, None, :] == document_segments[:, :, None])
    ).astype(jnp.float32)
    weighted = jnp.concatenate(
        [powered_lookups * value_row_block, powered_lookups], axis=2
    ) * jnp.concatenate([grow_exp, grow_exp], axis=1)
    past_sums = jnp.einsum(
        "rti,rie->rte", pair_mask, weighted, precision=highest
    ) * jnp.concatenate([shrink, shrink], axis=1)
    carry_fade = (document_segments == 0).astype(jnp.float32)[:, :, None] * jnp.exp(
        -step_pos * feature_forgetting_rate
    )
    present_token_contribution = jnp.exp(present_reward) * powered_lookups
    numer = (
        carry_fade * state_numerator[:, None, :]
        + past_sums[:, :, :width]
        + present_token_contribution * value_row_block
    )
    denom = (
        carry_fade * state_denominator[:, None, :]
        + past_sums[:, :, width:]
        + present_token_contribution
    )
    return numer / denom


def tail_terms(key_row_block, value_row_block, feature_forgetting_rate, document_segments):
    length = key_row_block.shape[1]
    step_pos = jnp.arange(length).astype(jnp.float32)[:, None]
    powered_lookups = jnp.exp(key_row_block)
    tail_fade = (document_segments == document_segments[:, -1:]).astype(jnp.float32)[
        :, :, None
    ] * jnp.exp((step_pos - (length - 1)) * feature_forgetting_rate)
    return (
        jnp.sum(tail_fade * powered_lookups * value_row_block, axis=1),
        jnp.sum(tail_fade * powered_lookups, axis=1),
        tail_fade,
        powered_lookups,
    )


def shards(
    tuned,
    incoming_activations,
    sequence_extents,
    upstream_sensitivity,
    initial_normalizer_scale,
    initial_normalizer_offset,
    temporal_lookup_fraction,
    temporal_content_fraction,
    temporal_receptance_fraction,
    feature_forgetting_rate,
    present_reward,
    temporal_lookup_projection,
    temporal_content_projection,
    temporal_receptance_projection,
    temporal_result_projection,
    later_normalizer_scale,
    later_normalizer_offset,
    feature_lookup_fraction,
    feature_receptance_fraction,
    feature_lookup_projection,
    feature_content_projection,
    feature_receptance_projection,
):
    flat = lax.axis_index("batch") * lax.axis_size("seq") + lax.axis_index("seq")
    vectors = jnp.stack(
        [
            initial_normalizer_scale,
            initial_normalizer_offset,
            temporal_lookup_fraction,
            temporal_content_fraction,
            temporal_receptance_fraction,
            feature_forgetting_rate,
            present_reward,
            later_normalizer_scale,
            later_normalizer_offset,
            feature_lookup_fraction,
            feature_receptance_fraction,
        ]
    )
    if tuned:
        order = long_slots(flat)
        late = lax.all_gather(
            pack_late(
                feature_lookup_projection,
                feature_content_projection,
                feature_receptance_projection,
            ),
            BOTH,
        )
        spread = jnp.tile(jnp.pad(vectors, ((0, 5), (0, 0))), (1, 32))
        packed = jnp.where(jnp.arange(1024) // 32 == flat, spread, jnp.zeros_like(spread))
        part = stacked(
            [
                temporal_lookup_projection,
                temporal_content_projection,
                temporal_receptance_projection,
                temporal_result_projection,
                packed,
            ]
        )
        column = jnp.stack([part] + around(part))
        from_x, from_y = sent(column, FLIP_X), sent(column, FLIP_Y)
        early = both_cores([column, from_x, from_y, *send_far(from_x, from_y)])
        vectors = jnp.sum(
            assemble(early, order, 128, 16, 1).reshape(32, 16, 1024).astype(jnp.float32), axis=0
        )
        lookup_weight = assemble(early, order, 0, 32, 1)
        content_weight = assemble(early, order, 32, 32, 1)
        receptance_weight = assemble(early, order, 64, 32, 1)
        result_weight = assemble(early, order, 96, 32, 1)
    else:
        (
            lookup_weight,
            content_weight,
            receptance_weight,
            result_weight,
            ffn_key_weight,
            ffn_gate_weight,
            ffn_value_weight,
        ) = [
            lax.all_gather(part, BOTH, axis=0, tiled=True)
            for part in (
                temporal_lookup_projection,
                temporal_content_projection,
                temporal_receptance_projection,
                temporal_result_projection,
                feature_lookup_projection,
                feature_receptance_projection,
                feature_content_projection,
            )
        ]
        vectors = lax.all_gather(vectors, BOTH, axis=1, tiled=True).astype(jnp.float32)
    (
        opening_standardize_scale,
        opening_standardize_offset,
        temporal_lookup_mixture,
        temporal_content_mixture,
        temporal_receptance_mixture,
        decay_vec,
        reward_array,
        closing_standardize_scale,
        closing_standardize_offset,
        feature_lookup_mixture,
        feature_receptance_mixture,
    ) = tuple(vectors[i] for i in range(11))
    rows, length, width = incoming_activations.shape
    starts = jnp.cumsum(sequence_extents, axis=1) - sequence_extents
    places = lax.axis_index("seq") * length + jnp.arange(length, dtype=jnp.int32)
    resets = jnp.any(
        (starts[:, None, :] == places[None, :, None]) & (sequence_extents[:, None, :] > 0), axis=2
    )
    document_segments = jnp.cumsum(resets.astype(jnp.int32), axis=1)
    keep_mask = 1.0 - resets.astype(jnp.float32)[:, :, None]
    clear_flag = (document_segments[:, -1:] == 0).astype(jnp.float32)
    starts_in = jnp.any(
        (starts[:, None, :] // length == jnp.arange(lax.axis_size("seq"))[None, :, None])
        & (sequence_extents[:, None, :] > 0),
        axis=2,
    )

    inputs = incoming_activations.astype(jnp.float32)
    left_rows = shifted(incoming_activations[:, length - 1 :, :], "seq", 1)
    normed_one, unit_one, inv_one = norm_forward(
        inputs, opening_standardize_scale, opening_standardize_offset
    )
    left_normed, _, _ = norm_forward(
        left_rows.astype(jnp.float32), opening_standardize_scale, opening_standardize_offset
    )
    before_one = jnp.concatenate([left_normed, normed_one[:, :-1, :]], axis=1) * keep_mask
    key_in = (
        normed_one * temporal_lookup_mixture + before_one * (1.0 - temporal_lookup_mixture)
    ).astype(jnp.bfloat16)
    value_in = (
        normed_one * temporal_content_mixture + before_one * (1.0 - temporal_content_mixture)
    ).astype(jnp.bfloat16)
    gate_in = (
        normed_one * temporal_receptance_mixture + before_one * (1.0 - temporal_receptance_mixture)
    ).astype(jnp.bfloat16)
    key_row_block = project(key_in, lookup_weight)
    value_row_block = project(value_in, content_weight)
    gates = jax.nn.sigmoid(project(gate_in, receptance_weight))
    tail_num, tail_den, tail_fade, powered_lookups = tail_terms(
        key_row_block, value_row_block, decay_vec, document_segments
    )
    state_numerator, state_denominator = carried_in(
        jnp.stack([tail_num, tail_den]), starts_in, decay_vec, length, False
    )
    mixed, weighted_value_backward = jax.vjp(
        partial(weighted_value_local, document_segments=document_segments),
        key_row_block,
        value_row_block,
        decay_vec,
        reward_array,
        state_numerator,
        state_denominator,
    )
    gated = (gates * mixed).astype(jnp.bfloat16)
    if tuned:
        own_key, far_key = ordered_halves(key_in, flat)
        own_value, far_value = ordered_halves(value_in, flat)
        own_gate, far_gate = ordered_halves(gate_in, flat)
        own_gated, far_gated = ordered_halves(gated, flat)
        other_time = sent(
            jnp.concatenate([far_key, far_value, far_gate, far_gated], axis=1), FLIP_C
        )
        own_time = jnp.concatenate([own_key, own_value, own_gate, own_gated], axis=1)
    middle = inputs + project(gated, result_weight)
    normed_two, unit_two, inv_two = norm_forward(
        middle, closing_standardize_scale, closing_standardize_offset
    )
    before_rows = shifted(normed_two[:, length - 1 :, :], "seq", 1)
    before_two = jnp.concatenate([before_rows, normed_two[:, :-1, :]], axis=1) * keep_mask
    ffn_key_in = (
        normed_two * feature_lookup_mixture + before_two * (1.0 - feature_lookup_mixture)
    ).astype(jnp.bfloat16)
    ffn_gate_in = (
        normed_two * feature_receptance_mixture + before_two * (1.0 - feature_receptance_mixture)
    ).astype(jnp.bfloat16)
    grad_out = upstream_sensitivity.astype(jnp.float32)
    if tuned:
        own_ffn_key, far_ffn_key = ordered_halves(ffn_key_in, flat)
        own_ffn_gate, far_ffn_gate = ordered_halves(ffn_gate_in, flat)
        other_ffn_key, other_ffn_gate = sent_together([far_ffn_key, far_ffn_gate])
        output, value_grad, ffn_gate_grad, key_two_grad, gate_two_grad, *kept = channel_mix(
            owner_slots(flat),
            ffn_key_in.reshape(-1, width),
            ffn_gate_in.reshape(-1, width),
            middle.reshape(-1, width),
            upstream_sensitivity.reshape(-1, width),
            late,
        )
        output, key_two_grad, gate_two_grad = (
            a.reshape(rows, length, width) for a in (output, key_two_grad, gate_two_grad)
        )
        own_hidden, far_hidden, pre_grad = kept
        other_value_grad = sent(value_grad, FLIP_C)
        other_hidden = sent(far_hidden, FLIP_C)
        other_gate_grad = sent(ffn_gate_grad, FLIP_C)
        other_pre_grad = sent(pre_grad, FLIP_C)
        value_parts = value_part(own_hidden, other_hidden, value_grad, other_value_grad)
        value_corner = send_corner(value_parts)
        key_parts = key_part(
            own_ffn_key,
            other_ffn_key,
            own_ffn_gate,
            other_ffn_gate,
            pre_grad,
            other_pre_grad,
            ffn_gate_grad,
            other_gate_grad,
        )
        value_sides = add_corner(value_parts, *all_tied(value_corner, key_parts[4]))
        value_from = send_sides(*value_sides)
    else:
        hidden_pre = project(ffn_key_in, ffn_key_weight)
        hidden = jnp.square(jax.nn.relu(hidden_pre)).astype(jnp.bfloat16)
        ffn_value = project(hidden, ffn_value_weight)
        ffn_gates = jax.nn.sigmoid(project(ffn_gate_in, ffn_gate_weight))
        output = (middle + ffn_gates * ffn_value).astype(jnp.bfloat16)
        value_grad = (grad_out * ffn_gates).astype(jnp.bfloat16)
        ffn_gate_grad = (grad_out * ffn_value * ffn_gates * (1.0 - ffn_gates)).astype(jnp.bfloat16)
        hidden_grad = project_back(value_grad, ffn_value_weight)
        pre_grad = (hidden_grad * 2.0 * jax.nn.relu(hidden_pre)).astype(jnp.bfloat16)
        grad_ffn_value = weight_grad(hidden, value_grad)
        grad_ffn_key = weight_grad(ffn_key_in, pre_grad)
        grad_ffn_gate = weight_grad(ffn_gate_in, ffn_gate_grad)
        key_two_grad = project_back(pre_grad, ffn_key_weight)
        gate_two_grad = project_back(ffn_gate_grad, ffn_gate_weight)
    spread_two = normed_two - before_two
    grad_ffn_mix_key = jnp.sum(key_two_grad * spread_two, axis=(0, 1))
    grad_ffn_mix_gate = jnp.sum(gate_two_grad * spread_two, axis=(0, 1))
    normed_two_grad = (
        key_two_grad * feature_lookup_mixture + gate_two_grad * feature_receptance_mixture
    )
    before_two_grad = (
        key_two_grad * (1.0 - feature_lookup_mixture)
        + gate_two_grad * (1.0 - feature_receptance_mixture)
    ) * keep_mask
    from_right = shifted(before_two_grad[:, :1, :], "seq", -1)
    normed_two_grad = normed_two_grad + jnp.concatenate(
        [before_two_grad[:, 1:, :], from_right], axis=1
    )
    middle_norm_grad, grad_gain_two, grad_bias_two = norm_backward(
        normed_two_grad, unit_two, inv_two, closing_standardize_scale
    )
    middle_grad = grad_out + middle_norm_grad
    branch_grad = middle_grad.astype(jnp.bfloat16)
    if tuned:
        flat_branch_grad = branch_grad.reshape(-1, width)
        other_branch_grad = sent(flat_branch_grad, FLIP_C)
        key_corner = send_corner(key_parts)
    else:
        grad_output = weight_grad(gated, branch_grad)
    if tuned:
        order_idx = jnp.arange(length)
        pair_mask = (
            (order_idx[None, :] < order_idx[:, None])[None]
            & (document_segments[:, None, :] == document_segments[:, :, None])
        ).astype(jnp.bfloat16)
        (
            gate_pre_grad,
            key_gradient,
            value_gradient,
            numerator_gradient,
            denominator_gradient,
            decay_gradient,
            reward_derivative,
        ) = time_mix_back(
            branch_grad.reshape(-1, width),
            result_weight,
            key_row_block.reshape(-1, width),
            value_row_block.reshape(-1, width),
            gates.reshape(-1, width),
            pair_mask,
            (document_segments == 0).astype(jnp.float32)[:, :, None],
            state_numerator[:, None, :],
            state_denominator[:, None, :],
            tied(decay_vec[None, :], value_sides[0], value_sides[1][2:]),
            reward_array[None, :],
        )
        gate_pre_grad, key_gradient, value_gradient = (
            a.reshape(rows, length, width) for a in (gate_pre_grad, key_gradient, value_gradient)
        )
        numerator_gradient = numerator_gradient[:, 0, :]
        denominator_gradient = denominator_gradient[:, 0, :]
        decay_gradient = jnp.sum(decay_gradient[:, 0, :], axis=0)
        reward_derivative = jnp.sum(reward_derivative[:, 0, :], axis=0)
    else:
        gated_grad = project_back(branch_grad, result_weight)
        gate_pre_grad = (gated_grad * mixed * gates * (1.0 - gates)).astype(jnp.bfloat16)
        blended_gradient = gated_grad * gates
        (
            key_gradient,
            value_gradient,
            decay_gradient,
            reward_derivative,
            numerator_gradient,
            denominator_gradient,
        ) = weighted_value_backward(blended_gradient)
    state_gradient = jnp.stack([numerator_gradient, denominator_gradient])
    if tuned:
        key_sides = add_corner(key_parts, *all_tied(key_corner, state_gradient))
        key_from = send_sides(*key_sides)
        state_gradient = tied(state_gradient, key_sides[0], key_sides[1][2:])
    num_next, den_next = carried_in(state_gradient, starts_in, decay_vec, length, True)
    if tuned:
        value_first, value_outgoing = add_sides(value_parts, *[tied(a, num_next, other_time) for a in value_from])
        num_next = tied(num_next, value_outgoing[0])
    num_tail = tail_fade * num_next[:, None, :]
    den_tail = tail_fade * den_next[:, None, :]
    tail_grad = powered_lookups * (value_row_block * num_tail + den_tail)
    key_gradient = key_gradient + tail_grad
    value_gradient = value_gradient + powered_lookups * num_tail
    offsets = (jnp.arange(length).astype(jnp.float32) - (length - 1))[:, None]
    block_fade = clear_flag * jnp.exp(-length * decay_vec)
    decay_gradient = decay_gradient + jnp.sum(offsets * tail_grad, axis=(0, 1))
    decay_gradient = decay_gradient - length * jnp.sum(
        block_fade * (state_numerator * num_next + state_denominator * den_next), axis=0
    )
    key_grad16 = key_gradient.astype(jnp.bfloat16)
    val_grad16 = value_gradient.astype(jnp.bfloat16)
    if tuned:
        flat_grads = jnp.concatenate(
            [g.reshape(-1, width) for g in (key_grad16, val_grad16, gate_pre_grad)], axis=1
        )
        other_grads = sent(flat_grads, FLIP_C)
        time_parts = time_part(
            own_time, other_time, flat_grads, other_grads, flat_branch_grad, other_branch_grad
        )
        value_got = all_tied(send_column(all_tied(value_outgoing, num_next)), time_parts[4])
        key_first, key_outgoing = add_sides(key_parts, *all_tied(key_from, time_parts[4]))
        time_corner = send_corner(time_parts)
    else:
        grad_key = weight_grad(key_in, key_grad16)
        grad_value = weight_grad(value_in, val_grad16)
        grad_gate = weight_grad(gate_in, gate_pre_grad)
    if tuned:
        key_grad16 = tied(key_grad16, key_outgoing[0])
    key_in_grad = project_back(key_grad16, lookup_weight)
    value_in_grad = project_back(val_grad16, content_weight)
    gate_in_grad = project_back(gate_pre_grad, receptance_weight)
    spread_one = normed_one - before_one
    grad_mix_key = jnp.sum(key_in_grad * spread_one, axis=(0, 1))
    grad_mix_value = jnp.sum(value_in_grad * spread_one, axis=(0, 1))
    grad_mix_gate = jnp.sum(gate_in_grad * spread_one, axis=(0, 1))
    normed_one_grad = (
        key_in_grad * temporal_lookup_mixture
        + value_in_grad * temporal_content_mixture
        + gate_in_grad * temporal_receptance_mixture
    )
    before_one_grad = (
        key_in_grad * (1.0 - temporal_lookup_mixture)
        + value_in_grad * (1.0 - temporal_content_mixture)
        + gate_in_grad * (1.0 - temporal_receptance_mixture)
    ) * keep_mask
    if tuned:
        time_sides = add_corner(time_parts, *all_tied(time_corner, before_one_grad))
        time_from = send_sides(*time_sides)
    from_next = shifted(before_one_grad[:, :1, :], "seq", -1)
    if tuned:
        key_got = send_column(all_tied(key_outgoing, from_next))
        from_next = tied(from_next, time_sides[0], time_sides[1][2:])
    normed_one_grad = normed_one_grad + jnp.concatenate(
        [before_one_grad[:, 1:, :], from_next], axis=1
    )
    input_norm_grad, grad_gain_one, grad_bias_one = norm_backward(
        normed_one_grad, unit_one, inv_one, opening_standardize_scale
    )
    input_grad = middle_grad + input_norm_grad
    vector_grads = jnp.stack(
        [
            grad_gain_one,
            grad_bias_one,
            grad_mix_key,
            grad_mix_value,
            grad_mix_gate,
            decay_gradient,
            reward_derivative,
            grad_gain_two,
            grad_bias_two,
            grad_ffn_mix_key,
            grad_ffn_mix_gate,
        ]
    )
    if tuned:
        time_first, time_outgoing = add_sides(time_parts, *all_tied(time_from, vector_grads))
        key_total = add_all(key_first, all_tied(key_got, vector_grads))
        time_got = send_column(time_outgoing)
        time_total = add_all(time_first, time_got)
        grad_key, grad_value, grad_gate, grad_output = (
            time_total[i : i + 32] for i in (0, 32, 64, 96)
        )
        grad_ffn_value = add_all(value_first, value_got)
        grad_ffn_key = jnp.concatenate([key_total[i : i + 32] for i in (0, 32, 64, 96)], axis=1)
        grad_ffn_gate = key_total[128:]
        vector_grads = sum_column(tied(sum_plane(vector_grads), time_got[0]), flat)
    else:
        vector_grads = lax.psum_scatter(vector_grads, BOTH, scatter_dimension=1, tiled=True)
    return (
        output,
        input_grad,
        vector_grads[0],
        vector_grads[1],
        vector_grads[2],
        vector_grads[3],
        vector_grads[4],
        vector_grads[5],
        vector_grads[6],
        grad_key,
        grad_value,
        grad_gate,
        grad_output,
        vector_grads[7],
        vector_grads[8],
        vector_grads[9],
        vector_grads[10],
        grad_ffn_key,
        grad_ffn_value,
        grad_ffn_gate,
    )


def solution(mesh):
    tuned = tuple(mesh.shape.items()) == (("batch", 4), ("seq", 8))
    return jax.shard_map(
        partial(shards, tuned),
        mesh=mesh,
        in_specs=(
            P("batch", "seq", None),
            P("batch", None),
            P("batch", "seq", None),
            P(("batch", "seq")),
            P(("batch", "seq")),
            P(("batch", "seq")),
            P(("batch", "seq")),
            P(("batch", "seq")),
            P(("batch", "seq")),
            P(("batch", "seq")),
            P(("batch", "seq"), None),
            P(("batch", "seq"), None),
            P(("batch", "seq"), None),
            P(("batch", "seq"), None),
            P(("batch", "seq")),
            P(("batch", "seq")),
            P(("batch", "seq")),
            P(("batch", "seq")),
            P(("batch", "seq"), None),
            P(("batch", "seq"), None),
            P(("batch", "seq"), None),
        ),
        out_specs=(
            P("batch", "seq", None),
            P("batch", "seq", None),
            P(("batch", "seq")),
            P(("batch", "seq")),
            P(("batch", "seq")),
            P(("batch", "seq")),
            P(("batch", "seq")),
            P(("batch", "seq")),
            P(("batch", "seq")),
            P(("batch", "seq"), None),
            P(("batch", "seq"), None),
            P(("batch", "seq"), None),
            P(("batch", "seq"), None),
            P(("batch", "seq")),
            P(("batch", "seq")),
            P(("batch", "seq")),
            P(("batch", "seq")),
            P(("batch", "seq"), None),
            P(("batch", "seq"), None),
            P(("batch", "seq"), None),
        ),
        check_vma=False,
    )
```

```python
from functools import partial

import jax
import jax.numpy as jnp
from jax import lax
from jax.experimental import pallas as pl
from jax.experimental.pallas import tpu as pltpu
from jax.sharding import PartitionSpec as P

eps = 1e-05
highest = lax.Precision.HIGHEST
BOTH = ("batch", "seq")


def moved(rule):
    return [(f, rule(f)) for f in range(32)]


FLIP_X = moved(lambda f: f ^ 8)
FLIP_Y = moved(lambda f: f ^ 16)
FLIP_C = moved(lambda f: f ^ 1)


def turn_z(by):
    return moved(lambda f: (f & 25) | ((((f >> 1) + by) & 3) << 1))


def sent(array, pairs):
    return lax.ppermute(array, BOTH, pairs)


def place_of(flat, dy, dx, dz, dc):
    turned = ((((flat >> 1) & 3) + dz) & 3) * 2
    return ((flat & 25) | turned) ^ (dy * 16 + dx * 8 + dc)


def tied(array, *after):
    zero = jnp.zeros((), jnp.float32)
    for other in after:
        first = other[(0,) * other.ndim].astype(jnp.float32)
        zero = zero + jnp.minimum(jnp.abs(first), 0.0)
    return array + zero.astype(array.dtype)


def all_tied(arrays, after):
    return [tied(array, after) for array in arrays]


def assemble_kernel(owners, start, columns, slots_ref, *refs):
    pieces, out_ref, sems = refs[:-2], refs[-2], refs[-1]
    rows = out_ref.shape[1]
    copies = []
    number = 0
    for piece, count in zip(pieces, owners):
        for k in range(count):
            for q in range(columns):
                copies.append(
                    pltpu.make_async_copy(
                        piece.at[k, pl.ds(start + q * rows, rows), :],
                        out_ref.at[slots_ref[number], :, pl.ds(q * 1024, 1024)],
                        sems.at[number, q],
                    )
                )
            number += 1
    for copy in copies:
        copy.start()
    for copy in copies:
        copy.wait()


def assemble(pieces, slots, start, rows, columns):
    counts = [piece.shape[0] for piece in pieces]
    shape = (32, rows, columns * 1024)
    whole = pl.pallas_call(
        partial(assemble_kernel, counts, start, columns),
        out_shape=jax.ShapeDtypeStruct(shape, pieces[0].dtype),
        in_specs=[pl.BlockSpec(memory_space=pltpu.SMEM)]
        + [pl.BlockSpec(memory_space=pltpu.HBM)] * len(pieces),
        out_specs=pl.BlockSpec(memory_space=pltpu.VMEM),
        scratch_shapes=[pltpu.SemaphoreType.DMA((32, columns))],
        compiler_params=pltpu.CompilerParams(vmem_limit_bytes=24 * 1024 * 1024),
        cost_estimate=pl.CostEstimate(
            flops=0, transcendentals=0, bytes_accessed=2 * 2 * 32 * rows * columns * 1024
        ),
    )(slots, *pieces)
    return whole.reshape(32 * rows, columns * 1024)


def stacked(parts):
    rows = [part[:, q : q + 1024] for part in parts for q in range(0, part.shape[1], 1024)]
    return jnp.concatenate(rows, axis=0) if len(rows) > 1 else rows[0]


def around(part):
    return [sent(part, turn_z(d)) for d in (1, 2, 3)]


def pack_kernel(key_ref, value_ref, gate_ref, out_ref):
    for q in range(4):
        out_ref[q * 32 : q * 32 + 32, :] = key_ref[:, q * 1024 : q * 1024 + 1024]
    out_ref[128:256, :] = value_ref[...]
    out_ref[256:288, :] = gate_ref[...]


def pack_late(key, value, gate):
    whole = pl.BlockSpec(memory_space=pltpu.VMEM)
    return pl.pallas_call(
        pack_kernel,
        out_shape=jax.ShapeDtypeStruct((288, 1024), key.dtype),
        in_specs=[whole] * 3,
        out_specs=whole,
    )(key, value, gate)


def long_slots(flat):
    every = (0, 1, 2, 3)
    steps = [(0, 0, every), (0, 1, every), (1, 0, every), (1, 1, (0, 1)), (1, 1, (2, 3))]
    return jnp.stack(
        [place_of(flat, dy, dx, -dz, dc) for dc in (0, 1) for dy, dx, dzs in steps for dz in dzs]
    ).astype(jnp.int32)


def send_far(from_x, from_y):
    half = from_x.shape[0] // 2
    return sent(from_x[:half], FLIP_Y), sent(from_y[half:], FLIP_X)


def both_cores(pieces):
    return pieces + [sent(piece, FLIP_C) for piece in pieces]


def choice(flat, width):
    index = jnp.arange(width)
    block, within = index // (width // 32), index % (width // 32)
    dc, rest = block >> 4, block & 15
    dy, dx, dz = rest >> 3, (rest >> 2) & 1, rest & 3
    wanted = place_of(flat, dy, dx, dz, dc) * (width // 32) + within
    return (jnp.arange(width)[:, None] == wanted[None, :]).astype(jnp.bfloat16)


def dot_nt(left, right):
    return lax.dot_general(
        left, right, (((1,), (1,)), ((), ())), preferred_element_type=jnp.float32
    )


def channel_kernel(slots_ref, *refs):
    key_in_ref, gate_in_ref, middle_ref, grad_ref, late_ref = refs[:5]
    refs = refs[5:]
    out_ref, value_grad_ref, gate_grad_ref, key_back_ref, gate_back_ref = refs[:5]
    hidden_ref, far_hidden_ref, pre_grad_ref, key_w, value_w, gate_w = refs[5:11]
    relu_s, hidden_s, pre_s, total_s, in_sems, hidden_sems, pre_sems = refs[11:]

    def key_copy(q):
        return pltpu.make_async_copy(
            late_ref.at[:, pl.ds(q * 32, 32), :], key_w.at[q], in_sems.at[q]
        )

    def value_copy(q):
        return pltpu.make_async_copy(
            late_ref.at[pl.ds(q * 8, 8), pl.ds(128, 128), :],
            value_w.at[pl.ds(q * 8, 8)],
            in_sems.at[4 + q],
        )

    gate_copy = pltpu.make_async_copy(
        late_ref.at[:, pl.ds(256, 32), :], gate_w, in_sems.at[8]
    )
    for q in range(4):
        key_copy(q).start()
        value_copy(q).start()
    gate_copy.start()

    def hidden_copy(q, k, target):
        return pltpu.make_async_copy(
            hidden_s.at[q, :, pl.ds(k * 128, 128)], target, hidden_sems.at[q, k]
        )

    def hidden_start(q, k):
        slot = slots_ref[q * 8 + k]
        columns = pl.ds(pl.multiple_of((slot & 3) * 128, 128), 128)

        @pl.when(slot < 16)
        def _():
            hidden_copy(q, k, hidden_ref.at[slot >> 2, :, columns]).start()

        @pl.when(slot >= 16)
        def _():
            hidden_copy(q, k, far_hidden_ref.at[(slot >> 2) - 4, :, columns]).start()

    def pre_copy(q):
        return pltpu.make_async_copy(
            pre_s.at[q], pre_grad_ref.at[:, pl.ds(pl.multiple_of(q * 1024, 1024), 1024)], pre_sems.at[q]
        )

    def forward(q, _):
        key_copy(q).wait()
        for half in range(1):
            rows = pl.ds(half * 512, 512)
            relu_s[q, rows, :] = jnp.maximum(
                jnp.dot(
                    key_in_ref[rows, :],
                    key_w[q].reshape(1024, 1024),
                    preferred_element_type=jnp.float32,
                ),
                0.0,
            )
            hidden_s[q, rows, :] = (relu_s[q, rows, :] * relu_s[q, rows, :]).astype(jnp.bfloat16)
        for k in range(8):
            hidden_start(q, k)
        value_copy(q).wait()
        for half in range(1):
            rows = pl.ds(half * 512, 512)
            more = jnp.dot(
                hidden_s[q, rows, :],
                value_w[pl.ds(q * 8, 8)].reshape(1024, 1024),
                preferred_element_type=jnp.float32,
            )

            @pl.when(q == 0)
            def _():
                total_s[rows, :] = more

            @pl.when(q > 0)
            def _():
                total_s[rows, :] += more

        return 0

    lax.fori_loop(0, 4, forward, 0)
    gate_copy.wait()
    for half in range(1):
        rows = pl.ds(half * 512, 512)
        gates = jax.nn.sigmoid(
            jnp.dot(
                gate_in_ref[rows, :],
                gate_w[...].reshape(1024, 1024),
                preferred_element_type=jnp.float32,
            )
        )
        value = total_s[rows, :]
        grads = grad_ref[rows, :].astype(jnp.float32)
        out_ref[rows, :] = (middle_ref[rows, :] + gates * value).astype(jnp.bfloat16)
        value_grad_ref[rows, :] = (grads * gates).astype(jnp.bfloat16)
        gate_grad_ref[rows, :] = (grads * value * gates * (1.0 - gates)).astype(jnp.bfloat16)

    def backward(q, _):
        for half in range(1):
            rows = pl.ds(half * 512, 512)
            pre_s[q, rows, :] = (
                dot_nt(value_grad_ref[rows, :], value_w[pl.ds(q * 8, 8)].reshape(1024, 1024))
                * 2.0
                * relu_s[q, rows, :]
            ).astype(jnp.bfloat16)
        pre_copy(q).start()
        for half in range(1):
            rows = pl.ds(half * 512, 512)
            more = dot_nt(pre_s[q, rows, :], key_w[q].reshape(1024, 1024))

            @pl.when(q == 0)
            def _():
                key_back_ref[rows, :] = more

            @pl.when(q > 0)
            def _():
                key_back_ref[rows, :] += more

        return 0

    lax.fori_loop(0, 4, backward, 0)
    for half in range(1):
        rows = pl.ds(half * 512, 512)
        gate_back_ref[rows, :] = dot_nt(gate_grad_ref[rows, :], gate_w[...].reshape(1024, 1024))
    for q in range(4):
        for k in range(8):
            hidden_copy(q, k, hidden_ref.at[0, :, pl.ds(0, 128)]).wait()
        pre_copy(q).wait()


def channel_mix(slots, key_in, gate_in, middle, grads, late):
    tokens = key_in.shape[0]
    wide_rows = jax.ShapeDtypeStruct((tokens, 1024), jnp.float32)
    half_rows = jax.ShapeDtypeStruct((tokens, 1024), jnp.bfloat16)
    whole = pl.BlockSpec(memory_space=pltpu.VMEM)
    far = pl.BlockSpec(memory_space=pltpu.HBM)
    return pl.pallas_call(
        channel_kernel,
        out_shape=(
            half_rows,
            half_rows,
            half_rows,
            wide_rows,
            wide_rows,
            jax.ShapeDtypeStruct((4, tokens, 512), jnp.bfloat16),
            jax.ShapeDtypeStruct((4, tokens, 512), jnp.bfloat16),
            jax.ShapeDtypeStruct((tokens, 4096), jnp.bfloat16),
        ),
        in_specs=[pl.BlockSpec(memory_space=pltpu.SMEM), whole, whole, whole, whole, far],
        out_specs=(whole,) * 5 + (far,) * 3,
        scratch_shapes=[
            pltpu.VMEM((4, 32, 32, 1024), jnp.bfloat16),
            pltpu.VMEM((32, 128, 1024), jnp.bfloat16),
            pltpu.VMEM((32, 32, 1024), jnp.bfloat16),
            pltpu.VMEM((4, tokens, 1024), jnp.float32),
            pltpu.VMEM((4, tokens, 1024), jnp.bfloat16),
            pltpu.VMEM((4, tokens, 1024), jnp.bfloat16),
            pltpu.VMEM((tokens, 1024), jnp.float32),
            pltpu.SemaphoreType.DMA((9,)),
            pltpu.SemaphoreType.DMA((4, 8)),
            pltpu.SemaphoreType.DMA((4,)),
        ],
        compiler_params=pltpu.CompilerParams(vmem_limit_bytes=54 * 1024 * 1024),
        cost_estimate=pl.CostEstimate(
            flops=2 * tokens * 1024 * 1024 * 18, transcendentals=0, bytes_accessed=40 * 1024 * 1024
        ),
    )(slots, key_in, gate_in, middle, grads, late)


def owner_slots(flat):
    other = jnp.arange(32)
    apart = other ^ flat
    dz = ((other >> 1) - (flat >> 1)) & 3
    return ((apart & 1) * 16 + ((apart >> 4) & 1) * 8 + ((apart >> 3) & 1) * 4 + dz).astype(jnp.int32)


def dot_tn(left, right):
    return lax.dot_general(
        left, right, (((0,), (0,)), ((), ())), preferred_element_type=jnp.float32
    )


def chip_rows(own_in, own_grads, other_in, other_grads):
    return (dot_tn(own_in, own_grads) + dot_tn(other_in, other_grads)).astype(jnp.bfloat16)


def value_part_kernel(own_ref, other_ref, grad_ref, other_grad_ref, near, side_x, side_y, far_a, far_b):
    quarter = pl.program_id(0)
    part = chip_rows(own_ref[0], grad_ref[...], other_ref[0], other_grad_ref[...])
    part = part.reshape((4, part.shape[0] // 4, 1024))

    @pl.when(quarter == 0)
    def _():
        near[...] = part

    @pl.when(quarter == 1)
    def _():
        side_x[...] = part

    @pl.when(quarter == 2)
    def _():
        side_y[...] = part

    @pl.when(quarter == 3)
    def _():
        far_a[...] = part[:2]
        far_b[...] = part[2:]


def store_quarters(part, outs):
    near, side_x, side_y, far_a, far_b = outs
    quarters = part.reshape(4, 4, 32, 1024)
    near[...] = quarters[0]
    side_x[...] = quarters[1]
    side_y[...] = quarters[2]
    far_a[...] = quarters[3, :2]
    far_b[...] = quarters[3, 2:]


def key_part_kernel(key_ref, other_key_ref, gate_ref, other_gate_ref, *refs):
    pre_ref, other_pre_ref, gate_grad_ref, other_gate_grad_ref = refs[:4]
    step = pl.program_id(0)

    @pl.when(step < 4)
    def _():
        store_quarters(
            chip_rows(key_ref[...], pre_ref[...], other_key_ref[...], other_pre_ref[...]), refs[4:]
        )

    @pl.when(step == 4)
    def _():
        store_quarters(
            chip_rows(
                gate_ref[...], gate_grad_ref[...], other_gate_ref[...], other_gate_grad_ref[...]
            ),
            refs[4:],
        )


def time_part_kernel(own_ref, other_ref, grad_ref, other_grad_ref, *refs):
    branch_ref, other_branch_ref = refs[:2]
    step = pl.program_id(0)

    @pl.when(step < 3)
    def _():
        store_quarters(
            chip_rows(own_ref[...], grad_ref[...], other_ref[...], other_grad_ref[...]), refs[2:]
        )

    @pl.when(step == 3)
    def _():
        store_quarters(
            chip_rows(own_ref[...], branch_ref[...], other_ref[...], other_branch_ref[...]), refs[2:]
        )


def in_three(array):
    high = array.astype(jnp.bfloat16)
    rest = array - high.astype(jnp.float32)
    middle = rest.astype(jnp.bfloat16)
    return high, middle, (rest - middle.astype(jnp.float32)).astype(jnp.bfloat16)


def time_mix_kernel(
    branch_ref,
    weight_ref,
    key_ref,
    value_ref,
    gates_ref,
    mask_ref,
    carry_ref,
    num_ref,
    den_ref,
    decay_ref,
    bonus_ref,
    gate_grad_ref,
    key_grad_ref,
    value_grad_ref,
    num_grad_ref,
    den_grad_ref,
    decay_grad_ref,
    bonus_grad_ref,
):
    length = mask_ref.shape[1]
    decay = decay_ref[...]
    bonus = jnp.exp(bonus_ref[...])
    place = lax.broadcasted_iota(jnp.int32, (length, 1), 0).astype(jnp.float32)
    grow = jnp.exp(place * decay)
    shrink = jnp.exp((1.0 - place) * decay)
    for row in range(mask_ref.shape[0]):
        rows = pl.ds(row * length, length)
        mask = mask_ref[row]
        gated_grad = dot_nt(branch_ref[rows, :], weight_ref[...])
        gates = gates_ref[rows, :]
        power = jnp.exp(key_ref[rows, :])
        value = value_ref[rows, :]
        product = power * value
        fade = carry_ref[row] * jnp.exp(-place * decay)
        num_in, den_in = num_ref[row], den_ref[row]
        num_sum = sum(
            jnp.dot(mask, part, preferred_element_type=jnp.float32)
            for part in in_three(product * grow)
        )
        den_sum = sum(
            jnp.dot(mask, part, preferred_element_type=jnp.float32)
            for part in in_three(power * grow)
        )
        numer = fade * num_in + shrink * num_sum + bonus * product
        denom = fade * den_in + shrink * den_sum + bonus * power
        mixed = numer / denom
        gate_grad_ref[rows, :] = (gated_grad * mixed * gates * (1.0 - gates)).astype(jnp.bfloat16)
        num_grad = gated_grad * gates / denom
        den_grad = -num_grad * mixed
        num_back, den_back = shrink * num_grad, shrink * den_grad
        num_past = grow * sum(dot_tn(mask, part) for part in in_three(num_back))
        den_past = grow * sum(dot_tn(mask, part) for part in in_three(den_back))
        product_grad = bonus * num_grad + num_past
        key_grad_ref[rows, :] = power * (value * product_grad + bonus * den_grad + den_past)
        value_grad_ref[rows, :] = power * product_grad
        num_grad_ref[row] = jnp.sum(fade * num_grad, axis=0, keepdims=True)
        den_grad_ref[row] = jnp.sum(fade * den_grad, axis=0, keepdims=True)
        bonus_grad_ref[row] = jnp.sum(
            bonus * (product * num_grad + power * den_grad), axis=0, keepdims=True
        )
        decay_grad_ref[row] = jnp.sum(
            place * (product * num_past + power * den_past)
            + (1.0 - place) * (num_back * num_sum + den_back * den_sum)
            - place * fade * (num_grad * num_in + den_grad * den_in),
            axis=0,
            keepdims=True,
        )


def time_mix_back(branch, weight, key, value, gates, mask, carry, num, den, decay, bonus):
    tokens = branch.shape[0]
    rows, length = mask.shape[:2]
    tile = 256
    wide_block = pl.BlockSpec((tokens, tile), lambda i: (0, i))
    state = pl.BlockSpec((rows, 1, tile), lambda i: (0, 0, i))
    vector = pl.BlockSpec((1, tile), lambda i: (0, i))
    states = jax.ShapeDtypeStruct((rows, 1, 1024), jnp.float32)
    wide_rows = jax.ShapeDtypeStruct((tokens, 1024), jnp.float32)
    return pl.pallas_call(
        time_mix_kernel,
        grid=(1024 // tile,),
        out_shape=(
            jax.ShapeDtypeStruct((tokens, 1024), jnp.bfloat16),
            wide_rows,
            wide_rows,
            states,
            states,
            states,
            states,
        ),
        in_specs=[
            pl.BlockSpec((tokens, 1024), lambda i: (0, 0)),
            pl.BlockSpec((tile, 1024), lambda i: (i, 0)),
            wide_block,
            wide_block,
            wide_block,
            pl.BlockSpec((rows, length, length), lambda i: (0, 0, 0)),
            pl.BlockSpec((rows, length, 1), lambda i: (0, 0, 0)),
            state,
            state,
            vector,
            vector,
        ],
        out_specs=(wide_block, wide_block, wide_block, state, state, state, state),
        compiler_params=pltpu.CompilerParams(vmem_limit_bytes=48 * 1024 * 1024),
        cost_estimate=pl.CostEstimate(flops=1, transcendentals=0, bytes_accessed=1),
    )(branch, weight, key, value, gates, mask, carry, num, den, decay, bonus)


def quarters_call(kernel, steps, rows, in_specs, by_quarter, arguments):
    if by_quarter:
        outs = [pl.BlockSpec((n, rows, 1024), lambda i: (0, 0, 0)) for n in (4, 4, 4, 2, 2)]
    else:
        outs = [pl.BlockSpec((n, 32, 1024), lambda i: (0, i, 0)) for n in (4, 4, 4, 2, 2)]
    return pl.pallas_call(
        kernel,
        grid=(steps,),
        out_shape=tuple(
            jax.ShapeDtypeStruct((n, rows, 1024), jnp.bfloat16) for n in (4, 4, 4, 2, 2)
        ),
        in_specs=in_specs,
        out_specs=tuple(outs),
        compiler_params=pltpu.CompilerParams(vmem_limit_bytes=48 * 1024 * 1024),
        cost_estimate=pl.CostEstimate(flops=1, transcendentals=0, bytes_accessed=1),
    )(*arguments)


def value_part(own_hidden, other_hidden, grads, other_grads):
    tokens = grads.shape[0]
    whole = pl.BlockSpec((tokens, 1024), lambda i: (0, 0))
    block = pl.BlockSpec((1, tokens, 512), lambda i: (i, 0, 0))
    return quarters_call(
        value_part_kernel,
        4,
        128,
        [block, block, whole, whole],
        True,
        (own_hidden, other_hidden, grads, other_grads),
    )


def key_part(key, other_key, gate, other_gate, pre, other_pre, gate_grad, other_gate_grad):
    tokens = pre.shape[0]
    half = pl.BlockSpec((tokens, 512), lambda i: (0, 0))
    whole = pl.BlockSpec((tokens, 1024), lambda i: (0, 0))
    block = pl.BlockSpec((tokens, 1024), lambda i: (0, jnp.minimum(i, 3)))
    return quarters_call(
        key_part_kernel,
        5,
        160,
        [half, half, half, half, block, block, whole, whole],
        False,
        (key, other_key, gate, other_gate, pre, other_pre, gate_grad, other_gate_grad),
    )


def time_part(own, other, grads, other_grads, branch, other_branch):
    tokens = grads.shape[0]
    half = pl.BlockSpec((tokens, 512), lambda i: (0, i))
    whole = pl.BlockSpec((tokens, 1024), lambda i: (0, 0))
    block = pl.BlockSpec((tokens, 1024), lambda i: (0, jnp.minimum(i, 2)))
    return quarters_call(
        time_part_kernel,
        4,
        128,
        [half, half, block, block, whole, whole],
        False,
        (own, other, grads, other_grads, branch, other_branch),
    )


def ordered_halves(rows_in, flat):
    width = rows_in.shape[-1]
    rows_in = rows_in.reshape(-1, width)
    ordered = jnp.dot(rows_in, choice(flat, width), preferred_element_type=jnp.bfloat16)
    return ordered[:, : width // 2], ordered[:, width // 2 :]


def sent_together(arrays):
    got = sent(jnp.concatenate(arrays, axis=1) if len(arrays) > 1 else arrays[0], FLIP_C)
    ends = [sum(a.shape[1] for a in arrays[: i + 1]) for i in range(len(arrays))]
    return [got[:, end - a.shape[1] : end] for a, end in zip(arrays, ends)]


def wide(array):
    return array.astype(jnp.float32)


def narrow(array):
    return array.astype(jnp.bfloat16)


def send_corner(parts):
    return sent(parts[3], FLIP_X), sent(parts[4], FLIP_Y)


def add_corner(parts, add_a, add_b):
    to_y = lax.dynamic_update_slice(parts[2], narrow(wide(parts[2][:2]) + wide(add_a)), (0, 0, 0))
    to_x = lax.dynamic_update_slice(parts[1], narrow(wide(parts[1][2:]) + wide(add_b)), (2, 0, 0))
    return to_y, to_x


def send_sides(to_y, to_x):
    return sent(to_y, FLIP_Y), sent(to_x, FLIP_X)


def add_sides(parts, from_y, from_x):
    column = wide(parts[0]) + wide(from_y) + wide(from_x)
    return column[0], [narrow(column[d]) for d in (1, 2, 3)]


def send_column(outgoing):
    return [sent(part, turn_z(d)) for d, part in zip((1, 2, 3), outgoing)]


def add_all(first, others):
    for other in others:
        first = first + wide(other)
    return first


def sum_plane(total):
    for pairs in (FLIP_C, FLIP_X, FLIP_Y):
        total = total + sent(total, pairs)
    return total


def sum_column(total, flat):
    total = total + sum(sent(total, turn_z(d)) for d in (1, 2, 3))
    count = total.shape[1] // 32
    return lax.dynamic_slice_in_dim(total, flat * count, count, 1)


def shifted(shard, axis, by):
    length = lax.axis_size(axis)
    pairs = [(i, i + by) for i in range(length) if 0 <= i + by < length]
    return lax.ppermute(shard, axis, pairs)


def carried_in(part, starts_in, decay_vec, length, reverse, between=None):
    count = lax.axis_size("seq")
    place = lax.axis_index("seq")
    clear = 1.0 - starts_in.astype(jnp.float32)
    block_fade = jnp.exp(-length * decay_vec)

    def clear_of(block):
        return lax.dynamic_index_in_dim(clear, jnp.clip(block, 0, count - 1), 1, True)

    if count == 8:
        chip, core = place >> 1, place & 1
        other = sent(part, FLIP_C)
        is_far = (core == 1) == (not reverse)
        near = jnp.where(is_far, other, part)
        last = jnp.where(is_far, part, other)
        first_block, second_block = chip * 2 + (1 if reverse else 0), chip * 2 + (0 if reverse else 1)
        joined = clear_of(second_block) * block_fade * near + last
        if between is not None:
            joined = between(joined)
        step = -1 if reverse else 1
        entering = jnp.zeros_like(part)
        open_way = jnp.ones((part.shape[1], 1), jnp.float32)
        for d in (1, 2, 3):
            beside = chip - step * d
            live = ((beside >= 0) & (beside < 4)).astype(jnp.float32)
            fade = live * open_way * jnp.exp(-float(2 * (d - 1) * length) * decay_vec)
            entering = entering + fade * sent(joined, turn_z(step * d))
            open_way = open_way * clear_of(2 * beside) * clear_of(2 * beside + 1)
        return jnp.where(is_far, clear_of(first_block) * block_fade * entering + near, entering)
    gathered = lax.all_gather(part, "seq")

    def one(lap, state):
        source = count - 1 - lap if reverse else lap
        return clear_of(source) * block_fade * state + lax.dynamic_index_in_dim(gathered, source, 0, False)

    ahead = count - 1 - place if reverse else place
    return lax.fori_loop(0, ahead, one, jnp.zeros_like(part))


def norm_forward(values, gain_vec, bias_vec):
    centre = values - jnp.mean(values, axis=-1, keepdims=True)
    inv_std = lax.rsqrt(jnp.mean(centre * centre, axis=-1, keepdims=True) + eps)
    normed = centre * inv_std
    return (normed * gain_vec + bias_vec, normed, inv_std)


def norm_backward(grads, normed, inv_std, gain_vec):
    scaled = grads * gain_vec
    inner = (
        scaled
        - jnp.mean(scaled, axis=-1, keepdims=True)
        - normed * jnp.mean(scaled * normed, axis=-1, keepdims=True)
    )
    return (inv_std * inner, jnp.sum(grads * normed, axis=(0, 1)), jnp.sum(grads, axis=(0, 1)))


def project(rows_in, weight):
    return jnp.einsum("rtd,de->rte", rows_in, weight, preferred_element_type=jnp.float32)


def project_back(grads, weight):
    return jnp.einsum("rte,de->rtd", grads, weight, preferred_element_type=jnp.float32)


def weight_grad(rows_in, grads):
    total = jnp.einsum("rtd,rte->de", rows_in, grads, preferred_element_type=jnp.float32)
    return lax.psum_scatter(total, BOTH, scatter_dimension=0, tiled=True)


def weighted_value_local(
    key_row_block,
    value_row_block,
    feature_forgetting_rate,
    present_reward,
    state_numerator,
    state_denominator,
    document_segments,
):
    length = key_row_block.shape[1]
    width = key_row_block.shape[2]
    order_idx = jnp.arange(length)
    step_pos = order_idx.astype(jnp.float32)[:, None]
    powered_lookups = jnp.exp(key_row_block)
    grow_exp = jnp.exp(step_pos * feature_forgetting_rate)
    shrink = jnp.exp((1.0 - step_pos) * feature_forgetting_rate)
    pair_mask = (
        (order_idx[None, :] < order_idx[:, None])[None]
        & (document_segments[:, None, :] == document_segments[:, :, None])
    ).astype(jnp.float32)
    weighted = jnp.concatenate(
        [powered_lookups * value_row_block, powered_lookups], axis=2
    ) * jnp.concatenate([grow_exp, grow_exp], axis=1)
    past_sums = jnp.einsum(
        "rti,rie->rte", pair_mask, weighted, precision=highest
    ) * jnp.concatenate([shrink, shrink], axis=1)
    carry_fade = (document_segments == 0).astype(jnp.float32)[:, :, None] * jnp.exp(
        -step_pos * feature_forgetting_rate
    )
    present_token_contribution = jnp.exp(present_reward) * powered_lookups
    numer = (
        carry_fade * state_numerator[:, None, :]
        + past_sums[:, :, :width]
        + present_token_contribution * value_row_block
    )
    denom = (
        carry_fade * state_denominator[:, None, :]
        + past_sums[:, :, width:]
        + present_token_contribution
    )
    return numer / denom


def tail_terms(key_row_block, value_row_block, feature_forgetting_rate, document_segments):
    length = key_row_block.shape[1]
    step_pos = jnp.arange(length).astype(jnp.float32)[:, None]
    powered_lookups = jnp.exp(key_row_block)
    tail_fade = (document_segments == document_segments[:, -1:]).astype(jnp.float32)[
        :, :, None
    ] * jnp.exp((step_pos - (length - 1)) * feature_forgetting_rate)
    return (
        jnp.sum(tail_fade * powered_lookups * value_row_block, axis=1),
        jnp.sum(tail_fade * powered_lookups, axis=1),
        tail_fade,
        powered_lookups,
    )


def shards(
    tuned,
    incoming_activations,
    sequence_extents,
    upstream_sensitivity,
    initial_normalizer_scale,
    initial_normalizer_offset,
    temporal_lookup_fraction,
    temporal_content_fraction,
    temporal_receptance_fraction,
    feature_forgetting_rate,
    present_reward,
    temporal_lookup_projection,
    temporal_content_projection,
    temporal_receptance_projection,
    temporal_result_projection,
    later_normalizer_scale,
    later_normalizer_offset,
    feature_lookup_fraction,
    feature_receptance_fraction,
    feature_lookup_projection,
    feature_content_projection,
    feature_receptance_projection,
):
    flat = lax.axis_index("batch") * lax.axis_size("seq") + lax.axis_index("seq")
    vectors = jnp.stack(
        [
            initial_normalizer_scale,
            initial_normalizer_offset,
            temporal_lookup_fraction,
            temporal_content_fraction,
            temporal_receptance_fraction,
            feature_forgetting_rate,
            present_reward,
            later_normalizer_scale,
            later_normalizer_offset,
            feature_lookup_fraction,
            feature_receptance_fraction,
        ]
    )
    if tuned:
        order = long_slots(flat)
        late = lax.all_gather(
            pack_late(
                feature_lookup_projection,
                feature_content_projection,
                feature_receptance_projection,
            ),
            BOTH,
        )
        spread = jnp.tile(jnp.pad(vectors, ((0, 5), (0, 0))), (1, 32))
        packed = jnp.where(jnp.arange(1024) // 32 == flat, spread, jnp.zeros_like(spread))
        part = stacked(
            [
                temporal_lookup_projection,
                temporal_content_projection,
                temporal_receptance_projection,
                temporal_result_projection,
                packed,
            ]
        )
        column = jnp.stack([part] + around(part))
        from_x, from_y = sent(column, FLIP_X), sent(column, FLIP_Y)
        early = both_cores([column, from_x, from_y, *send_far(from_x, from_y)])
        vectors = jnp.sum(
            assemble(early, order, 128, 16, 1).reshape(32, 16, 1024).astype(jnp.float32), axis=0
        )
        lookup_weight = assemble(early, order, 0, 32, 1)
        content_weight = assemble(early, order, 32, 32, 1)
        receptance_weight = assemble(early, order, 64, 32, 1)
        result_weight = assemble(early, order, 96, 32, 1)
    else:
        (
            lookup_weight,
            content_weight,
            receptance_weight,
            result_weight,
            ffn_key_weight,
            ffn_gate_weight,
            ffn_value_weight,
        ) = [
            lax.all_gather(part, BOTH, axis=0, tiled=True)
            for part in (
                temporal_lookup_projection,
                temporal_content_projection,
                temporal_receptance_projection,
                temporal_result_projection,
                feature_lookup_projection,
                feature_receptance_projection,
                feature_content_projection,
            )
        ]
        vectors = lax.all_gather(vectors, BOTH, axis=1, tiled=True).astype(jnp.float32)
    (
        opening_standardize_scale,
        opening_standardize_offset,
        temporal_lookup_mixture,
        temporal_content_mixture,
        temporal_receptance_mixture,
        decay_vec,
        reward_array,
        closing_standardize_scale,
        closing_standardize_offset,
        feature_lookup_mixture,
        feature_receptance_mixture,
    ) = tuple(vectors[i] for i in range(11))
    rows, length, width = incoming_activations.shape
    starts = jnp.cumsum(sequence_extents, axis=1) - sequence_extents
    places = lax.axis_index("seq") * length + jnp.arange(length, dtype=jnp.int32)
    resets = jnp.any(
        (starts[:, None, :] == places[None, :, None]) & (sequence_extents[:, None, :] > 0), axis=2
    )
    document_segments = jnp.cumsum(resets.astype(jnp.int32), axis=1)
    keep_mask = 1.0 - resets.astype(jnp.float32)[:, :, None]
    clear_flag = (document_segments[:, -1:] == 0).astype(jnp.float32)
    starts_in = jnp.any(
        (starts[:, None, :] // length == jnp.arange(lax.axis_size("seq"))[None, :, None])
        & (sequence_extents[:, None, :] > 0),
        axis=2,
    )

    inputs = incoming_activations.astype(jnp.float32)
    left_rows = shifted(incoming_activations[:, length - 1 :, :], "seq", 1)
    normed_one, unit_one, inv_one = norm_forward(
        inputs, opening_standardize_scale, opening_standardize_offset
    )
    left_normed, _, _ = norm_forward(
        left_rows.astype(jnp.float32), opening_standardize_scale, opening_standardize_offset
    )
    before_one = jnp.concatenate([left_normed, normed_one[:, :-1, :]], axis=1) * keep_mask
    key_in = (
        normed_one * temporal_lookup_mixture + before_one * (1.0 - temporal_lookup_mixture)
    ).astype(jnp.bfloat16)
    value_in = (
        normed_one * temporal_content_mixture + before_one * (1.0 - temporal_content_mixture)
    ).astype(jnp.bfloat16)
    gate_in = (
        normed_one * temporal_receptance_mixture + before_one * (1.0 - temporal_receptance_mixture)
    ).astype(jnp.bfloat16)
    key_row_block = project(key_in, lookup_weight)
    value_row_block = project(value_in, content_weight)
    gates = jax.nn.sigmoid(project(gate_in, receptance_weight))
    tail_num, tail_den, tail_fade, powered_lookups = tail_terms(
        key_row_block, value_row_block, decay_vec, document_segments
    )
    state_numerator, state_denominator = carried_in(
        jnp.stack([tail_num, tail_den]), starts_in, decay_vec, length, False
    )
    mixed, weighted_value_backward = jax.vjp(
        partial(weighted_value_local, document_segments=document_segments),
        key_row_block,
        value_row_block,
        decay_vec,
        reward_array,
        state_numerator,
        state_denominator,
    )
    gated = (gates * mixed).astype(jnp.bfloat16)
    if tuned:
        own_key, far_key = ordered_halves(key_in, flat)
        own_value, far_value = ordered_halves(value_in, flat)
        own_gate, far_gate = ordered_halves(gate_in, flat)
        own_gated, far_gated = ordered_halves(gated, flat)
        other_time = sent(
            jnp.concatenate([far_key, far_value, far_gate, far_gated], axis=1), FLIP_C
        )
        own_time = jnp.concatenate([own_key, own_value, own_gate, own_gated], axis=1)
    middle = inputs + project(gated, result_weight)
    normed_two, unit_two, inv_two = norm_forward(
        middle, closing_standardize_scale, closing_standardize_offset
    )
    before_rows = shifted(normed_two[:, length - 1 :, :], "seq", 1)
    before_two = jnp.concatenate([before_rows, normed_two[:, :-1, :]], axis=1) * keep_mask
    ffn_key_in = (
        normed_two * feature_lookup_mixture + before_two * (1.0 - feature_lookup_mixture)
    ).astype(jnp.bfloat16)
    ffn_gate_in = (
        normed_two * feature_receptance_mixture + before_two * (1.0 - feature_receptance_mixture)
    ).astype(jnp.bfloat16)
    grad_out = upstream_sensitivity.astype(jnp.float32)
    if tuned:
        own_ffn_key, far_ffn_key = ordered_halves(ffn_key_in, flat)
        own_ffn_gate, far_ffn_gate = ordered_halves(ffn_gate_in, flat)
        other_ffn_key, other_ffn_gate = sent_together([far_ffn_key, far_ffn_gate])
        output, value_grad, ffn_gate_grad, key_two_grad, gate_two_grad, *kept = channel_mix(
            owner_slots(flat),
            ffn_key_in.reshape(-1, width),
            ffn_gate_in.reshape(-1, width),
            middle.reshape(-1, width),
            upstream_sensitivity.reshape(-1, width),
            late,
        )
        output, key_two_grad, gate_two_grad = (
            a.reshape(rows, length, width) for a in (output, key_two_grad, gate_two_grad)
        )
        own_hidden, far_hidden, pre_grad = kept
        other_value_grad = sent(value_grad, FLIP_C)
        other_hidden = sent(far_hidden, FLIP_C)
        other_gate_grad = sent(ffn_gate_grad, FLIP_C)
        other_pre_grad = sent(pre_grad, FLIP_C)
        value_parts = value_part(own_hidden, other_hidden, value_grad, other_value_grad)
        value_corner = send_corner(value_parts)
        key_parts = key_part(
            own_ffn_key,
            other_ffn_key,
            own_ffn_gate,
            other_ffn_gate,
            pre_grad,
            other_pre_grad,
            ffn_gate_grad,
            other_gate_grad,
        )
        value_sides = add_corner(value_parts, *all_tied(value_corner, key_parts[4]))
        value_from = send_sides(*value_sides)
    else:
        hidden_pre = project(ffn_key_in, ffn_key_weight)
        hidden = jnp.square(jax.nn.relu(hidden_pre)).astype(jnp.bfloat16)
        ffn_value = project(hidden, ffn_value_weight)
        ffn_gates = jax.nn.sigmoid(project(ffn_gate_in, ffn_gate_weight))
        output = (middle + ffn_gates * ffn_value).astype(jnp.bfloat16)
        value_grad = (grad_out * ffn_gates).astype(jnp.bfloat16)
        ffn_gate_grad = (grad_out * ffn_value * ffn_gates * (1.0 - ffn_gates)).astype(jnp.bfloat16)
        hidden_grad = project_back(value_grad, ffn_value_weight)
        pre_grad = (hidden_grad * 2.0 * jax.nn.relu(hidden_pre)).astype(jnp.bfloat16)
        grad_ffn_value = weight_grad(hidden, value_grad)
        grad_ffn_key = weight_grad(ffn_key_in, pre_grad)
        grad_ffn_gate = weight_grad(ffn_gate_in, ffn_gate_grad)
        key_two_grad = project_back(pre_grad, ffn_key_weight)
        gate_two_grad = project_back(ffn_gate_grad, ffn_gate_weight)
    spread_two = normed_two - before_two
    grad_ffn_mix_key = jnp.sum(key_two_grad * spread_two, axis=(0, 1))
    grad_ffn_mix_gate = jnp.sum(gate_two_grad * spread_two, axis=(0, 1))
    normed_two_grad = (
        key_two_grad * feature_lookup_mixture + gate_two_grad * feature_receptance_mixture
    )
    before_two_grad = (
        key_two_grad * (1.0 - feature_lookup_mixture)
        + gate_two_grad * (1.0 - feature_receptance_mixture)
    ) * keep_mask
    from_right = shifted(before_two_grad[:, :1, :], "seq", -1)
    normed_two_grad = normed_two_grad + jnp.concatenate(
        [before_two_grad[:, 1:, :], from_right], axis=1
    )
    middle_norm_grad, grad_gain_two, grad_bias_two = norm_backward(
        normed_two_grad, unit_two, inv_two, closing_standardize_scale
    )
    middle_grad = grad_out + middle_norm_grad
    branch_grad = middle_grad.astype(jnp.bfloat16)
    if tuned:
        flat_branch_grad = branch_grad.reshape(-1, width)
        other_branch_grad = sent(flat_branch_grad, FLIP_C)
        key_corner = send_corner(key_parts)
    else:
        grad_output = weight_grad(gated, branch_grad)
    if tuned:
        order_idx = jnp.arange(length)
        pair_mask = (
            (order_idx[None, :] < order_idx[:, None])[None]
            & (document_segments[:, None, :] == document_segments[:, :, None])
        ).astype(jnp.bfloat16)
        (
            gate_pre_grad,
            key_gradient,
            value_gradient,
            numerator_gradient,
            denominator_gradient,
            decay_gradient,
            reward_derivative,
        ) = time_mix_back(
            branch_grad.reshape(-1, width),
            result_weight,
            key_row_block.reshape(-1, width),
            value_row_block.reshape(-1, width),
            gates.reshape(-1, width),
            pair_mask,
            (document_segments == 0).astype(jnp.float32)[:, :, None],
            state_numerator[:, None, :],
            state_denominator[:, None, :],
            tied(decay_vec[None, :], value_sides[0], value_sides[1][2:]),
            reward_array[None, :],
        )
        gate_pre_grad, key_gradient, value_gradient = (
            a.reshape(rows, length, width) for a in (gate_pre_grad, key_gradient, value_gradient)
        )
        numerator_gradient = numerator_gradient[:, 0, :]
        denominator_gradient = denominator_gradient[:, 0, :]
        decay_gradient = jnp.sum(decay_gradient[:, 0, :], axis=0)
        reward_derivative = jnp.sum(reward_derivative[:, 0, :], axis=0)
    else:
        gated_grad = project_back(branch_grad, result_weight)
        gate_pre_grad = (gated_grad * mixed * gates * (1.0 - gates)).astype(jnp.bfloat16)
        blended_gradient = gated_grad * gates
        (
            key_gradient,
            value_gradient,
            decay_gradient,
            reward_derivative,
            numerator_gradient,
            denominator_gradient,
        ) = weighted_value_backward(blended_gradient)
    state_gradient = jnp.stack([numerator_gradient, denominator_gradient])
    if tuned:
        key_sides = add_corner(key_parts, *all_tied(key_corner, state_gradient))
        key_from = send_sides(*key_sides)
        state_gradient = tied(state_gradient, key_sides[0], key_sides[1][2:])
    summed = []

    def beside_sides(joined):
        summed.extend(
            add_sides(value_parts, *[tied(a, joined, other_time) for a in value_from])
        )
        return tied(joined, summed[1][0])

    num_next, den_next = carried_in(
        state_gradient, starts_in, decay_vec, length, True, beside_sides if tuned else None
    )
    if tuned:
        value_first, value_outgoing = summed
    num_tail = tail_fade * num_next[:, None, :]
    den_tail = tail_fade * den_next[:, None, :]
    tail_grad = powered_lookups * (value_row_block * num_tail + den_tail)
    key_gradient = key_gradient + tail_grad
    value_gradient = value_gradient + powered_lookups * num_tail
    offsets = (jnp.arange(length).astype(jnp.float32) - (length - 1))[:, None]
    block_fade = clear_flag * jnp.exp(-length * decay_vec)
    decay_gradient = decay_gradient + jnp.sum(offsets * tail_grad, axis=(0, 1))
    decay_gradient = decay_gradient - length * jnp.sum(
        block_fade * (state_numerator * num_next + state_denominator * den_next), axis=0
    )
    key_grad16 = key_gradient.astype(jnp.bfloat16)
    val_grad16 = value_gradient.astype(jnp.bfloat16)
    if tuned:
        flat_grads = jnp.concatenate(
            [g.reshape(-1, width) for g in (key_grad16, val_grad16, gate_pre_grad)], axis=1
        )
        other_grads = sent(flat_grads, FLIP_C)
        time_parts = time_part(
            own_time, other_time, flat_grads, other_grads, flat_branch_grad, other_branch_grad
        )
        value_got = all_tied(send_column(all_tied(value_outgoing, num_next)), time_parts[4])
        key_first, key_outgoing = add_sides(key_parts, *all_tied(key_from, time_parts[4]))
        time_corner = send_corner(time_parts)
    else:
        grad_key = weight_grad(key_in, key_grad16)
        grad_value = weight_grad(value_in, val_grad16)
        grad_gate = weight_grad(gate_in, gate_pre_grad)
    if tuned:
        key_grad16 = tied(key_grad16, key_outgoing[0])
    key_in_grad = project_back(key_grad16, lookup_weight)
    value_in_grad = project_back(val_grad16, content_weight)
    gate_in_grad = project_back(gate_pre_grad, receptance_weight)
    spread_one = normed_one - before_one
    grad_mix_key = jnp.sum(key_in_grad * spread_one, axis=(0, 1))
    grad_mix_value = jnp.sum(value_in_grad * spread_one, axis=(0, 1))
    grad_mix_gate = jnp.sum(gate_in_grad * spread_one, axis=(0, 1))
    normed_one_grad = (
        key_in_grad * temporal_lookup_mixture
        + value_in_grad * temporal_content_mixture
        + gate_in_grad * temporal_receptance_mixture
    )
    before_one_grad = (
        key_in_grad * (1.0 - temporal_lookup_mixture)
        + value_in_grad * (1.0 - temporal_content_mixture)
        + gate_in_grad * (1.0 - temporal_receptance_mixture)
    ) * keep_mask
    if tuned:
        time_sides = add_corner(time_parts, *all_tied(time_corner, before_one_grad))
        time_from = send_sides(*time_sides)
    from_next = shifted(before_one_grad[:, :1, :], "seq", -1)
    if tuned:
        key_got = send_column(all_tied(key_outgoing, from_next))
        from_next = tied(from_next, time_sides[0], time_sides[1][2:])
    normed_one_grad = normed_one_grad + jnp.concatenate(
        [before_one_grad[:, 1:, :], from_next], axis=1
    )
    input_norm_grad, grad_gain_one, grad_bias_one = norm_backward(
        normed_one_grad, unit_one, inv_one, opening_standardize_scale
    )
    input_grad = middle_grad + input_norm_grad
    vector_grads = jnp.stack(
        [
            grad_gain_one,
            grad_bias_one,
            grad_mix_key,
            grad_mix_value,
            grad_mix_gate,
            decay_gradient,
            reward_derivative,
            grad_gain_two,
            grad_bias_two,
            grad_ffn_mix_key,
            grad_ffn_mix_gate,
        ]
    )
    if tuned:
        time_first, time_outgoing = add_sides(time_parts, *all_tied(time_from, vector_grads))
        key_total = add_all(key_first, all_tied(key_got, vector_grads))
        time_got = send_column(time_outgoing)
        time_total = add_all(time_first, time_got)
        grad_key, grad_value, grad_gate, grad_output = (
            time_total[i : i + 32] for i in (0, 32, 64, 96)
        )
        grad_ffn_value = add_all(value_first, value_got)
        grad_ffn_key = jnp.concatenate([key_total[i : i + 32] for i in (0, 32, 64, 96)], axis=1)
        grad_ffn_gate = key_total[128:]
        vector_grads = sum_column(tied(sum_plane(vector_grads), time_got[0]), flat)
    else:
        vector_grads = lax.psum_scatter(vector_grads, BOTH, scatter_dimension=1, tiled=True)
    return (
        output,
        input_grad,
        vector_grads[0],
        vector_grads[1],
        vector_grads[2],
        vector_grads[3],
        vector_grads[4],
        vector_grads[5],
        vector_grads[6],
        grad_key,
        grad_value,
        grad_gate,
        grad_output,
        vector_grads[7],
        vector_grads[8],
        vector_grads[9],
        vector_grads[10],
        grad_ffn_key,
        grad_ffn_value,
        grad_ffn_gate,
    )


def solution(mesh):
    tuned = tuple(mesh.shape.items()) == (("batch", 4), ("seq", 8))
    return jax.shard_map(
        partial(shards, tuned),
        mesh=mesh,
        in_specs=(
            P("batch", "seq", None),
            P("batch", None),
            P("batch", "seq", None),
            P(("batch", "seq")),
            P(("batch", "seq")),
            P(("batch", "seq")),
            P(("batch", "seq")),
            P(("batch", "seq")),
            P(("batch", "seq")),
            P(("batch", "seq")),
            P(("batch", "seq"), None),
            P(("batch", "seq"), None),
            P(("batch", "seq"), None),
            P(("batch", "seq"), None),
            P(("batch", "seq")),
            P(("batch", "seq")),
            P(("batch", "seq")),
            P(("batch", "seq")),
            P(("batch", "seq"), None),
            P(("batch", "seq"), None),
            P(("batch", "seq"), None),
        ),
        out_specs=(
            P("batch", "seq", None),
            P("batch", "seq", None),
            P(("batch", "seq")),
            P(("batch", "seq")),
            P(("batch", "seq")),
            P(("batch", "seq")),
            P(("batch", "seq")),
            P(("batch", "seq")),
            P(("batch", "seq")),
            P(("batch", "seq"), None),
            P(("batch", "seq"), None),
            P(("batch", "seq"), None),
            P(("batch", "seq"), None),
            P(("batch", "seq")),
            P(("batch", "seq")),
            P(("batch", "seq")),
            P(("batch", "seq")),
            P(("batch", "seq"), None),
            P(("batch", "seq"), None),
            P(("batch", "seq"), None),
        ),
        check_vma=False,
    )
```

```python
from functools import partial

import jax
import jax.numpy as jnp
from jax import lax
from jax.experimental import pallas as pl
from jax.experimental.pallas import tpu as pltpu
from jax.sharding import PartitionSpec as P

eps = 1e-05
highest = lax.Precision.HIGHEST
BOTH = ("batch", "seq")


def moved(rule):
    return [(f, rule(f)) for f in range(32)]


FLIP_X = moved(lambda f: f ^ 8)
FLIP_Y = moved(lambda f: f ^ 16)
FLIP_C = moved(lambda f: f ^ 1)


def turn_z(by):
    return moved(lambda f: (f & 25) | ((((f >> 1) + by) & 3) << 1))


def sent(array, pairs):
    return lax.ppermute(array, BOTH, pairs)


def place_of(flat, dy, dx, dz, dc):
    turned = ((((flat >> 1) & 3) + dz) & 3) * 2
    return ((flat & 25) | turned) ^ (dy * 16 + dx * 8 + dc)


def tied(array, *after):
    zero = jnp.zeros((), jnp.float32)
    for other in after:
        first = other[(0,) * other.ndim].astype(jnp.float32)
        zero = zero + jnp.minimum(jnp.abs(first), 0.0)
    return array + zero.astype(array.dtype)


def all_tied(arrays, after):
    return [tied(array, after) for array in arrays]


def assemble_kernel(owners, start, columns, slots_ref, *refs):
    pieces, out_ref, sems = refs[:-2], refs[-2], refs[-1]
    rows = out_ref.shape[1]
    copies = []
    number = 0
    for piece, count in zip(pieces, owners):
        for k in range(count):
            for q in range(columns):
                copies.append(
                    pltpu.make_async_copy(
                        piece.at[k, pl.ds(start + q * rows, rows), :],
                        out_ref.at[slots_ref[number], :, pl.ds(q * 1024, 1024)],
                        sems.at[number, q],
                    )
                )
            number += 1
    for copy in copies:
        copy.start()
    for copy in copies:
        copy.wait()


def assemble(pieces, slots, start, rows, columns):
    counts = [piece.shape[0] for piece in pieces]
    shape = (32, rows, columns * 1024)
    whole = pl.pallas_call(
        partial(assemble_kernel, counts, start, columns),
        out_shape=jax.ShapeDtypeStruct(shape, pieces[0].dtype),
        in_specs=[pl.BlockSpec(memory_space=pltpu.SMEM)]
        + [pl.BlockSpec(memory_space=pltpu.HBM)] * len(pieces),
        out_specs=pl.BlockSpec(memory_space=pltpu.VMEM),
        scratch_shapes=[pltpu.SemaphoreType.DMA((32, columns))],
        compiler_params=pltpu.CompilerParams(vmem_limit_bytes=24 * 1024 * 1024),
        cost_estimate=pl.CostEstimate(
            flops=0, transcendentals=0, bytes_accessed=2 * 2 * 32 * rows * columns * 1024
        ),
    )(slots, *pieces)
    return whole.reshape(32 * rows, columns * 1024)


def stacked(parts):
    rows = [part[:, q : q + 1024] for part in parts for q in range(0, part.shape[1], 1024)]
    return jnp.concatenate(rows, axis=0) if len(rows) > 1 else rows[0]


def around(part):
    return [sent(part, turn_z(d)) for d in (1, 2, 3)]


def pack_kernel(key_ref, value_ref, gate_ref, out_ref):
    for q in range(4):
        out_ref[q * 32 : q * 32 + 32, :] = key_ref[:, q * 1024 : q * 1024 + 1024]
    out_ref[128:256, :] = value_ref[...]
    out_ref[256:288, :] = gate_ref[...]


def pack_late(key, value, gate):
    whole = pl.BlockSpec(memory_space=pltpu.VMEM)
    return pl.pallas_call(
        pack_kernel,
        out_shape=jax.ShapeDtypeStruct((288, 1024), key.dtype),
        in_specs=[whole] * 3,
        out_specs=whole,
    )(key, value, gate)


def long_slots(flat):
    every = (0, 1, 2, 3)
    steps = [(0, 0, every), (0, 1, every), (1, 0, every), (1, 1, (0, 1)), (1, 1, (2, 3))]
    return jnp.stack(
        [place_of(flat, dy, dx, -dz, dc) for dc in (0, 1) for dy, dx, dzs in steps for dz in dzs]
    ).astype(jnp.int32)


def send_far(from_x, from_y):
    half = from_x.shape[0] // 2
    return sent(from_x[:half], FLIP_Y), sent(from_y[half:], FLIP_X)


def both_cores(pieces):
    return pieces + [sent(piece, FLIP_C) for piece in pieces]


def choice(flat, width):
    index = jnp.arange(width)
    block, within = index // (width // 32), index % (width // 32)
    dc, rest = block >> 4, block & 15
    dy, dx, dz = rest >> 3, (rest >> 2) & 1, rest & 3
    wanted = place_of(flat, dy, dx, dz, dc) * (width // 32) + within
    return (jnp.arange(width)[:, None] == wanted[None, :]).astype(jnp.bfloat16)


def dot_nt(left, right):
    return lax.dot_general(
        left, right, (((1,), (1,)), ((), ())), preferred_element_type=jnp.float32
    )


def channel_kernel(slots_ref, *refs):
    key_in_ref, gate_in_ref, middle_ref, grad_ref, late_ref = refs[:5]
    refs = refs[5:]
    out_ref, value_grad_ref, gate_grad_ref, key_back_ref, gate_back_ref = refs[:5]
    hidden_ref, far_hidden_ref, pre_grad_ref, key_w, value_w, gate_w = refs[5:11]
    relu_s, hidden_s, pre_s, total_s, in_sems, hidden_sems, pre_sems = refs[11:]

    def key_copy(q):
        return pltpu.make_async_copy(
            late_ref.at[:, pl.ds(q * 32, 32), :], key_w.at[q], in_sems.at[q]
        )

    def value_copy(q):
        return pltpu.make_async_copy(
            late_ref.at[pl.ds(q * 8, 8), pl.ds(128, 128), :],
            value_w.at[pl.ds(q * 8, 8)],
            in_sems.at[4 + q],
        )

    gate_copy = pltpu.make_async_copy(
        late_ref.at[:, pl.ds(256, 32), :], gate_w, in_sems.at[8]
    )
    for q in range(4):
        key_copy(q).start()
        value_copy(q).start()
    gate_copy.start()

    def hidden_copy(q, k, target):
        return pltpu.make_async_copy(
            hidden_s.at[q, :, pl.ds(k * 128, 128)], target, hidden_sems.at[q, k]
        )

    def hidden_start(q, k):
        slot = slots_ref[q * 8 + k]
        columns = pl.ds(pl.multiple_of((slot & 3) * 128, 128), 128)

        @pl.when(slot < 16)
        def _():
            hidden_copy(q, k, hidden_ref.at[slot >> 2, :, columns]).start()

        @pl.when(slot >= 16)
        def _():
            hidden_copy(q, k, far_hidden_ref.at[(slot >> 2) - 4, :, columns]).start()

    def pre_copy(q):
        return pltpu.make_async_copy(
            pre_s.at[q], pre_grad_ref.at[:, pl.ds(pl.multiple_of(q * 1024, 1024), 1024)], pre_sems.at[q]
        )

    def forward(q, _):
        key_copy(q).wait()
        for half in range(1):
            rows = pl.ds(half * 512, 512)
            relu_s[q, rows, :] = jnp.maximum(
                jnp.dot(
                    key_in_ref[rows, :],
                    key_w[q].reshape(1024, 1024),
                    preferred_element_type=jnp.float32,
                ),
                0.0,
            )
            hidden_s[q, rows, :] = (relu_s[q, rows, :] * relu_s[q, rows, :]).astype(jnp.bfloat16)
        for k in range(8):
            hidden_start(q, k)
        value_copy(q).wait()
        for half in range(1):
            rows = pl.ds(half * 512, 512)
            more = jnp.dot(
                hidden_s[q, rows, :],
                value_w[pl.ds(q * 8, 8)].reshape(1024, 1024),
                preferred_element_type=jnp.float32,
            )

            @pl.when(q == 0)
            def _():
                total_s[rows, :] = more

            @pl.when(q > 0)
            def _():
                total_s[rows, :] += more

        return 0

    lax.fori_loop(0, 4, forward, 0)
    gate_copy.wait()
    for half in range(1):
        rows = pl.ds(half * 512, 512)
        gates = jax.nn.sigmoid(
            jnp.dot(
                gate_in_ref[rows, :],
                gate_w[...].reshape(1024, 1024),
                preferred_element_type=jnp.float32,
            )
        )
        value = total_s[rows, :]
        grads = grad_ref[rows, :].astype(jnp.float32)
        out_ref[rows, :] = (middle_ref[rows, :] + gates * value).astype(jnp.bfloat16)
        value_grad_ref[rows, :] = (grads * gates).astype(jnp.bfloat16)
        gate_grad_ref[rows, :] = (grads * value * gates * (1.0 - gates)).astype(jnp.bfloat16)

    def backward(q, _):
        for half in range(1):
            rows = pl.ds(half * 512, 512)
            pre_s[q, rows, :] = (
                dot_nt(value_grad_ref[rows, :], value_w[pl.ds(q * 8, 8)].reshape(1024, 1024))
                * 2.0
                * relu_s[q, rows, :]
            ).astype(jnp.bfloat16)
        pre_copy(q).start()
        for half in range(1):
            rows = pl.ds(half * 512, 512)
            more = dot_nt(pre_s[q, rows, :], key_w[q].reshape(1024, 1024))

            @pl.when(q == 0)
            def _():
                key_back_ref[rows, :] = more

            @pl.when(q > 0)
            def _():
                key_back_ref[rows, :] += more

        return 0

    lax.fori_loop(0, 4, backward, 0)
    for half in range(1):
        rows = pl.ds(half * 512, 512)
        gate_back_ref[rows, :] = dot_nt(gate_grad_ref[rows, :], gate_w[...].reshape(1024, 1024))
    for q in range(4):
        for k in range(8):
            hidden_copy(q, k, hidden_ref.at[0, :, pl.ds(0, 128)]).wait()
        pre_copy(q).wait()


def channel_mix(slots, key_in, gate_in, middle, grads, late):
    tokens = key_in.shape[0]
    wide_rows = jax.ShapeDtypeStruct((tokens, 1024), jnp.float32)
    half_rows = jax.ShapeDtypeStruct((tokens, 1024), jnp.bfloat16)
    whole = pl.BlockSpec(memory_space=pltpu.VMEM)
    far = pl.BlockSpec(memory_space=pltpu.HBM)
    return pl.pallas_call(
        channel_kernel,
        out_shape=(
            half_rows,
            half_rows,
            half_rows,
            wide_rows,
            wide_rows,
            jax.ShapeDtypeStruct((4, tokens, 512), jnp.bfloat16),
            jax.ShapeDtypeStruct((4, tokens, 512), jnp.bfloat16),
            jax.ShapeDtypeStruct((tokens, 4096), jnp.bfloat16),
        ),
        in_specs=[pl.BlockSpec(memory_space=pltpu.SMEM), whole, whole, whole, whole, far],
        out_specs=(whole,) * 5 + (far,) * 3,
        scratch_shapes=[
            pltpu.VMEM((4, 32, 32, 1024), jnp.bfloat16),
            pltpu.VMEM((32, 128, 1024), jnp.bfloat16),
            pltpu.VMEM((32, 32, 1024), jnp.bfloat16),
            pltpu.VMEM((4, tokens, 1024), jnp.float32),
            pltpu.VMEM((4, tokens, 1024), jnp.bfloat16),
            pltpu.VMEM((4, tokens, 1024), jnp.bfloat16),
            pltpu.VMEM((tokens, 1024), jnp.float32),
            pltpu.SemaphoreType.DMA((9,)),
            pltpu.SemaphoreType.DMA((4, 8)),
            pltpu.SemaphoreType.DMA((4,)),
        ],
        compiler_params=pltpu.CompilerParams(vmem_limit_bytes=54 * 1024 * 1024),
        cost_estimate=pl.CostEstimate(
            flops=2 * tokens * 1024 * 1024 * 18, transcendentals=0, bytes_accessed=40 * 1024 * 1024
        ),
    )(slots, key_in, gate_in, middle, grads, late)


def owner_slots(flat):
    other = jnp.arange(32)
    apart = other ^ flat
    dz = ((other >> 1) - (flat >> 1)) & 3
    return ((apart & 1) * 16 + ((apart >> 4) & 1) * 8 + ((apart >> 3) & 1) * 4 + dz).astype(jnp.int32)


def dot_tn(left, right):
    return lax.dot_general(
        left, right, (((0,), (0,)), ((), ())), preferred_element_type=jnp.float32
    )


def chip_rows(own_in, own_grads, other_in, other_grads):
    return (dot_tn(own_in, own_grads) + dot_tn(other_in, other_grads)).astype(jnp.bfloat16)


def value_part_kernel(own_ref, other_ref, grad_ref, other_grad_ref, near, side_x, side_y, far_a, far_b):
    quarter = pl.program_id(0)
    part = chip_rows(own_ref[0], grad_ref[...], other_ref[0], other_grad_ref[...])
    part = part.reshape((4, part.shape[0] // 4, 1024))

    @pl.when(quarter == 0)
    def _():
        near[...] = part

    @pl.when(quarter == 1)
    def _():
        side_x[...] = part

    @pl.when(quarter == 2)
    def _():
        side_y[...] = part

    @pl.when(quarter == 3)
    def _():
        far_a[...] = part[:2]
        far_b[...] = part[2:]


def store_quarters(part, outs):
    near, side_x, side_y, far_a, far_b = outs
    quarters = part.reshape(4, 4, 32, 1024)
    near[...] = quarters[0]
    side_x[...] = quarters[1]
    side_y[...] = quarters[2]
    far_a[...] = quarters[3, :2]
    far_b[...] = quarters[3, 2:]


def key_part_kernel(key_ref, other_key_ref, gate_ref, other_gate_ref, *refs):
    pre_ref, other_pre_ref, gate_grad_ref, other_gate_grad_ref = refs[:4]
    step = pl.program_id(0)

    @pl.when(step < 4)
    def _():
        store_quarters(
            chip_rows(key_ref[...], pre_ref[...], other_key_ref[...], other_pre_ref[...]), refs[4:]
        )

    @pl.when(step == 4)
    def _():
        store_quarters(
            chip_rows(
                gate_ref[...], gate_grad_ref[...], other_gate_ref[...], other_gate_grad_ref[...]
            ),
            refs[4:],
        )


def time_part_kernel(own_ref, other_ref, grad_ref, other_grad_ref, *refs):
    branch_ref, other_branch_ref = refs[:2]
    step = pl.program_id(0)

    @pl.when(step < 3)
    def _():
        store_quarters(
            chip_rows(own_ref[...], grad_ref[...], other_ref[...], other_grad_ref[...]), refs[2:]
        )

    @pl.when(step == 3)
    def _():
        store_quarters(
            chip_rows(own_ref[...], branch_ref[...], other_ref[...], other_branch_ref[...]), refs[2:]
        )


def in_three(array):
    high = array.astype(jnp.bfloat16)
    rest = array - high.astype(jnp.float32)
    middle = rest.astype(jnp.bfloat16)
    return high, middle, (rest - middle.astype(jnp.float32)).astype(jnp.bfloat16)


def time_mix_kernel(
    branch_ref,
    weight_ref,
    key_ref,
    value_ref,
    gates_ref,
    mask_ref,
    carry_ref,
    num_ref,
    den_ref,
    decay_ref,
    bonus_ref,
    gate_grad_ref,
    key_grad_ref,
    value_grad_ref,
    num_grad_ref,
    den_grad_ref,
    decay_grad_ref,
    bonus_grad_ref,
):
    length = mask_ref.shape[1]
    decay = decay_ref[...]
    bonus = jnp.exp(bonus_ref[...])
    place = lax.broadcasted_iota(jnp.int32, (length, 1), 0).astype(jnp.float32)
    grow = jnp.exp(place * decay)
    shrink = jnp.exp((1.0 - place) * decay)
    for row in range(mask_ref.shape[0]):
        rows = pl.ds(row * length, length)
        mask = mask_ref[row]
        gated_grad = dot_nt(branch_ref[rows, :], weight_ref[...])
        gates = gates_ref[rows, :]
        power = jnp.exp(key_ref[rows, :])
        value = value_ref[rows, :]
        product = power * value
        fade = carry_ref[row] * jnp.exp(-place * decay)
        num_in, den_in = num_ref[row], den_ref[row]
        num_sum = sum(
            jnp.dot(mask, part, preferred_element_type=jnp.float32)
            for part in in_three(product * grow)
        )
        den_sum = sum(
            jnp.dot(mask, part, preferred_element_type=jnp.float32)
            for part in in_three(power * grow)
        )
        numer = fade * num_in + shrink * num_sum + bonus * product
        denom = fade * den_in + shrink * den_sum + bonus * power
        mixed = numer / denom
        gate_grad_ref[rows, :] = (gated_grad * mixed * gates * (1.0 - gates)).astype(jnp.bfloat16)
        num_grad = gated_grad * gates / denom
        den_grad = -num_grad * mixed
        num_back, den_back = shrink * num_grad, shrink * den_grad
        num_past = grow * sum(dot_tn(mask, part) for part in in_three(num_back))
        den_past = grow * sum(dot_tn(mask, part) for part in in_three(den_back))
        product_grad = bonus * num_grad + num_past
        key_grad_ref[rows, :] = power * (value * product_grad + bonus * den_grad + den_past)
        value_grad_ref[rows, :] = power * product_grad
        num_grad_ref[row] = jnp.sum(fade * num_grad, axis=0, keepdims=True)
        den_grad_ref[row] = jnp.sum(fade * den_grad, axis=0, keepdims=True)
        bonus_grad_ref[row] = jnp.sum(
            bonus * (product * num_grad + power * den_grad), axis=0, keepdims=True
        )
        decay_grad_ref[row] = jnp.sum(
            place * (product * num_past + power * den_past)
            + (1.0 - place) * (num_back * num_sum + den_back * den_sum)
            - place * fade * (num_grad * num_in + den_grad * den_in),
            axis=0,
            keepdims=True,
        )


def time_mix_back(branch, weight, key, value, gates, mask, carry, num, den, decay, bonus):
    tokens = branch.shape[0]
    rows, length = mask.shape[:2]
    tile = 256
    wide_block = pl.BlockSpec((tokens, tile), lambda i: (0, i))
    state = pl.BlockSpec((rows, 1, tile), lambda i: (0, 0, i))
    vector = pl.BlockSpec((1, tile), lambda i: (0, i))
    states = jax.ShapeDtypeStruct((rows, 1, 1024), jnp.float32)
    wide_rows = jax.ShapeDtypeStruct((tokens, 1024), jnp.float32)
    return pl.pallas_call(
        time_mix_kernel,
        grid=(1024 // tile,),
        out_shape=(
            jax.ShapeDtypeStruct((tokens, 1024), jnp.bfloat16),
            wide_rows,
            wide_rows,
            states,
            states,
            states,
            states,
        ),
        in_specs=[
            pl.BlockSpec((tokens, 1024), lambda i: (0, 0)),
            pl.BlockSpec((tile, 1024), lambda i: (i, 0)),
            wide_block,
            wide_block,
            wide_block,
            pl.BlockSpec((rows, length, length), lambda i: (0, 0, 0)),
            pl.BlockSpec((rows, length, 1), lambda i: (0, 0, 0)),
            state,
            state,
            vector,
            vector,
        ],
        out_specs=(wide_block, wide_block, wide_block, state, state, state, state),
        compiler_params=pltpu.CompilerParams(vmem_limit_bytes=48 * 1024 * 1024),
        cost_estimate=pl.CostEstimate(flops=1, transcendentals=0, bytes_accessed=1),
    )(branch, weight, key, value, gates, mask, carry, num, den, decay, bonus)


def quarters_call(kernel, steps, rows, in_specs, by_quarter, arguments):
    if by_quarter:
        outs = [pl.BlockSpec((n, rows, 1024), lambda i: (0, 0, 0)) for n in (4, 4, 4, 2, 2)]
    else:
        outs = [pl.BlockSpec((n, 32, 1024), lambda i: (0, i, 0)) for n in (4, 4, 4, 2, 2)]
    return pl.pallas_call(
        kernel,
        grid=(steps,),
        out_shape=tuple(
            jax.ShapeDtypeStruct((n, rows, 1024), jnp.bfloat16) for n in (4, 4, 4, 2, 2)
        ),
        in_specs=in_specs,
        out_specs=tuple(outs),
        compiler_params=pltpu.CompilerParams(vmem_limit_bytes=48 * 1024 * 1024),
        cost_estimate=pl.CostEstimate(flops=1, transcendentals=0, bytes_accessed=1),
    )(*arguments)


def value_part(own_hidden, other_hidden, grads, other_grads):
    tokens = grads.shape[0]
    whole = pl.BlockSpec((tokens, 1024), lambda i: (0, 0))
    block = pl.BlockSpec((1, tokens, 512), lambda i: (i, 0, 0))
    return quarters_call(
        value_part_kernel,
        4,
        128,
        [block, block, whole, whole],
        True,
        (own_hidden, other_hidden, grads, other_grads),
    )


def key_part(key, other_key, gate, other_gate, pre, other_pre, gate_grad, other_gate_grad):
    tokens = pre.shape[0]
    half = pl.BlockSpec((tokens, 512), lambda i: (0, 0))
    whole = pl.BlockSpec((tokens, 1024), lambda i: (0, 0))
    block = pl.BlockSpec((tokens, 1024), lambda i: (0, jnp.minimum(i, 3)))
    return quarters_call(
        key_part_kernel,
        5,
        160,
        [half, half, half, half, block, block, whole, whole],
        False,
        (key, other_key, gate, other_gate, pre, other_pre, gate_grad, other_gate_grad),
    )


def time_part(own, other, grads, other_grads, branch, other_branch):
    tokens = grads.shape[0]
    half = pl.BlockSpec((tokens, 512), lambda i: (0, i))
    whole = pl.BlockSpec((tokens, 1024), lambda i: (0, 0))
    block = pl.BlockSpec((tokens, 1024), lambda i: (0, jnp.minimum(i, 2)))
    return quarters_call(
        time_part_kernel,
        4,
        128,
        [half, half, block, block, whole, whole],
        False,
        (own, other, grads, other_grads, branch, other_branch),
    )


def ordered_halves(rows_in, flat):
    width = rows_in.shape[-1]
    rows_in = rows_in.reshape(-1, width)
    ordered = jnp.dot(rows_in, choice(flat, width), preferred_element_type=jnp.bfloat16)
    return ordered[:, : width // 2], ordered[:, width // 2 :]


def sent_together(arrays):
    got = sent(jnp.concatenate(arrays, axis=1) if len(arrays) > 1 else arrays[0], FLIP_C)
    ends = [sum(a.shape[1] for a in arrays[: i + 1]) for i in range(len(arrays))]
    return [got[:, end - a.shape[1] : end] for a, end in zip(arrays, ends)]


def wide(array):
    return array.astype(jnp.float32)


def narrow(array):
    return array.astype(jnp.bfloat16)


def send_corner(parts):
    return sent(parts[3], FLIP_X), sent(parts[4], FLIP_Y)


def add_corner(parts, add_a, add_b):
    to_y = lax.dynamic_update_slice(parts[2], narrow(wide(parts[2][:2]) + wide(add_a)), (0, 0, 0))
    to_x = lax.dynamic_update_slice(parts[1], narrow(wide(parts[1][2:]) + wide(add_b)), (2, 0, 0))
    return to_y, to_x


def send_sides(to_y, to_x):
    return sent(to_y, FLIP_Y), sent(to_x, FLIP_X)


def add_sides(parts, from_y, from_x):
    column = wide(parts[0]) + wide(from_y) + wide(from_x)
    return column[0], [narrow(column[d]) for d in (1, 2, 3)]


def send_column(outgoing):
    return [sent(part, turn_z(d)) for d, part in zip((1, 2, 3), outgoing)]


def add_all(first, others):
    for other in others:
        first = first + wide(other)
    return first


def sum_plane(total):
    for pairs in (FLIP_C, FLIP_X, FLIP_Y):
        total = total + sent(total, pairs)
    return total


def sum_column(total, flat):
    total = total + sum(sent(total, turn_z(d)) for d in (1, 2, 3))
    count = total.shape[1] // 32
    return lax.dynamic_slice_in_dim(total, flat * count, count, 1)


def shifted(shard, axis, by):
    length = lax.axis_size(axis)
    pairs = [(i, i + by) for i in range(length) if 0 <= i + by < length]
    return lax.ppermute(shard, axis, pairs)


def carried_in(part, starts_in, decay_vec, length, reverse, between=None):
    count = lax.axis_size("seq")
    place = lax.axis_index("seq")
    clear = 1.0 - starts_in.astype(jnp.float32)
    block_fade = jnp.exp(-length * decay_vec)

    def clear_of(block):
        return lax.dynamic_index_in_dim(clear, jnp.clip(block, 0, count - 1), 1, True)

    if count == 8:
        chip, core = place >> 1, place & 1
        other = sent(part, FLIP_C)
        is_far = (core == 1) == (not reverse)
        near = jnp.where(is_far, other, part)
        last = jnp.where(is_far, part, other)
        first_block, second_block = chip * 2 + (1 if reverse else 0), chip * 2 + (0 if reverse else 1)
        joined = clear_of(second_block) * block_fade * near + last
        if between is not None:
            joined = between(joined)
        step = -1 if reverse else 1
        entering = jnp.zeros_like(part)
        open_way = jnp.ones((part.shape[1], 1), jnp.float32)
        for d in (1, 2, 3):
            beside = chip - step * d
            live = ((beside >= 0) & (beside < 4)).astype(jnp.float32)
            fade = live * open_way * jnp.exp(-float(2 * (d - 1) * length) * decay_vec)
            entering = entering + fade * sent(joined, turn_z(step * d))
            open_way = open_way * clear_of(2 * beside) * clear_of(2 * beside + 1)
        return jnp.where(is_far, clear_of(first_block) * block_fade * entering + near, entering)
    gathered = lax.all_gather(part, "seq")

    def one(lap, state):
        source = count - 1 - lap if reverse else lap
        return clear_of(source) * block_fade * state + lax.dynamic_index_in_dim(gathered, source, 0, False)

    ahead = count - 1 - place if reverse else place
    return lax.fori_loop(0, ahead, one, jnp.zeros_like(part))


def norm_forward(values, gain_vec, bias_vec):
    centre = values - jnp.mean(values, axis=-1, keepdims=True)
    inv_std = lax.rsqrt(jnp.mean(centre * centre, axis=-1, keepdims=True) + eps)
    normed = centre * inv_std
    return (normed * gain_vec + bias_vec, normed, inv_std)


def norm_backward(grads, normed, inv_std, gain_vec):
    scaled = grads * gain_vec
    inner = (
        scaled
        - jnp.mean(scaled, axis=-1, keepdims=True)
        - normed * jnp.mean(scaled * normed, axis=-1, keepdims=True)
    )
    return (inv_std * inner, jnp.sum(grads * normed, axis=(0, 1)), jnp.sum(grads, axis=(0, 1)))


def project(rows_in, weight):
    return jnp.einsum("rtd,de->rte", rows_in, weight, preferred_element_type=jnp.float32)


def project_back(grads, weight):
    return jnp.einsum("rte,de->rtd", grads, weight, preferred_element_type=jnp.float32)


def weight_grad(rows_in, grads):
    total = jnp.einsum("rtd,rte->de", rows_in, grads, preferred_element_type=jnp.float32)
    return lax.psum_scatter(total, BOTH, scatter_dimension=0, tiled=True)


def weighted_value_local(
    key_row_block,
    value_row_block,
    feature_forgetting_rate,
    present_reward,
    state_numerator,
    state_denominator,
    document_segments,
):
    length = key_row_block.shape[1]
    width = key_row_block.shape[2]
    order_idx = jnp.arange(length)
    step_pos = order_idx.astype(jnp.float32)[:, None]
    powered_lookups = jnp.exp(key_row_block)
    grow_exp = jnp.exp(step_pos * feature_forgetting_rate)
    shrink = jnp.exp((1.0 - step_pos) * feature_forgetting_rate)
    pair_mask = (
        (order_idx[None, :] < order_idx[:, None])[None]
        & (document_segments[:, None, :] == document_segments[:, :, None])
    ).astype(jnp.float32)
    weighted = jnp.concatenate(
        [powered_lookups * value_row_block, powered_lookups], axis=2
    ) * jnp.concatenate([grow_exp, grow_exp], axis=1)
    past_sums = jnp.einsum(
        "rti,rie->rte", pair_mask, weighted, precision=highest
    ) * jnp.concatenate([shrink, shrink], axis=1)
    carry_fade = (document_segments == 0).astype(jnp.float32)[:, :, None] * jnp.exp(
        -step_pos * feature_forgetting_rate
    )
    present_token_contribution = jnp.exp(present_reward) * powered_lookups
    numer = (
        carry_fade * state_numerator[:, None, :]
        + past_sums[:, :, :width]
        + present_token_contribution * value_row_block
    )
    denom = (
        carry_fade * state_denominator[:, None, :]
        + past_sums[:, :, width:]
        + present_token_contribution
    )
    return numer / denom


def tail_terms(key_row_block, value_row_block, feature_forgetting_rate, document_segments):
    length = key_row_block.shape[1]
    step_pos = jnp.arange(length).astype(jnp.float32)[:, None]
    powered_lookups = jnp.exp(key_row_block)
    tail_fade = (document_segments == document_segments[:, -1:]).astype(jnp.float32)[
        :, :, None
    ] * jnp.exp((step_pos - (length - 1)) * feature_forgetting_rate)
    return (
        jnp.sum(tail_fade * powered_lookups * value_row_block, axis=1),
        jnp.sum(tail_fade * powered_lookups, axis=1),
        tail_fade,
        powered_lookups,
    )


def shards(
    tuned,
    incoming_activations,
    sequence_extents,
    upstream_sensitivity,
    initial_normalizer_scale,
    initial_normalizer_offset,
    temporal_lookup_fraction,
    temporal_content_fraction,
    temporal_receptance_fraction,
    feature_forgetting_rate,
    present_reward,
    temporal_lookup_projection,
    temporal_content_projection,
    temporal_receptance_projection,
    temporal_result_projection,
    later_normalizer_scale,
    later_normalizer_offset,
    feature_lookup_fraction,
    feature_receptance_fraction,
    feature_lookup_projection,
    feature_content_projection,
    feature_receptance_projection,
):
    flat = lax.axis_index("batch") * lax.axis_size("seq") + lax.axis_index("seq")
    vectors = jnp.stack(
        [
            initial_normalizer_scale,
            initial_normalizer_offset,
            temporal_lookup_fraction,
            temporal_content_fraction,
            temporal_receptance_fraction,
            feature_forgetting_rate,
            present_reward,
            later_normalizer_scale,
            later_normalizer_offset,
            feature_lookup_fraction,
            feature_receptance_fraction,
        ]
    )
    if tuned:
        order = long_slots(flat)
        late = lax.all_gather(
            pack_late(
                feature_lookup_projection,
                feature_content_projection,
                feature_receptance_projection,
            ),
            BOTH,
        )
        spread = jnp.tile(jnp.pad(vectors, ((0, 5), (0, 0))), (1, 32))
        packed = jnp.where(jnp.arange(1024) // 32 == flat, spread, jnp.zeros_like(spread))
        part = stacked(
            [
                temporal_lookup_projection,
                temporal_content_projection,
                temporal_receptance_projection,
                temporal_result_projection,
                packed,
            ]
        )
        column = jnp.stack([part] + around(part))
        from_x, from_y = sent(column, FLIP_X), sent(column, FLIP_Y)
        early = both_cores([column, from_x, from_y, *send_far(from_x, from_y)])
        vectors = jnp.sum(
            assemble(early, order, 128, 16, 1).reshape(32, 16, 1024).astype(jnp.float32), axis=0
        )
        lookup_weight = assemble(early, order, 0, 32, 1)
        content_weight = assemble(early, order, 32, 32, 1)
        receptance_weight = assemble(early, order, 64, 32, 1)
        result_weight = assemble(early, order, 96, 32, 1)
    else:
        (
            lookup_weight,
            content_weight,
            receptance_weight,
            result_weight,
            ffn_key_weight,
            ffn_gate_weight,
            ffn_value_weight,
        ) = [
            lax.all_gather(part, BOTH, axis=0, tiled=True)
            for part in (
                temporal_lookup_projection,
                temporal_content_projection,
                temporal_receptance_projection,
                temporal_result_projection,
                feature_lookup_projection,
                feature_receptance_projection,
                feature_content_projection,
            )
        ]
        vectors = lax.all_gather(vectors, BOTH, axis=1, tiled=True).astype(jnp.float32)
    (
        opening_standardize_scale,
        opening_standardize_offset,
        temporal_lookup_mixture,
        temporal_content_mixture,
        temporal_receptance_mixture,
        decay_vec,
        reward_array,
        closing_standardize_scale,
        closing_standardize_offset,
        feature_lookup_mixture,
        feature_receptance_mixture,
    ) = tuple(vectors[i] for i in range(11))
    rows, length, width = incoming_activations.shape
    starts = jnp.cumsum(sequence_extents, axis=1) - sequence_extents
    places = lax.axis_index("seq") * length + jnp.arange(length, dtype=jnp.int32)
    resets = jnp.any(
        (starts[:, None, :] == places[None, :, None]) & (sequence_extents[:, None, :] > 0), axis=2
    )
    document_segments = jnp.cumsum(resets.astype(jnp.int32), axis=1)
    keep_mask = 1.0 - resets.astype(jnp.float32)[:, :, None]
    clear_flag = (document_segments[:, -1:] == 0).astype(jnp.float32)
    starts_in = jnp.any(
        (starts[:, None, :] // length == jnp.arange(lax.axis_size("seq"))[None, :, None])
        & (sequence_extents[:, None, :] > 0),
        axis=2,
    )

    inputs = incoming_activations.astype(jnp.float32)
    left_rows = shifted(incoming_activations[:, length - 1 :, :], "seq", 1)
    normed_one, unit_one, inv_one = norm_forward(
        inputs, opening_standardize_scale, opening_standardize_offset
    )
    left_normed, _, _ = norm_forward(
        left_rows.astype(jnp.float32), opening_standardize_scale, opening_standardize_offset
    )
    before_one = jnp.concatenate([left_normed, normed_one[:, :-1, :]], axis=1) * keep_mask
    key_in = (
        normed_one * temporal_lookup_mixture + before_one * (1.0 - temporal_lookup_mixture)
    ).astype(jnp.bfloat16)
    value_in = (
        normed_one * temporal_content_mixture + before_one * (1.0 - temporal_content_mixture)
    ).astype(jnp.bfloat16)
    gate_in = (
        normed_one * temporal_receptance_mixture + before_one * (1.0 - temporal_receptance_mixture)
    ).astype(jnp.bfloat16)
    key_row_block = project(key_in, lookup_weight)
    value_row_block = project(value_in, content_weight)
    gates = jax.nn.sigmoid(project(gate_in, receptance_weight))
    tail_num, tail_den, tail_fade, powered_lookups = tail_terms(
        key_row_block, value_row_block, decay_vec, document_segments
    )
    state_numerator, state_denominator = carried_in(
        jnp.stack([tail_num, tail_den]), starts_in, decay_vec, length, False
    )
    mixed, weighted_value_backward = jax.vjp(
        partial(weighted_value_local, document_segments=document_segments),
        key_row_block,
        value_row_block,
        decay_vec,
        reward_array,
        state_numerator,
        state_denominator,
    )
    gated = (gates * mixed).astype(jnp.bfloat16)
    if tuned:
        own_key, far_key = ordered_halves(key_in, flat)
        own_value, far_value = ordered_halves(value_in, flat)
        own_gate, far_gate = ordered_halves(gate_in, flat)
        own_gated, far_gated = ordered_halves(gated, flat)
        other_time = sent(
            jnp.concatenate([far_key, far_value, far_gate, far_gated], axis=1), FLIP_C
        )
        own_time = jnp.concatenate([own_key, own_value, own_gate, own_gated], axis=1)
    middle = inputs + project(gated, result_weight)
    normed_two, unit_two, inv_two = norm_forward(
        middle, closing_standardize_scale, closing_standardize_offset
    )
    before_rows = shifted(normed_two[:, length - 1 :, :], "seq", 1)
    before_two = jnp.concatenate([before_rows, normed_two[:, :-1, :]], axis=1) * keep_mask
    ffn_key_in = (
        normed_two * feature_lookup_mixture + before_two * (1.0 - feature_lookup_mixture)
    ).astype(jnp.bfloat16)
    ffn_gate_in = (
        normed_two * feature_receptance_mixture + before_two * (1.0 - feature_receptance_mixture)
    ).astype(jnp.bfloat16)
    grad_out = upstream_sensitivity.astype(jnp.float32)
    if tuned:
        own_ffn_key, far_ffn_key = ordered_halves(ffn_key_in, flat)
        own_ffn_gate, far_ffn_gate = ordered_halves(ffn_gate_in, flat)
        other_ffn_key, other_ffn_gate = sent_together([far_ffn_key, far_ffn_gate])
        output, value_grad, ffn_gate_grad, key_two_grad, gate_two_grad, *kept = channel_mix(
            owner_slots(flat),
            ffn_key_in.reshape(-1, width),
            ffn_gate_in.reshape(-1, width),
            middle.reshape(-1, width),
            upstream_sensitivity.reshape(-1, width),
            late,
        )
        output, key_two_grad, gate_two_grad = (
            a.reshape(rows, length, width) for a in (output, key_two_grad, gate_two_grad)
        )
        own_hidden, far_hidden, pre_grad = kept
        other_value_grad = sent(value_grad, FLIP_C)
        other_hidden = sent(far_hidden, FLIP_C)
        other_gate_grad = sent(ffn_gate_grad, FLIP_C)
        other_pre_grad = sent(pre_grad, FLIP_C)
        value_parts = value_part(own_hidden, other_hidden, value_grad, other_value_grad)
        value_corner = send_corner(value_parts)
        key_parts = key_part(
            own_ffn_key,
            other_ffn_key,
            own_ffn_gate,
            other_ffn_gate,
            pre_grad,
            other_pre_grad,
            ffn_gate_grad,
            other_gate_grad,
        )
        value_sides = add_corner(value_parts, *all_tied(value_corner, key_parts[4]))
        value_from = send_sides(*value_sides)
    else:
        hidden_pre = project(ffn_key_in, ffn_key_weight)
        hidden = jnp.square(jax.nn.relu(hidden_pre)).astype(jnp.bfloat16)
        ffn_value = project(hidden, ffn_value_weight)
        ffn_gates = jax.nn.sigmoid(project(ffn_gate_in, ffn_gate_weight))
        output = (middle + ffn_gates * ffn_value).astype(jnp.bfloat16)
        value_grad = (grad_out * ffn_gates).astype(jnp.bfloat16)
        ffn_gate_grad = (grad_out * ffn_value * ffn_gates * (1.0 - ffn_gates)).astype(jnp.bfloat16)
        hidden_grad = project_back(value_grad, ffn_value_weight)
        pre_grad = (hidden_grad * 2.0 * jax.nn.relu(hidden_pre)).astype(jnp.bfloat16)
        grad_ffn_value = weight_grad(hidden, value_grad)
        grad_ffn_key = weight_grad(ffn_key_in, pre_grad)
        grad_ffn_gate = weight_grad(ffn_gate_in, ffn_gate_grad)
        key_two_grad = project_back(pre_grad, ffn_key_weight)
        gate_two_grad = project_back(ffn_gate_grad, ffn_gate_weight)
    spread_two = normed_two - before_two
    grad_ffn_mix_key = jnp.sum(key_two_grad * spread_two, axis=(0, 1))
    grad_ffn_mix_gate = jnp.sum(gate_two_grad * spread_two, axis=(0, 1))
    normed_two_grad = (
        key_two_grad * feature_lookup_mixture + gate_two_grad * feature_receptance_mixture
    )
    before_two_grad = (
        key_two_grad * (1.0 - feature_lookup_mixture)
        + gate_two_grad * (1.0 - feature_receptance_mixture)
    ) * keep_mask
    from_right = shifted(before_two_grad[:, :1, :], "seq", -1)
    normed_two_grad = normed_two_grad + jnp.concatenate(
        [before_two_grad[:, 1:, :], from_right], axis=1
    )
    middle_norm_grad, grad_gain_two, grad_bias_two = norm_backward(
        normed_two_grad, unit_two, inv_two, closing_standardize_scale
    )
    middle_grad = grad_out + middle_norm_grad
    branch_grad = middle_grad.astype(jnp.bfloat16)
    if tuned:
        flat_branch_grad = branch_grad.reshape(-1, width)
        other_branch_grad = sent(flat_branch_grad, FLIP_C)
        key_corner = send_corner(key_parts)
    else:
        grad_output = weight_grad(gated, branch_grad)
    if tuned:
        order_idx = jnp.arange(length)
        pair_mask = (
            (order_idx[None, :] < order_idx[:, None])[None]
            & (document_segments[:, None, :] == document_segments[:, :, None])
        ).astype(jnp.bfloat16)
        (
            gate_pre_grad,
            key_gradient,
            value_gradient,
            numerator_gradient,
            denominator_gradient,
            decay_gradient,
            reward_derivative,
        ) = time_mix_back(
            branch_grad.reshape(-1, width),
            result_weight,
            key_row_block.reshape(-1, width),
            value_row_block.reshape(-1, width),
            gates.reshape(-1, width),
            pair_mask,
            (document_segments == 0).astype(jnp.float32)[:, :, None],
            state_numerator[:, None, :],
            state_denominator[:, None, :],
            tied(decay_vec[None, :], value_sides[0], value_sides[1][2:]),
            reward_array[None, :],
        )
        gate_pre_grad, key_gradient, value_gradient = (
            a.reshape(rows, length, width) for a in (gate_pre_grad, key_gradient, value_gradient)
        )
        numerator_gradient = numerator_gradient[:, 0, :]
        denominator_gradient = denominator_gradient[:, 0, :]
        decay_gradient = jnp.sum(decay_gradient[:, 0, :], axis=0)
        reward_derivative = jnp.sum(reward_derivative[:, 0, :], axis=0)
    else:
        gated_grad = project_back(branch_grad, result_weight)
        gate_pre_grad = (gated_grad * mixed * gates * (1.0 - gates)).astype(jnp.bfloat16)
        blended_gradient = gated_grad * gates
        (
            key_gradient,
            value_gradient,
            decay_gradient,
            reward_derivative,
            numerator_gradient,
            denominator_gradient,
        ) = weighted_value_backward(blended_gradient)
    state_gradient = jnp.stack([numerator_gradient, denominator_gradient])
    if tuned:
        key_sides = add_corner(key_parts, *all_tied(key_corner, state_gradient))
        key_from = send_sides(*key_sides)
        state_gradient = tied(state_gradient, key_sides[0], key_sides[1][2:])
    summed = []

    def beside_sides(joined):
        summed.extend(
            add_sides(value_parts, *[tied(a, joined, other_time) for a in value_from])
        )
        return tied(joined, summed[1][0])

    num_next, den_next = carried_in(
        state_gradient, starts_in, decay_vec, length, True, beside_sides if tuned else None
    )
    if tuned:
        value_first, value_outgoing = summed
    num_tail = tail_fade * num_next[:, None, :]
    den_tail = tail_fade * den_next[:, None, :]
    tail_grad = powered_lookups * (value_row_block * num_tail + den_tail)
    key_gradient = key_gradient + tail_grad
    value_gradient = value_gradient + powered_lookups * num_tail
    offsets = (jnp.arange(length).astype(jnp.float32) - (length - 1))[:, None]
    block_fade = clear_flag * jnp.exp(-length * decay_vec)
    decay_gradient = decay_gradient + jnp.sum(offsets * tail_grad, axis=(0, 1))
    decay_gradient = decay_gradient - length * jnp.sum(
        block_fade * (state_numerator * num_next + state_denominator * den_next), axis=0
    )
    key_grad16 = key_gradient.astype(jnp.bfloat16)
    val_grad16 = value_gradient.astype(jnp.bfloat16)
    if tuned:
        flat_grads = jnp.concatenate(
            [g.reshape(-1, width) for g in (key_grad16, val_grad16, gate_pre_grad)], axis=1
        )
        other_grads = sent(flat_grads, FLIP_C)
        time_parts = time_part(
            own_time, other_time, flat_grads, other_grads, flat_branch_grad, other_branch_grad
        )
        value_got = all_tied(send_column(all_tied(value_outgoing, num_next)), time_parts[4])
        time_corner = send_corner(time_parts)
    else:
        grad_key = weight_grad(key_in, key_grad16)
        grad_value = weight_grad(value_in, val_grad16)
        grad_gate = weight_grad(gate_in, gate_pre_grad)
    if tuned:
        key_grad16 = tied(key_grad16, time_parts[4])
    key_in_grad = project_back(key_grad16, lookup_weight)
    value_in_grad = project_back(val_grad16, content_weight)
    gate_in_grad = project_back(gate_pre_grad, receptance_weight)
    spread_one = normed_one - before_one
    grad_mix_key = jnp.sum(key_in_grad * spread_one, axis=(0, 1))
    grad_mix_value = jnp.sum(value_in_grad * spread_one, axis=(0, 1))
    grad_mix_gate = jnp.sum(gate_in_grad * spread_one, axis=(0, 1))
    normed_one_grad = (
        key_in_grad * temporal_lookup_mixture
        + value_in_grad * temporal_content_mixture
        + gate_in_grad * temporal_receptance_mixture
    )
    before_one_grad = (
        key_in_grad * (1.0 - temporal_lookup_mixture)
        + value_in_grad * (1.0 - temporal_content_mixture)
        + gate_in_grad * (1.0 - temporal_receptance_mixture)
    ) * keep_mask
    if tuned:
        key_first, key_outgoing = add_sides(key_parts, *all_tied(key_from, before_one_grad))
        time_sides = add_corner(time_parts, *all_tied(time_corner, before_one_grad))
        time_from = send_sides(*time_sides)
    from_next = shifted(before_one_grad[:, :1, :], "seq", -1)
    if tuned:
        key_got = send_column(all_tied(key_outgoing, from_next))
        from_next = tied(from_next, time_sides[0], time_sides[1][2:])
    normed_one_grad = normed_one_grad + jnp.concatenate(
        [before_one_grad[:, 1:, :], from_next], axis=1
    )
    input_norm_grad, grad_gain_one, grad_bias_one = norm_backward(
        normed_one_grad, unit_one, inv_one, opening_standardize_scale
    )
    input_grad = middle_grad + input_norm_grad
    vector_grads = jnp.stack(
        [
            grad_gain_one,
            grad_bias_one,
            grad_mix_key,
            grad_mix_value,
            grad_mix_gate,
            decay_gradient,
            reward_derivative,
            grad_gain_two,
            grad_bias_two,
            grad_ffn_mix_key,
            grad_ffn_mix_gate,
        ]
    )
    if tuned:
        time_first, time_outgoing = add_sides(time_parts, *all_tied(time_from, vector_grads))
        key_total = add_all(key_first, all_tied(key_got, vector_grads))
        time_got = send_column(time_outgoing)
        time_total = add_all(time_first, time_got)
        grad_key, grad_value, grad_gate, grad_output = (
            time_total[i : i + 32] for i in (0, 32, 64, 96)
        )
        grad_ffn_value = add_all(value_first, value_got)
        grad_ffn_key = jnp.concatenate([key_total[i : i + 32] for i in (0, 32, 64, 96)], axis=1)
        grad_ffn_gate = key_total[128:]
        vector_grads = sum_column(tied(sum_plane(vector_grads), time_got[0]), flat)
    else:
        vector_grads = lax.psum_scatter(vector_grads, BOTH, scatter_dimension=1, tiled=True)
    return (
        output,
        input_grad,
        vector_grads[0],
        vector_grads[1],
        vector_grads[2],
        vector_grads[3],
        vector_grads[4],
        vector_grads[5],
        vector_grads[6],
        grad_key,
        grad_value,
        grad_gate,
        grad_output,
        vector_grads[7],
        vector_grads[8],
        vector_grads[9],
        vector_grads[10],
        grad_ffn_key,
        grad_ffn_value,
        grad_ffn_gate,
    )


def solution(mesh):
    tuned = tuple(mesh.shape.items()) == (("batch", 4), ("seq", 8))
    return jax.shard_map(
        partial(shards, tuned),
        mesh=mesh,
        in_specs=(
            P("batch", "seq", None),
            P("batch", None),
            P("batch", "seq", None),
            P(("batch", "seq")),
            P(("batch", "seq")),
            P(("batch", "seq")),
            P(("batch", "seq")),
            P(("batch", "seq")),
            P(("batch", "seq")),
            P(("batch", "seq")),
            P(("batch", "seq"), None),
            P(("batch", "seq"), None),
            P(("batch", "seq"), None),
            P(("batch", "seq"), None),
            P(("batch", "seq")),
            P(("batch", "seq")),
            P(("batch", "seq")),
            P(("batch", "seq")),
            P(("batch", "seq"), None),
            P(("batch", "seq"), None),
            P(("batch", "seq"), None),
        ),
        out_specs=(
            P("batch", "seq", None),
            P("batch", "seq", None),
            P(("batch", "seq")),
            P(("batch", "seq")),
            P(("batch", "seq")),
            P(("batch", "seq")),
            P(("batch", "seq")),
            P(("batch", "seq")),
            P(("batch", "seq")),
            P(("batch", "seq"), None),
            P(("batch", "seq"), None),
            P(("batch", "seq"), None),
            P(("batch", "seq"), None),
            P(("batch", "seq")),
            P(("batch", "seq")),
            P(("batch", "seq")),
            P(("batch", "seq")),
            P(("batch", "seq"), None),
            P(("batch", "seq"), None),
            P(("batch", "seq"), None),
        ),
        check_vma=False,
    )
```

```python
from functools import partial

import jax
import jax.numpy as jnp
from jax import lax
from jax.experimental import pallas as pl
from jax.experimental.pallas import tpu as pltpu
from jax.sharding import PartitionSpec as P

eps = 1e-05
highest = lax.Precision.HIGHEST
BOTH = ("batch", "seq")


def moved(rule):
    return [(f, rule(f)) for f in range(32)]


FLIP_X = moved(lambda f: f ^ 8)
FLIP_Y = moved(lambda f: f ^ 16)
FLIP_C = moved(lambda f: f ^ 1)


def turn_z(by):
    return moved(lambda f: (f & 25) | ((((f >> 1) + by) & 3) << 1))


def sent(array, pairs):
    return lax.ppermute(array, BOTH, pairs)


def place_of(flat, dy, dx, dz, dc):
    turned = ((((flat >> 1) & 3) + dz) & 3) * 2
    return ((flat & 25) | turned) ^ (dy * 16 + dx * 8 + dc)


def tied(array, *after):
    zero = jnp.zeros((), jnp.float32)
    for other in after:
        first = other[(0,) * other.ndim].astype(jnp.float32)
        zero = zero + jnp.minimum(jnp.abs(first), 0.0)
    return array + zero.astype(array.dtype)


def all_tied(arrays, after):
    return [tied(array, after) for array in arrays]


def assemble_kernel(owners, start, columns, slots_ref, *refs):
    pieces, out_ref, sems = refs[:-2], refs[-2], refs[-1]
    rows = out_ref.shape[1]
    copies = []
    number = 0
    for piece, count in zip(pieces, owners):
        for k in range(count):
            for q in range(columns):
                copies.append(
                    pltpu.make_async_copy(
                        piece.at[k, pl.ds(start + q * rows, rows), :],
                        out_ref.at[slots_ref[number], :, pl.ds(q * 1024, 1024)],
                        sems.at[number, q],
                    )
                )
            number += 1
    for copy in copies:
        copy.start()
    for copy in copies:
        copy.wait()


def assemble(pieces, slots, start, rows, columns):
    counts = [piece.shape[0] for piece in pieces]
    shape = (32, rows, columns * 1024)
    whole = pl.pallas_call(
        partial(assemble_kernel, counts, start, columns),
        out_shape=jax.ShapeDtypeStruct(shape, pieces[0].dtype),
        in_specs=[pl.BlockSpec(memory_space=pltpu.SMEM)]
        + [pl.BlockSpec(memory_space=pltpu.HBM)] * len(pieces),
        out_specs=pl.BlockSpec(memory_space=pltpu.VMEM),
        scratch_shapes=[pltpu.SemaphoreType.DMA((32, columns))],
        compiler_params=pltpu.CompilerParams(vmem_limit_bytes=24 * 1024 * 1024),
        cost_estimate=pl.CostEstimate(
            flops=0, transcendentals=0, bytes_accessed=2 * 2 * 32 * rows * columns * 1024
        ),
    )(slots, *pieces)
    return whole.reshape(32 * rows, columns * 1024)


def stacked(parts):
    rows = [part[:, q : q + 1024] for part in parts for q in range(0, part.shape[1], 1024)]
    return jnp.concatenate(rows, axis=0) if len(rows) > 1 else rows[0]


def around(part):
    return [sent(part, turn_z(d)) for d in (1, 2, 3)]


def pack_kernel(key_ref, value_ref, gate_ref, out_ref):
    for q in range(4):
        out_ref[q * 32 : q * 32 + 32, :] = key_ref[:, q * 1024 : q * 1024 + 1024]
    out_ref[128:256, :] = value_ref[...]
    out_ref[256:288, :] = gate_ref[...]


def pack_late(key, value, gate):
    whole = pl.BlockSpec(memory_space=pltpu.VMEM)
    return pl.pallas_call(
        pack_kernel,
        out_shape=jax.ShapeDtypeStruct((288, 1024), key.dtype),
        in_specs=[whole] * 3,
        out_specs=whole,
    )(key, value, gate)


def long_slots(flat):
    every = (0, 1, 2, 3)
    steps = [(0, 0, every), (0, 1, every), (1, 0, every), (1, 1, (0, 1)), (1, 1, (2, 3))]
    return jnp.stack(
        [place_of(flat, dy, dx, -dz, dc) for dc in (0, 1) for dy, dx, dzs in steps for dz in dzs]
    ).astype(jnp.int32)


def send_far(from_x, from_y):
    half = from_x.shape[0] // 2
    return sent(from_x[:half], FLIP_Y), sent(from_y[half:], FLIP_X)


def both_cores(pieces):
    return pieces + [sent(piece, FLIP_C) for piece in pieces]


def choice(flat, width):
    index = jnp.arange(width)
    block, within = index // (width // 32), index % (width // 32)
    dc, rest = block >> 4, block & 15
    dy, dx, dz = rest >> 3, (rest >> 2) & 1, rest & 3
    wanted = place_of(flat, dy, dx, dz, dc) * (width // 32) + within
    return (jnp.arange(width)[:, None] == wanted[None, :]).astype(jnp.bfloat16)


def dot_nt(left, right):
    return lax.dot_general(
        left, right, (((1,), (1,)), ((), ())), preferred_element_type=jnp.float32
    )


def channel_kernel(slots_ref, *refs):
    key_in_ref, gate_in_ref, middle_ref, grad_ref, late_ref = refs[:5]
    refs = refs[5:]
    out_ref, value_grad_ref, gate_grad_ref, key_back_ref, gate_back_ref = refs[:5]
    hidden_ref, far_hidden_ref, pre_grad_ref, key_w, value_w, gate_w = refs[5:11]
    relu_s, hidden_s, pre_s, total_s, in_sems, hidden_sems, pre_sems = refs[11:]

    def key_copy(q):
        return pltpu.make_async_copy(
            late_ref.at[:, pl.ds(q * 32, 32), :], key_w.at[q], in_sems.at[q]
        )

    def value_copy(q):
        return pltpu.make_async_copy(
            late_ref.at[pl.ds(q * 8, 8), pl.ds(128, 128), :],
            value_w.at[pl.ds(q * 8, 8)],
            in_sems.at[4 + q],
        )

    gate_copy = pltpu.make_async_copy(
        late_ref.at[:, pl.ds(256, 32), :], gate_w, in_sems.at[8]
    )
    for q in range(4):
        key_copy(q).start()
        value_copy(q).start()
    gate_copy.start()

    def hidden_copy(q, k, target):
        return pltpu.make_async_copy(
            hidden_s.at[q, :, pl.ds(k * 128, 128)], target, hidden_sems.at[q, k]
        )

    def hidden_start(q, k):
        slot = slots_ref[q * 8 + k]
        columns = pl.ds(pl.multiple_of((slot & 3) * 128, 128), 128)

        @pl.when(slot < 16)
        def _():
            hidden_copy(q, k, hidden_ref.at[slot >> 2, :, columns]).start()

        @pl.when(slot >= 16)
        def _():
            hidden_copy(q, k, far_hidden_ref.at[(slot >> 2) - 4, :, columns]).start()

    def pre_copy(q):
        return pltpu.make_async_copy(
            pre_s.at[q], pre_grad_ref.at[:, pl.ds(pl.multiple_of(q * 1024, 1024), 1024)], pre_sems.at[q]
        )

    def forward(q, _):
        key_copy(q).wait()
        for half in range(1):
            rows = pl.ds(half * 512, 512)
            relu_s[q, rows, :] = jnp.maximum(
                jnp.dot(
                    key_in_ref[rows, :],
                    key_w[q].reshape(1024, 1024),
                    preferred_element_type=jnp.float32,
                ),
                0.0,
            )
            hidden_s[q, rows, :] = (relu_s[q, rows, :] * relu_s[q, rows, :]).astype(jnp.bfloat16)
        for k in range(8):
            hidden_start(q, k)
        value_copy(q).wait()
        for half in range(1):
            rows = pl.ds(half * 512, 512)
            more = jnp.dot(
                hidden_s[q, rows, :],
                value_w[pl.ds(q * 8, 8)].reshape(1024, 1024),
                preferred_element_type=jnp.float32,
            )

            @pl.when(q == 0)
            def _():
                total_s[rows, :] = more

            @pl.when(q > 0)
            def _():
                total_s[rows, :] += more

        return 0

    lax.fori_loop(0, 4, forward, 0)
    gate_copy.wait()
    for half in range(1):
        rows = pl.ds(half * 512, 512)
        gates = jax.nn.sigmoid(
            jnp.dot(
                gate_in_ref[rows, :],
                gate_w[...].reshape(1024, 1024),
                preferred_element_type=jnp.float32,
            )
        )
        value = total_s[rows, :]
        grads = grad_ref[rows, :].astype(jnp.float32)
        out_ref[rows, :] = (middle_ref[rows, :] + gates * value).astype(jnp.bfloat16)
        value_grad_ref[rows, :] = (grads * gates).astype(jnp.bfloat16)
        gate_grad_ref[rows, :] = (grads * value * gates * (1.0 - gates)).astype(jnp.bfloat16)

    def backward(q, _):
        for half in range(1):
            rows = pl.ds(half * 512, 512)
            pre_s[q, rows, :] = (
                dot_nt(value_grad_ref[rows, :], value_w[pl.ds(q * 8, 8)].reshape(1024, 1024))
                * 2.0
                * relu_s[q, rows, :]
            ).astype(jnp.bfloat16)
        pre_copy(q).start()
        for half in range(1):
            rows = pl.ds(half * 512, 512)
            more = dot_nt(pre_s[q, rows, :], key_w[q].reshape(1024, 1024))

            @pl.when(q == 0)
            def _():
                key_back_ref[rows, :] = more

            @pl.when(q > 0)
            def _():
                key_back_ref[rows, :] += more

        return 0

    lax.fori_loop(0, 4, backward, 0)
    for half in range(1):
        rows = pl.ds(half * 512, 512)
        gate_back_ref[rows, :] = dot_nt(gate_grad_ref[rows, :], gate_w[...].reshape(1024, 1024))
    for q in range(4):
        for k in range(8):
            hidden_copy(q, k, hidden_ref.at[0, :, pl.ds(0, 128)]).wait()
        pre_copy(q).wait()


def channel_mix(slots, key_in, gate_in, middle, grads, late):
    tokens = key_in.shape[0]
    wide_rows = jax.ShapeDtypeStruct((tokens, 1024), jnp.float32)
    half_rows = jax.ShapeDtypeStruct((tokens, 1024), jnp.bfloat16)
    whole = pl.BlockSpec(memory_space=pltpu.VMEM)
    far = pl.BlockSpec(memory_space=pltpu.HBM)
    return pl.pallas_call(
        channel_kernel,
        out_shape=(
            half_rows,
            half_rows,
            half_rows,
            wide_rows,
            wide_rows,
            jax.ShapeDtypeStruct((4, tokens, 512), jnp.bfloat16),
            jax.ShapeDtypeStruct((4, tokens, 512), jnp.bfloat16),
            jax.ShapeDtypeStruct((tokens, 4096), jnp.bfloat16),
        ),
        in_specs=[pl.BlockSpec(memory_space=pltpu.SMEM), whole, whole, whole, whole, far],
        out_specs=(whole,) * 5 + (far,) * 3,
        scratch_shapes=[
            pltpu.VMEM((4, 32, 32, 1024), jnp.bfloat16),
            pltpu.VMEM((32, 128, 1024), jnp.bfloat16),
            pltpu.VMEM((32, 32, 1024), jnp.bfloat16),
            pltpu.VMEM((4, tokens, 1024), jnp.float32),
            pltpu.VMEM((4, tokens, 1024), jnp.bfloat16),
            pltpu.VMEM((4, tokens, 1024), jnp.bfloat16),
            pltpu.VMEM((tokens, 1024), jnp.float32),
            pltpu.SemaphoreType.DMA((9,)),
            pltpu.SemaphoreType.DMA((4, 8)),
            pltpu.SemaphoreType.DMA((4,)),
        ],
        compiler_params=pltpu.CompilerParams(vmem_limit_bytes=54 * 1024 * 1024),
        cost_estimate=pl.CostEstimate(
            flops=2 * tokens * 1024 * 1024 * 18, transcendentals=0, bytes_accessed=40 * 1024 * 1024
        ),
    )(slots, key_in, gate_in, middle, grads, late)


def owner_slots(flat):
    other = jnp.arange(32)
    apart = other ^ flat
    dz = ((other >> 1) - (flat >> 1)) & 3
    return ((apart & 1) * 16 + ((apart >> 4) & 1) * 8 + ((apart >> 3) & 1) * 4 + dz).astype(jnp.int32)


def dot_tn(left, right):
    return lax.dot_general(
        left, right, (((0,), (0,)), ((), ())), preferred_element_type=jnp.float32
    )


def chip_rows(own_in, own_grads, other_in, other_grads):
    return (dot_tn(own_in, own_grads) + dot_tn(other_in, other_grads)).astype(jnp.bfloat16)


def value_part_kernel(own_ref, other_ref, grad_ref, other_grad_ref, near, side_x, side_y, far_a, far_b):
    quarter = pl.program_id(0)
    part = chip_rows(own_ref[0], grad_ref[...], other_ref[0], other_grad_ref[...])
    part = part.reshape((4, part.shape[0] // 4, 1024))

    @pl.when(quarter == 0)
    def _():
        near[...] = part

    @pl.when(quarter == 1)
    def _():
        side_x[...] = part

    @pl.when(quarter == 2)
    def _():
        side_y[...] = part

    @pl.when(quarter == 3)
    def _():
        far_a[...] = part[:2]
        far_b[...] = part[2:]


def store_quarters(part, outs):
    near, side_x, side_y, far_a, far_b = outs
    quarters = part.reshape(4, 4, 32, 1024)
    near[...] = quarters[0]
    side_x[...] = quarters[1]
    side_y[...] = quarters[2]
    far_a[...] = quarters[3, :2]
    far_b[...] = quarters[3, 2:]


def key_part_kernel(key_ref, other_key_ref, gate_ref, other_gate_ref, *refs):
    pre_ref, other_pre_ref, gate_grad_ref, other_gate_grad_ref = refs[:4]
    step = pl.program_id(0)

    @pl.when(step < 4)
    def _():
        store_quarters(
            chip_rows(key_ref[...], pre_ref[...], other_key_ref[...], other_pre_ref[...]), refs[4:]
        )

    @pl.when(step == 4)
    def _():
        store_quarters(
            chip_rows(
                gate_ref[...], gate_grad_ref[...], other_gate_ref[...], other_gate_grad_ref[...]
            ),
            refs[4:],
        )


def time_part_kernel(own_ref, other_ref, grad_ref, other_grad_ref, *refs):
    branch_ref, other_branch_ref = refs[:2]
    step = pl.program_id(0)

    @pl.when(step < 3)
    def _():
        store_quarters(
            chip_rows(own_ref[...], grad_ref[...], other_ref[...], other_grad_ref[...]), refs[2:]
        )

    @pl.when(step == 3)
    def _():
        store_quarters(
            chip_rows(own_ref[...], branch_ref[...], other_ref[...], other_branch_ref[...]), refs[2:]
        )


def in_three(array):
    high = array.astype(jnp.bfloat16)
    rest = array - high.astype(jnp.float32)
    middle = rest.astype(jnp.bfloat16)
    return high, middle, (rest - middle.astype(jnp.float32)).astype(jnp.bfloat16)


def time_mix_kernel(
    branch_ref,
    weight_ref,
    key_ref,
    value_ref,
    gates_ref,
    mask_ref,
    carry_ref,
    num_ref,
    den_ref,
    decay_ref,
    bonus_ref,
    gate_grad_ref,
    key_grad_ref,
    value_grad_ref,
    num_grad_ref,
    den_grad_ref,
    decay_grad_ref,
    bonus_grad_ref,
):
    length = mask_ref.shape[1]
    decay = decay_ref[...]
    bonus = jnp.exp(bonus_ref[...])
    place = lax.broadcasted_iota(jnp.int32, (length, 1), 0).astype(jnp.float32)
    grow = jnp.exp(place * decay)
    shrink = jnp.exp((1.0 - place) * decay)
    for row in range(mask_ref.shape[0]):
        rows = pl.ds(row * length, length)
        mask = mask_ref[row]
        gated_grad = dot_nt(branch_ref[rows, :], weight_ref[...])
        gates = gates_ref[rows, :]
        power = jnp.exp(key_ref[rows, :])
        value = value_ref[rows, :]
        product = power * value
        fade = carry_ref[row] * jnp.exp(-place * decay)
        num_in, den_in = num_ref[row], den_ref[row]
        num_sum = sum(
            jnp.dot(mask, part, preferred_element_type=jnp.float32)
            for part in in_three(product * grow)
        )
        den_sum = sum(
            jnp.dot(mask, part, preferred_element_type=jnp.float32)
            for part in in_three(power * grow)
        )
        numer = fade * num_in + shrink * num_sum + bonus * product
        denom = fade * den_in + shrink * den_sum + bonus * power
        mixed = numer / denom
        gate_grad_ref[rows, :] = (gated_grad * mixed * gates * (1.0 - gates)).astype(jnp.bfloat16)
        num_grad = gated_grad * gates / denom
        den_grad = -num_grad * mixed
        num_back, den_back = shrink * num_grad, shrink * den_grad
        num_past = grow * sum(dot_tn(mask, part) for part in in_three(num_back))
        den_past = grow * sum(dot_tn(mask, part) for part in in_three(den_back))
        product_grad = bonus * num_grad + num_past
        key_grad_ref[rows, :] = power * (value * product_grad + bonus * den_grad + den_past)
        value_grad_ref[rows, :] = power * product_grad
        num_grad_ref[row] = jnp.sum(fade * num_grad, axis=0, keepdims=True)
        den_grad_ref[row] = jnp.sum(fade * den_grad, axis=0, keepdims=True)
        bonus_grad_ref[row] = jnp.sum(
            bonus * (product * num_grad + power * den_grad), axis=0, keepdims=True
        )
        decay_grad_ref[row] = jnp.sum(
            place * (product * num_past + power * den_past)
            + (1.0 - place) * (num_back * num_sum + den_back * den_sum)
            - place * fade * (num_grad * num_in + den_grad * den_in),
            axis=0,
            keepdims=True,
        )


def time_mix_back(branch, weight, key, value, gates, mask, carry, num, den, decay, bonus):
    tokens = branch.shape[0]
    rows, length = mask.shape[:2]
    tile = 256
    wide_block = pl.BlockSpec((tokens, tile), lambda i: (0, i))
    state = pl.BlockSpec((rows, 1, tile), lambda i: (0, 0, i))
    vector = pl.BlockSpec((1, tile), lambda i: (0, i))
    states = jax.ShapeDtypeStruct((rows, 1, 1024), jnp.float32)
    wide_rows = jax.ShapeDtypeStruct((tokens, 1024), jnp.float32)
    return pl.pallas_call(
        time_mix_kernel,
        grid=(1024 // tile,),
        out_shape=(
            jax.ShapeDtypeStruct((tokens, 1024), jnp.bfloat16),
            wide_rows,
            wide_rows,
            states,
            states,
            states,
            states,
        ),
        in_specs=[
            pl.BlockSpec((tokens, 1024), lambda i: (0, 0)),
            pl.BlockSpec((tile, 1024), lambda i: (i, 0)),
            wide_block,
            wide_block,
            wide_block,
            pl.BlockSpec((rows, length, length), lambda i: (0, 0, 0)),
            pl.BlockSpec((rows, length, 1), lambda i: (0, 0, 0)),
            state,
            state,
            vector,
            vector,
        ],
        out_specs=(wide_block, wide_block, wide_block, state, state, state, state),
        compiler_params=pltpu.CompilerParams(vmem_limit_bytes=48 * 1024 * 1024),
        cost_estimate=pl.CostEstimate(flops=1, transcendentals=0, bytes_accessed=1),
    )(branch, weight, key, value, gates, mask, carry, num, den, decay, bonus)


def quarters_call(kernel, steps, rows, in_specs, by_quarter, arguments):
    if by_quarter:
        outs = [pl.BlockSpec((n, rows, 1024), lambda i: (0, 0, 0)) for n in (4, 4, 4, 2, 2)]
    else:
        outs = [pl.BlockSpec((n, 32, 1024), lambda i: (0, i, 0)) for n in (4, 4, 4, 2, 2)]
    return pl.pallas_call(
        kernel,
        grid=(steps,),
        out_shape=tuple(
            jax.ShapeDtypeStruct((n, rows, 1024), jnp.bfloat16) for n in (4, 4, 4, 2, 2)
        ),
        in_specs=in_specs,
        out_specs=tuple(outs),
        compiler_params=pltpu.CompilerParams(vmem_limit_bytes=48 * 1024 * 1024),
        cost_estimate=pl.CostEstimate(flops=1, transcendentals=0, bytes_accessed=1),
    )(*arguments)


def value_part(own_hidden, other_hidden, grads, other_grads):
    tokens = grads.shape[0]
    whole = pl.BlockSpec((tokens, 1024), lambda i: (0, 0))
    block = pl.BlockSpec((1, tokens, 512), lambda i: (i, 0, 0))
    return quarters_call(
        value_part_kernel,
        4,
        128,
        [block, block, whole, whole],
        True,
        (own_hidden, other_hidden, grads, other_grads),
    )


def key_part(key, other_key, gate, other_gate, pre, other_pre, gate_grad, other_gate_grad):
    tokens = pre.shape[0]
    half = pl.BlockSpec((tokens, 512), lambda i: (0, 0))
    whole = pl.BlockSpec((tokens, 1024), lambda i: (0, 0))
    block = pl.BlockSpec((tokens, 1024), lambda i: (0, jnp.minimum(i, 3)))
    return quarters_call(
        key_part_kernel,
        5,
        160,
        [half, half, half, half, block, block, whole, whole],
        False,
        (key, other_key, gate, other_gate, pre, other_pre, gate_grad, other_gate_grad),
    )


def time_part(own, other, grads, other_grads, branch, other_branch):
    tokens = grads.shape[0]
    half = pl.BlockSpec((tokens, 512), lambda i: (0, i))
    whole = pl.BlockSpec((tokens, 1024), lambda i: (0, 0))
    block = pl.BlockSpec((tokens, 1024), lambda i: (0, jnp.minimum(i, 2)))
    return quarters_call(
        time_part_kernel,
        4,
        128,
        [half, half, block, block, whole, whole],
        False,
        (own, other, grads, other_grads, branch, other_branch),
    )


def ordered_halves(rows_in, flat):
    width = rows_in.shape[-1]
    rows_in = rows_in.reshape(-1, width)
    ordered = jnp.dot(rows_in, choice(flat, width), preferred_element_type=jnp.bfloat16)
    return ordered[:, : width // 2], ordered[:, width // 2 :]


def sent_together(arrays):
    got = sent(jnp.concatenate(arrays, axis=1) if len(arrays) > 1 else arrays[0], FLIP_C)
    ends = [sum(a.shape[1] for a in arrays[: i + 1]) for i in range(len(arrays))]
    return [got[:, end - a.shape[1] : end] for a, end in zip(arrays, ends)]


def wide(array):
    return array.astype(jnp.float32)


def narrow(array):
    return array.astype(jnp.bfloat16)


def send_corner(parts):
    return sent(parts[3], FLIP_X), sent(parts[4], FLIP_Y)


def add_corner(parts, add_a, add_b):
    to_y = lax.dynamic_update_slice(parts[2], narrow(wide(parts[2][:2]) + wide(add_a)), (0, 0, 0))
    to_x = lax.dynamic_update_slice(parts[1], narrow(wide(parts[1][2:]) + wide(add_b)), (2, 0, 0))
    return to_y, to_x


def send_sides(to_y, to_x):
    return sent(to_y, FLIP_Y), sent(to_x, FLIP_X)


def add_sides(parts, from_y, from_x):
    column = wide(parts[0]) + wide(from_y) + wide(from_x)
    return column[0], [narrow(column[d]) for d in (1, 2, 3)]


def send_column(outgoing):
    return [sent(part, turn_z(d)) for d, part in zip((1, 2, 3), outgoing)]


def add_all(first, others):
    for other in others:
        first = first + wide(other)
    return first


def sum_plane(total):
    for pairs in (FLIP_C, FLIP_X, FLIP_Y):
        total = total + sent(total, pairs)
    return total


def sum_column(total, flat):
    total = total + sum(sent(total, turn_z(d)) for d in (1, 2, 3))
    count = total.shape[1] // 32
    return lax.dynamic_slice_in_dim(total, flat * count, count, 1)


def shifted(shard, axis, by):
    length = lax.axis_size(axis)
    pairs = [(i, i + by) for i in range(length) if 0 <= i + by < length]
    return lax.ppermute(shard, axis, pairs)


def carried_in(part, starts_in, decay_vec, length, reverse, between=None):
    count = lax.axis_size("seq")
    place = lax.axis_index("seq")
    clear = 1.0 - starts_in.astype(jnp.float32)
    block_fade = jnp.exp(-length * decay_vec)

    def clear_of(block):
        return lax.dynamic_index_in_dim(clear, jnp.clip(block, 0, count - 1), 1, True)

    if count == 8:
        chip, core = place >> 1, place & 1
        other = sent(part, FLIP_C)
        is_far = (core == 1) == (not reverse)
        near = jnp.where(is_far, other, part)
        last = jnp.where(is_far, part, other)
        first_block, second_block = chip * 2 + (1 if reverse else 0), chip * 2 + (0 if reverse else 1)
        joined = clear_of(second_block) * block_fade * near + last
        if between is not None:
            joined = between(joined)
        step = -1 if reverse else 1
        entering = jnp.zeros_like(part)
        open_way = jnp.ones((part.shape[1], 1), jnp.float32)
        for d in (1, 2, 3):
            beside = chip - step * d
            live = ((beside >= 0) & (beside < 4)).astype(jnp.float32)
            fade = live * open_way * jnp.exp(-float(2 * (d - 1) * length) * decay_vec)
            entering = entering + fade * sent(joined, turn_z(step * d))
            open_way = open_way * clear_of(2 * beside) * clear_of(2 * beside + 1)
        return jnp.where(is_far, clear_of(first_block) * block_fade * entering + near, entering)
    gathered = lax.all_gather(part, "seq")

    def one(lap, state):
        source = count - 1 - lap if reverse else lap
        return clear_of(source) * block_fade * state + lax.dynamic_index_in_dim(gathered, source, 0, False)

    ahead = count - 1 - place if reverse else place
    return lax.fori_loop(0, ahead, one, jnp.zeros_like(part))


def norm_forward(values, gain_vec, bias_vec):
    centre = values - jnp.mean(values, axis=-1, keepdims=True)
    inv_std = lax.rsqrt(jnp.mean(centre * centre, axis=-1, keepdims=True) + eps)
    normed = centre * inv_std
    return (normed * gain_vec + bias_vec, normed, inv_std)


def norm_backward(grads, normed, inv_std, gain_vec):
    scaled = grads * gain_vec
    inner = (
        scaled
        - jnp.mean(scaled, axis=-1, keepdims=True)
        - normed * jnp.mean(scaled * normed, axis=-1, keepdims=True)
    )
    return (inv_std * inner, jnp.sum(grads * normed, axis=(0, 1)), jnp.sum(grads, axis=(0, 1)))


def project(rows_in, weight):
    return jnp.einsum("rtd,de->rte", rows_in, weight, preferred_element_type=jnp.float32)


def project_back(grads, weight):
    return jnp.einsum("rte,de->rtd", grads, weight, preferred_element_type=jnp.float32)


def weight_grad(rows_in, grads):
    total = jnp.einsum("rtd,rte->de", rows_in, grads, preferred_element_type=jnp.float32)
    return lax.psum_scatter(total, BOTH, scatter_dimension=0, tiled=True)


def weighted_value_local(
    key_row_block,
    value_row_block,
    feature_forgetting_rate,
    present_reward,
    state_numerator,
    state_denominator,
    document_segments,
):
    length = key_row_block.shape[1]
    width = key_row_block.shape[2]
    order_idx = jnp.arange(length)
    step_pos = order_idx.astype(jnp.float32)[:, None]
    powered_lookups = jnp.exp(key_row_block)
    grow_exp = jnp.exp(step_pos * feature_forgetting_rate)
    shrink = jnp.exp((1.0 - step_pos) * feature_forgetting_rate)
    pair_mask = (
        (order_idx[None, :] < order_idx[:, None])[None]
        & (document_segments[:, None, :] == document_segments[:, :, None])
    ).astype(jnp.float32)
    weighted = jnp.concatenate(
        [powered_lookups * value_row_block, powered_lookups], axis=2
    ) * jnp.concatenate([grow_exp, grow_exp], axis=1)
    past_sums = jnp.einsum(
        "rti,rie->rte", pair_mask, weighted, precision=highest
    ) * jnp.concatenate([shrink, shrink], axis=1)
    carry_fade = (document_segments == 0).astype(jnp.float32)[:, :, None] * jnp.exp(
        -step_pos * feature_forgetting_rate
    )
    present_token_contribution = jnp.exp(present_reward) * powered_lookups
    numer = (
        carry_fade * state_numerator[:, None, :]
        + past_sums[:, :, :width]
        + present_token_contribution * value_row_block
    )
    denom = (
        carry_fade * state_denominator[:, None, :]
        + past_sums[:, :, width:]
        + present_token_contribution
    )
    return numer / denom


def tail_terms(key_row_block, value_row_block, feature_forgetting_rate, document_segments):
    length = key_row_block.shape[1]
    step_pos = jnp.arange(length).astype(jnp.float32)[:, None]
    powered_lookups = jnp.exp(key_row_block)
    tail_fade = (document_segments == document_segments[:, -1:]).astype(jnp.float32)[
        :, :, None
    ] * jnp.exp((step_pos - (length - 1)) * feature_forgetting_rate)
    return (
        jnp.sum(tail_fade * powered_lookups * value_row_block, axis=1),
        jnp.sum(tail_fade * powered_lookups, axis=1),
        tail_fade,
        powered_lookups,
    )


def shards(
    tuned,
    incoming_activations,
    sequence_extents,
    upstream_sensitivity,
    initial_normalizer_scale,
    initial_normalizer_offset,
    temporal_lookup_fraction,
    temporal_content_fraction,
    temporal_receptance_fraction,
    feature_forgetting_rate,
    present_reward,
    temporal_lookup_projection,
    temporal_content_projection,
    temporal_receptance_projection,
    temporal_result_projection,
    later_normalizer_scale,
    later_normalizer_offset,
    feature_lookup_fraction,
    feature_receptance_fraction,
    feature_lookup_projection,
    feature_content_projection,
    feature_receptance_projection,
):
    flat = lax.axis_index("batch") * lax.axis_size("seq") + lax.axis_index("seq")
    vectors = jnp.stack(
        [
            initial_normalizer_scale,
            initial_normalizer_offset,
            temporal_lookup_fraction,
            temporal_content_fraction,
            temporal_receptance_fraction,
            feature_forgetting_rate,
            present_reward,
            later_normalizer_scale,
            later_normalizer_offset,
            feature_lookup_fraction,
            feature_receptance_fraction,
        ]
    )
    if tuned:
        order = long_slots(flat)
        late = lax.all_gather(
            pack_late(
                feature_lookup_projection,
                feature_content_projection,
                feature_receptance_projection,
            ),
            BOTH,
        )
        spread = jnp.tile(jnp.pad(vectors, ((0, 5), (0, 0))), (1, 32))
        packed = jnp.where(jnp.arange(1024) // 32 == flat, spread, jnp.zeros_like(spread))
        part = stacked(
            [
                temporal_lookup_projection,
                temporal_content_projection,
                temporal_receptance_projection,
                temporal_result_projection,
                packed,
            ]
        )
        column = jnp.stack([part] + around(part))
        from_x, from_y = sent(column, FLIP_X), sent(column, FLIP_Y)
        early = both_cores([column, from_x, from_y, *send_far(from_x, from_y)])
        vectors = jnp.sum(
            assemble(early, order, 128, 16, 1).reshape(32, 16, 1024).astype(jnp.float32), axis=0
        )
        lookup_weight = assemble(early, order, 0, 32, 1)
        content_weight = assemble(early, order, 32, 32, 1)
        receptance_weight = assemble(early, order, 64, 32, 1)
        result_weight = assemble(early, order, 96, 32, 1)
    else:
        (
            lookup_weight,
            content_weight,
            receptance_weight,
            result_weight,
            ffn_key_weight,
            ffn_gate_weight,
            ffn_value_weight,
        ) = [
            lax.all_gather(part, BOTH, axis=0, tiled=True)
            for part in (
                temporal_lookup_projection,
                temporal_content_projection,
                temporal_receptance_projection,
                temporal_result_projection,
                feature_lookup_projection,
                feature_receptance_projection,
                feature_content_projection,
            )
        ]
        vectors = lax.all_gather(vectors, BOTH, axis=1, tiled=True).astype(jnp.float32)
    (
        opening_standardize_scale,
        opening_standardize_offset,
        temporal_lookup_mixture,
        temporal_content_mixture,
        temporal_receptance_mixture,
        decay_vec,
        reward_array,
        closing_standardize_scale,
        closing_standardize_offset,
        feature_lookup_mixture,
        feature_receptance_mixture,
    ) = tuple(vectors[i] for i in range(11))
    rows, length, width = incoming_activations.shape
    starts = jnp.cumsum(sequence_extents, axis=1) - sequence_extents
    places = lax.axis_index("seq") * length + jnp.arange(length, dtype=jnp.int32)
    resets = jnp.any(
        (starts[:, None, :] == places[None, :, None]) & (sequence_extents[:, None, :] > 0), axis=2
    )
    document_segments = jnp.cumsum(resets.astype(jnp.int32), axis=1)
    keep_mask = 1.0 - resets.astype(jnp.float32)[:, :, None]
    clear_flag = (document_segments[:, -1:] == 0).astype(jnp.float32)
    starts_in = jnp.any(
        (starts[:, None, :] // length == jnp.arange(lax.axis_size("seq"))[None, :, None])
        & (sequence_extents[:, None, :] > 0),
        axis=2,
    )

    inputs = incoming_activations.astype(jnp.float32)
    left_rows = shifted(incoming_activations[:, length - 1 :, :], "seq", 1)
    normed_one, unit_one, inv_one = norm_forward(
        inputs, opening_standardize_scale, opening_standardize_offset
    )
    left_normed, _, _ = norm_forward(
        left_rows.astype(jnp.float32), opening_standardize_scale, opening_standardize_offset
    )
    before_one = jnp.concatenate([left_normed, normed_one[:, :-1, :]], axis=1) * keep_mask
    key_in = (
        normed_one * temporal_lookup_mixture + before_one * (1.0 - temporal_lookup_mixture)
    ).astype(jnp.bfloat16)
    value_in = (
        normed_one * temporal_content_mixture + before_one * (1.0 - temporal_content_mixture)
    ).astype(jnp.bfloat16)
    gate_in = (
        normed_one * temporal_receptance_mixture + before_one * (1.0 - temporal_receptance_mixture)
    ).astype(jnp.bfloat16)
    key_row_block = project(key_in, lookup_weight)
    value_row_block = project(value_in, content_weight)
    gates = jax.nn.sigmoid(project(gate_in, receptance_weight))
    tail_num, tail_den, tail_fade, powered_lookups = tail_terms(
        key_row_block, value_row_block, decay_vec, document_segments
    )
    state_numerator, state_denominator = carried_in(
        jnp.stack([tail_num, tail_den]), starts_in, decay_vec, length, False
    )
    mixed, weighted_value_backward = jax.vjp(
        partial(weighted_value_local, document_segments=document_segments),
        key_row_block,
        value_row_block,
        decay_vec,
        reward_array,
        state_numerator,
        state_denominator,
    )
    gated = (gates * mixed).astype(jnp.bfloat16)
    if tuned:
        own_key, far_key = ordered_halves(key_in, flat)
        own_value, far_value = ordered_halves(value_in, flat)
        own_gate, far_gate = ordered_halves(gate_in, flat)
        own_gated, far_gated = ordered_halves(gated, flat)
        other_time = sent(
            jnp.concatenate([far_key, far_value, far_gate, far_gated], axis=1), FLIP_C
        )
        own_time = jnp.concatenate([own_key, own_value, own_gate, own_gated], axis=1)
    middle = inputs + project(gated, result_weight)
    normed_two, unit_two, inv_two = norm_forward(
        middle, closing_standardize_scale, closing_standardize_offset
    )
    before_rows = shifted(normed_two[:, length - 1 :, :], "seq", 1)
    before_two = jnp.concatenate([before_rows, normed_two[:, :-1, :]], axis=1) * keep_mask
    ffn_key_in = (
        normed_two * feature_lookup_mixture + before_two * (1.0 - feature_lookup_mixture)
    ).astype(jnp.bfloat16)
    ffn_gate_in = (
        normed_two * feature_receptance_mixture + before_two * (1.0 - feature_receptance_mixture)
    ).astype(jnp.bfloat16)
    grad_out = upstream_sensitivity.astype(jnp.float32)
    if tuned:
        own_ffn_key, far_ffn_key = ordered_halves(ffn_key_in, flat)
        own_ffn_gate, far_ffn_gate = ordered_halves(ffn_gate_in, flat)
        other_ffn_key, other_ffn_gate = sent_together([far_ffn_key, far_ffn_gate])
        output, value_grad, ffn_gate_grad, key_two_grad, gate_two_grad, *kept = channel_mix(
            owner_slots(flat),
            ffn_key_in.reshape(-1, width),
            ffn_gate_in.reshape(-1, width),
            middle.reshape(-1, width),
            upstream_sensitivity.reshape(-1, width),
            late,
        )
        output, key_two_grad, gate_two_grad = (
            a.reshape(rows, length, width) for a in (output, key_two_grad, gate_two_grad)
        )
        own_hidden, far_hidden, pre_grad = kept
        other_value_grad = sent(value_grad, FLIP_C)
        other_hidden = sent(far_hidden, FLIP_C)
        other_gate_grad = sent(ffn_gate_grad, FLIP_C)
        other_pre_grad = sent(pre_grad, FLIP_C)
        value_parts = value_part(own_hidden, other_hidden, value_grad, other_value_grad)
        value_corner = send_corner(value_parts)
        key_parts = key_part(
            own_ffn_key,
            other_ffn_key,
            own_ffn_gate,
            other_ffn_gate,
            pre_grad,
            other_pre_grad,
            ffn_gate_grad,
            other_gate_grad,
        )
        value_sides = add_corner(value_parts, *all_tied(value_corner, key_parts[4]))
        value_from = send_sides(*value_sides)
    else:
        hidden_pre = project(ffn_key_in, ffn_key_weight)
        hidden = jnp.square(jax.nn.relu(hidden_pre)).astype(jnp.bfloat16)
        ffn_value = project(hidden, ffn_value_weight)
        ffn_gates = jax.nn.sigmoid(project(ffn_gate_in, ffn_gate_weight))
        output = (middle + ffn_gates * ffn_value).astype(jnp.bfloat16)
        value_grad = (grad_out * ffn_gates).astype(jnp.bfloat16)
        ffn_gate_grad = (grad_out * ffn_value * ffn_gates * (1.0 - ffn_gates)).astype(jnp.bfloat16)
        hidden_grad = project_back(value_grad, ffn_value_weight)
        pre_grad = (hidden_grad * 2.0 * jax.nn.relu(hidden_pre)).astype(jnp.bfloat16)
        grad_ffn_value = weight_grad(hidden, value_grad)
        grad_ffn_key = weight_grad(ffn_key_in, pre_grad)
        grad_ffn_gate = weight_grad(ffn_gate_in, ffn_gate_grad)
        key_two_grad = project_back(pre_grad, ffn_key_weight)
        gate_two_grad = project_back(ffn_gate_grad, ffn_gate_weight)
    spread_two = normed_two - before_two
    grad_ffn_mix_key = jnp.sum(key_two_grad * spread_two, axis=(0, 1))
    grad_ffn_mix_gate = jnp.sum(gate_two_grad * spread_two, axis=(0, 1))
    normed_two_grad = (
        key_two_grad * feature_lookup_mixture + gate_two_grad * feature_receptance_mixture
    )
    before_two_grad = (
        key_two_grad * (1.0 - feature_lookup_mixture)
        + gate_two_grad * (1.0 - feature_receptance_mixture)
    ) * keep_mask
    from_right = shifted(before_two_grad[:, :1, :], "seq", -1)
    normed_two_grad = normed_two_grad + jnp.concatenate(
        [before_two_grad[:, 1:, :], from_right], axis=1
    )
    middle_norm_grad, grad_gain_two, grad_bias_two = norm_backward(
        normed_two_grad, unit_two, inv_two, closing_standardize_scale
    )
    middle_grad = grad_out + middle_norm_grad
    branch_grad = middle_grad.astype(jnp.bfloat16)
    if tuned:
        flat_branch_grad = branch_grad.reshape(-1, width)
        other_branch_grad = sent(flat_branch_grad, FLIP_C)
        key_corner = send_corner(key_parts)
    else:
        grad_output = weight_grad(gated, branch_grad)
    if tuned:
        order_idx = jnp.arange(length)
        pair_mask = (
            (order_idx[None, :] < order_idx[:, None])[None]
            & (document_segments[:, None, :] == document_segments[:, :, None])
        ).astype(jnp.bfloat16)
        (
            gate_pre_grad,
            key_gradient,
            value_gradient,
            numerator_gradient,
            denominator_gradient,
            decay_gradient,
            reward_derivative,
        ) = time_mix_back(
            branch_grad.reshape(-1, width),
            result_weight,
            key_row_block.reshape(-1, width),
            value_row_block.reshape(-1, width),
            gates.reshape(-1, width),
            pair_mask,
            (document_segments == 0).astype(jnp.float32)[:, :, None],
            state_numerator[:, None, :],
            state_denominator[:, None, :],
            tied(decay_vec[None, :], value_sides[0], value_sides[1][2:]),
            reward_array[None, :],
        )
        gate_pre_grad, key_gradient, value_gradient = (
            a.reshape(rows, length, width) for a in (gate_pre_grad, key_gradient, value_gradient)
        )
        numerator_gradient = numerator_gradient[:, 0, :]
        denominator_gradient = denominator_gradient[:, 0, :]
        decay_gradient = jnp.sum(decay_gradient[:, 0, :], axis=0)
        reward_derivative = jnp.sum(reward_derivative[:, 0, :], axis=0)
    else:
        gated_grad = project_back(branch_grad, result_weight)
        gate_pre_grad = (gated_grad * mixed * gates * (1.0 - gates)).astype(jnp.bfloat16)
        blended_gradient = gated_grad * gates
        (
            key_gradient,
            value_gradient,
            decay_gradient,
            reward_derivative,
            numerator_gradient,
            denominator_gradient,
        ) = weighted_value_backward(blended_gradient)
    state_gradient = jnp.stack([numerator_gradient, denominator_gradient])
    if tuned:
        key_sides = add_corner(key_parts, *all_tied(key_corner, state_gradient))
        key_from = send_sides(*key_sides)
        state_gradient = tied(state_gradient, key_sides[0], key_sides[1][2:])
    summed = []

    def beside_sides(joined):
        summed.extend(
            add_sides(value_parts, *[tied(a, joined, other_time) for a in value_from])
        )
        return tied(joined, summed[1][0])

    num_next, den_next = carried_in(
        state_gradient, starts_in, decay_vec, length, True, beside_sides if tuned else None
    )
    if tuned:
        value_first, value_outgoing = summed
    num_tail = tail_fade * num_next[:, None, :]
    den_tail = tail_fade * den_next[:, None, :]
    tail_grad = powered_lookups * (value_row_block * num_tail + den_tail)
    key_gradient = key_gradient + tail_grad
    value_gradient = value_gradient + powered_lookups * num_tail
    offsets = (jnp.arange(length).astype(jnp.float32) - (length - 1))[:, None]
    block_fade = clear_flag * jnp.exp(-length * decay_vec)
    decay_gradient = decay_gradient + jnp.sum(offsets * tail_grad, axis=(0, 1))
    decay_gradient = decay_gradient - length * jnp.sum(
        block_fade * (state_numerator * num_next + state_denominator * den_next), axis=0
    )
    key_grad16 = key_gradient.astype(jnp.bfloat16)
    val_grad16 = value_gradient.astype(jnp.bfloat16)
    if tuned:
        flat_grads = jnp.concatenate(
            [g.reshape(-1, width) for g in (key_grad16, val_grad16, gate_pre_grad)], axis=1
        )
        other_grads = sent(flat_grads, FLIP_C)
        time_parts = time_part(
            own_time, other_time, flat_grads, other_grads, flat_branch_grad, other_branch_grad
        )
        value_got = all_tied(send_column(all_tied(value_outgoing, num_next)), time_parts[4])
        time_corner = send_corner(time_parts)
    else:
        grad_key = weight_grad(key_in, key_grad16)
        grad_value = weight_grad(value_in, val_grad16)
        grad_gate = weight_grad(gate_in, gate_pre_grad)
    if tuned:
        key_grad16 = tied(key_grad16, time_parts[4])
    key_in_grad = project_back(key_grad16, lookup_weight)
    value_in_grad = project_back(val_grad16, content_weight)
    gate_in_grad = project_back(gate_pre_grad, receptance_weight)
    spread_one = normed_one - before_one
    grad_mix_key = jnp.sum(key_in_grad * spread_one, axis=(0, 1))
    grad_mix_value = jnp.sum(value_in_grad * spread_one, axis=(0, 1))
    grad_mix_gate = jnp.sum(gate_in_grad * spread_one, axis=(0, 1))
    normed_one_grad = (
        key_in_grad * temporal_lookup_mixture
        + value_in_grad * temporal_content_mixture
        + gate_in_grad * temporal_receptance_mixture
    )
    before_one_grad = (
        key_in_grad * (1.0 - temporal_lookup_mixture)
        + value_in_grad * (1.0 - temporal_content_mixture)
        + gate_in_grad * (1.0 - temporal_receptance_mixture)
    ) * keep_mask
    if tuned:
        key_first, key_outgoing = add_sides(key_parts, *all_tied(key_from, before_one_grad))
        time_sides = add_corner(time_parts, *all_tied(time_corner, before_one_grad))
        time_from = send_sides(*time_sides)
    from_next = shifted(before_one_grad[:, :1, :], "seq", -1)
    if tuned:
        key_got = send_column(all_tied(key_outgoing, from_next))
        from_next = tied(from_next, time_sides[0])
    normed_one_grad = normed_one_grad + jnp.concatenate(
        [before_one_grad[:, 1:, :], from_next], axis=1
    )
    input_norm_grad, grad_gain_one, grad_bias_one = norm_backward(
        normed_one_grad, unit_one, inv_one, opening_standardize_scale
    )
    input_grad = middle_grad + input_norm_grad
    vector_grads = jnp.stack(
        [
            grad_gain_one,
            grad_bias_one,
            grad_mix_key,
            grad_mix_value,
            grad_mix_gate,
            decay_gradient,
            reward_derivative,
            grad_gain_two,
            grad_bias_two,
            grad_ffn_mix_key,
            grad_ffn_mix_gate,
        ]
    )
    if tuned:
        time_first, time_outgoing = add_sides(time_parts, *all_tied(time_from, vector_grads))
        key_total = add_all(key_first, all_tied(key_got, vector_grads))
        time_got = send_column(time_outgoing)
        time_total = add_all(time_first, time_got)
        grad_key, grad_value, grad_gate, grad_output = (
            time_total[i : i + 32] for i in (0, 32, 64, 96)
        )
        grad_ffn_value = add_all(value_first, value_got)
        grad_ffn_key = jnp.concatenate([key_total[i : i + 32] for i in (0, 32, 64, 96)], axis=1)
        grad_ffn_gate = key_total[128:]
        vector_grads = sum_column(tied(sum_plane(vector_grads), time_got[0]), flat)
    else:
        vector_grads = lax.psum_scatter(vector_grads, BOTH, scatter_dimension=1, tiled=True)
    return (
        output,
        input_grad,
        vector_grads[0],
        vector_grads[1],
        vector_grads[2],
        vector_grads[3],
        vector_grads[4],
        vector_grads[5],
        vector_grads[6],
        grad_key,
        grad_value,
        grad_gate,
        grad_output,
        vector_grads[7],
        vector_grads[8],
        vector_grads[9],
        vector_grads[10],
        grad_ffn_key,
        grad_ffn_value,
        grad_ffn_gate,
    )


def solution(mesh):
    tuned = tuple(mesh.shape.items()) == (("batch", 4), ("seq", 8))
    return jax.shard_map(
        partial(shards, tuned),
        mesh=mesh,
        in_specs=(
            P("batch", "seq", None),
            P("batch", None),
            P("batch", "seq", None),
            P(("batch", "seq")),
            P(("batch", "seq")),
            P(("batch", "seq")),
            P(("batch", "seq")),
            P(("batch", "seq")),
            P(("batch", "seq")),
            P(("batch", "seq")),
            P(("batch", "seq"), None),
            P(("batch", "seq"), None),
            P(("batch", "seq"), None),
            P(("batch", "seq"), None),
            P(("batch", "seq")),
            P(("batch", "seq")),
            P(("batch", "seq")),
            P(("batch", "seq")),
            P(("batch", "seq"), None),
            P(("batch", "seq"), None),
            P(("batch", "seq"), None),
        ),
        out_specs=(
            P("batch", "seq", None),
            P("batch", "seq", None),
            P(("batch", "seq")),
            P(("batch", "seq")),
            P(("batch", "seq")),
            P(("batch", "seq")),
            P(("batch", "seq")),
            P(("batch", "seq")),
            P(("batch", "seq")),
            P(("batch", "seq"), None),
            P(("batch", "seq"), None),
            P(("batch", "seq"), None),
            P(("batch", "seq"), None),
            P(("batch", "seq")),
            P(("batch", "seq")),
            P(("batch", "seq")),
            P(("batch", "seq")),
            P(("batch", "seq"), None),
            P(("batch", "seq"), None),
            P(("batch", "seq"), None),
        ),
        check_vma=False,
    )
```
